128 devices in a mesh: gx: 8 (over x_hi, z), gy: 8 (over y, x_lo), dp: 2 (over core).
Axes of the slice: x: 4 (x_hi: 2, x_lo: 2; x = x_hi * 2 + x_lo), y: 4, z: 4, core: 2. Of those that a mesh axis runs over, the one named last changes fastest.
Arguments:
- inputs: bfloat16 [4, 4, 64, 128, 128], P('dp', None, 'gx', 'gy'), may hold values from -6 to 6
- cotangent: bfloat16 [4, 64, 16, 32, 32], P('dp', None, 'gx', 'gy'), may hold values from -96 to 96
- w_first: bfloat16 [32, 4, 3, 3, 3], replicated, may hold values from -0.625 to 0.625
- w_second: bfloat16 [64, 32, 3, 3, 3], replicated, may hold values from -0.21875 to 0.21875
- b_first: float32 [32], replicated, may hold values from -3 to 3
- b_second: float32 [64], replicated, may hold values from -3 to 3
Outputs:
- grad_input: bfloat16 [4, 4, 64, 128, 128], P('dp', None, 'gx', 'gy')
- grad_w1: float32 [3456], P(('gx', 'gy', 'dp'))
- grad_w2: float32 [55296], P(('gx', 'gy', 'dp'))
The draws below stay inside these ranges and needn't reach their ends.
All inputs are finite; a program needn't handle non-finite values.
Results may differ from the reference program's by a relative error of at most 0.014.
Values may be sent and summed in bfloat16 or wider, within the bound.
A program may use at most 192 MiB of HBM per device.

```python
import jax
import jax.numpy as jnp
from jax import lax

C0 = 4
C1 = 32
C2 = 64
ZC = 128
BATCH = 4
NX = 64
NY = 128


def block_levels(stream_key, dims, cuts, least, top_value):
    level = 1.0
    for dim, blocks in cuts:
        steps = jax.random.uniform(jax.random.fold_in(jax.random.fold_in(stream_key, 6), dim), (blocks,), jnp.float32, least / len(cuts), top_value / len(cuts))
        level = level * jnp.repeat(jnp.exp(steps), dims[dim] // blocks).reshape((-1,) + (1,) * (len(dims) - 1 - dim))
    return level


def gaussian(key, extent, deviation, bound, cuts=(), dtype=jnp.bfloat16):
    factor_of = block_levels(key, extent, cuts, -0.22, 0.18) if cuts else 1.0
    drawn = jax.random.normal(key, extent, jnp.float32) * deviation * factor_of
    return jnp.minimum(jnp.maximum(drawn, -bound), bound).astype(dtype)


def setup_inputs(seed: int = 0) -> dict:
    arg_keys = jax.random.split(jax.random.key(seed), 7)
    inputs = gaussian(arg_keys[0], (BATCH, C0, NX, NY, ZC), 1.0, 6.0, ((0, 2), (2, 8), (3, 8)))
    cotangent = gaussian(arg_keys[1], (BATCH, C2, NX // 4, NY // 4, ZC // 4), 16.0, 96.0, ((0, 2), (2, 8), (3, 8)))
    w_first = gaussian(arg_keys[2], (C1, C0, 3, 3, 3), (27 * C0) ** -0.5, 0.625)
    w_second = gaussian(arg_keys[3], (C2, C1, 3, 3, 3), (27 * C1) ** -0.5, 0.21875)
    b_first = gaussian(arg_keys[4], (C1,), 0.5, 3.0, (), jnp.float32)
    b_second = gaussian(arg_keys[5], (C2,), 0.5, 3.0, (), jnp.float32)
    return {"inputs": inputs, "cotangent": cotangent, "w_first": w_first, "w_second": w_second, "b_first": b_first, "b_second": b_second}


def leaky_smooth(values):
    return 0.3 * values + 0.7 * values * jax.nn.sigmoid(values)


def leaky_slope(values):
    sig = jax.nn.sigmoid(values)
    return 0.3 + 0.7 * (sig + values * sig * (1.0 - sig))


def average_pool(values):
    count, chans, height, width, depth = values.shape
    blocks = values.reshape(count, chans, height // 2, 2, width // 2, 2, depth // 2, 2)
    return jnp.mean(blocks, axis=(3, 5, 7))


def spread_back(values):
    count, chans, height, width, depth = values.shape
    wide = jnp.broadcast_to(values[:, :, :, None, :, None, :, None], (count, chans, height, 2, width, 2, depth, 2))
    return wide.reshape(count, chans, 2 * height, 2 * width, 2 * depth) * 0.125


def conv_same(values, kernel):
    return lax.conv_general_dilated(values.astype(jnp.float32), kernel.astype(jnp.float32), (1, 1, 1), [(1, 1), (1, 1), (1, 1)], dimension_numbers=("NCDHW", "OIDHW", "NCDHW"), precision=lax.Precision.HIGHEST)


def conv_back(grads, kernel):
    flipped = jnp.flip(kernel, (2, 3, 4)).astype(jnp.float32)
    return lax.conv_general_dilated(grads.astype(jnp.float32), flipped, (1, 1, 1), [(1, 1), (1, 1), (1, 1)], dimension_numbers=("NCDHW", "IODHW", "NCDHW"), precision=lax.Precision.HIGHEST)


def tap_grads(values, grads):
    height, width, depth = values.shape[2], values.shape[3], values.shape[4]
    padded = jnp.pad(values.astype(jnp.float32), ((0, 0), (0, 0), (1, 1), (1, 1), (1, 1)))
    grads_f = grads.astype(jnp.float32)
    taps = []
    for first in range(3):
        for second in range(3):
            for third in range(3):
                window = padded[:, :, first:first + height, second:second + width, third:third + depth]
                taps.append(jnp.einsum("nohwz,nihwz->oi", grads_f, window, precision=lax.Precision.HIGHEST))
    stacked = jnp.stack(taps, axis=-1)
    return stacked.reshape(stacked.shape[0], stacked.shape[1], 3, 3, 3)


def one_sample(inputs, cotangent, w_first, w_second, b_first, b_second):
    pre_first = conv_same(inputs, w_first) + b_first[None, :, None, None, None]
    pooled = average_pool(leaky_smooth(pre_first)).astype(jnp.bfloat16)
    pre_second = conv_same(pooled, w_second) + b_second[None, :, None, None, None]
    grad_second = (leaky_slope(pre_second) * spread_back(cotangent.astype(jnp.float32))).astype(jnp.bfloat16)
    grad_pooled = conv_back(grad_second, w_second)
    grad_first = (leaky_slope(pre_first) * spread_back(grad_pooled)).astype(jnp.bfloat16)
    grad_input = conv_back(grad_first, w_first).astype(jnp.bfloat16)
    return grad_input, tap_grads(inputs, grad_first), tap_grads(pooled, grad_second)


def reference(inputs, cotangent, w_first, w_second, b_first, b_second):
    def step(pair):
        sample_in, sample_cot = pair
        result = one_sample(sample_in[None], sample_cot[None], w_first, w_second, b_first, b_second)
        return result[0][0], result[1], result[2]

    grad_input, first_terms, second_terms = lax.map(step, (inputs, cotangent))
    cells = BATCH * NX * NY * ZC
    grad_w1 = (jnp.sum(first_terms, axis=0) * (1.0 / (cells ** 0.5))).reshape(-1).astype(jnp.float32)
    grad_w2 = (jnp.sum(second_terms, axis=0) * (1.0 / ((cells / 8) ** 0.5))).reshape(-1).astype(jnp.float32)
    return grad_input, grad_w1, grad_w2
```

```python
import functools

import jax
import jax.numpy as jnp
import ml_dtypes
import numpy as np
from jax import lax
from jax.experimental import pallas as pl
from jax.experimental.pallas import tpu as pltpu
from jax.sharding import PartitionSpec as P

MESH = pl.DeviceIdType.MESH
F32 = jnp.float32
BF16 = jnp.bfloat16
DIRS = [(0, 1), (0, -1), (1, 0), (-1, 0), (1, 1), (1, -1), (-1, 1), (-1, -1)]
CELLS = 4194304


def constants():
    depth_map = np.zeros((256, 768), np.float32)
    for n in range(2):
        for z in range(128):
            lane = (z % 2) * 128 + (z // 2 % 2) * 64 + n * 32 + z // 4
            for t in range(3):
                src = z + t - 1
                if 0 <= src < 128:
                    depth_map[n * 128 + src, t * 256 + lane] = 1
    restore = depth_map[:, 256:512].T.copy()
    pool_map = np.zeros((128, 256), np.float32)
    for n in range(2):
        for z in range(64):
            lane = (z % 2) * 64 + n * 32 + z // 2
            for half, src in ((0, z - 1), (1, z + 1)):
                if 0 <= src < 64:
                    pool_map[(src % 2) * 64 + n * 32 + src // 2, half * 128 + lane] = 1
    cot_map = np.zeros((128, 256), np.float32)
    for h in range(2):
        for b in range(2):
            for n in range(2):
                for k in range(32):
                    cot_map[n * 64 + h * 32 + k, h * 128 + b * 64 + n * 32 + k] = 1
    row_of = {}
    place = np.full((80,), -100.0, np.float32)
    chan = np.full((80,), -1)
    for c in range(4):
        for y in range(-1, 17):
            row = 64 + c if y < 0 else 68 + c if y > 15 else c * 16 + y
            row_of[c, y] = row
            place[row] = y
            chan[row] = c
    toeplitz = np.zeros((16, 128, 720), np.float32)
    for r in range(16):
        y = 2 * (r % 8) + r // 8
        for dx in range(3):
            for dy in range(3):
                for dz in range(3):
                    for c in range(4):
                        tap = (dx * 3 + dy) * 3 + dz
                        toeplitz[r, tap * 4 + c, dx * 240 + dz * 80 + row_of[c, y + dy - 1]] = 1
    gather = np.zeros((3, 720, 128), np.float32)
    for dy in range(3):
        for dx in range(3):
            for dz in range(3):
                for row in range(72):
                    gather[dy, dx * 240 + dz * 80 + row, chan[row] * 32 + dx * 9 + dy * 3 + dz] = 1
    select = np.zeros((16, 64), np.float32)
    for c in range(4):
        select[c, c * 16 + 15] = 1
        select[4 + c, c * 16] = 1
    b16 = lambda v: v.astype(ml_dtypes.bfloat16)
    return (
        b16(depth_map), b16(restore), b16(pool_map), b16(cot_map), b16(toeplitz), b16(gather), b16(select),
        b16(np.eye(128, dtype=np.float32)), np.tile(place, 9)[None, :],
    )


def dot(a, b):
    return jnp.dot(a, b, preferred_element_type=F32)


def dot_nt(a, b):
    return lax.dot_general(a, b, (((1,), (1,)), ((), ())), preferred_element_type=F32)


def before2(u):
    lane = lax.broadcasted_iota(jnp.int32, u.shape, 1)
    return jnp.where(
        lane < 64, jnp.where(lane % 32 != 0, pltpu.roll(u, 65, 1), 0.0), pltpu.roll(u, 64, 1)
    )


def after2(u):
    lane = lax.broadcasted_iota(jnp.int32, u.shape, 1)
    return jnp.where(
        lane >= 64, jnp.where(lane % 32 != 31, pltpu.roll(u, 63, 1), 0.0), pltpu.roll(u, 64, 1)
    )


def before(v):
    return jnp.concatenate([before2(v[:, 128:]), v[:, :128]], axis=1)


def after(v):
    return jnp.concatenate([v[:, 128:], after2(v[:, :128])], axis=1)


def kernel(
    gxn, gyn,
    inp, cot, w1t, w2t, b1r, b2r, depth_map, restore, pool_map, cot_map, toeplitz, gather, select, eye, place,
    out, gw1, gw2,
    xs, hb, hlr, hx, hc, w1, w1tr, w2, w2b, bias1, bias2, sl, gf, pool, cots, gs, gp,
    acc2, r2dp, s2a, r2gx, s2b, r2gy, gi, sby, ry, sx_, rx, sc, rc, acc1, s1, r1dp, s1a, r1gx, s1b, r1gy,
    ssem, rsem,
):
    gx, gy, dp = lax.axis_index("gx"), lax.axis_index("gy"), lax.axis_index("dp")

    def at(sx, sy):
        return (lax.rem(gx + sx + gxn, gxn), lax.rem(gy + sy + gyn, gyn), dp)

    def remote(src, dst, k, device):
        return pltpu.make_async_remote_copy(
            src_ref=src, dst_ref=dst, send_sem=ssem.at[k], recv_sem=rsem.at[k], device_id=device, device_id_type=MESH
        )

    barrier = pltpu.get_barrier_semaphore()
    peers = [at(*d) for d in DIRS]
    peers += [at(d, 0) for d in range(2, gxn - 1)] + [at(0, d) for d in range(2, gyn - 1)]
    peers += [(gx, gy, 1 - dp)]
    for peer in peers:
        pl.semaphore_signal(barrier, inc=1, device_id=peer, device_id_type=MESH)

    def raw(x):
        halves = [inp[n, :, x].reshape(64, 128) for n in range(2)]
        return jnp.concatenate(halves, axis=1)

    for x in range(8):
        hb[x] = dot(select[...], raw(x)).astype(BF16)
    pl.semaphore_wait(barrier, len(peers))
    first = []
    for k, (sx, sy) in enumerate(DIRS):
        a, b = (0 if sx == 1 else 1), (0 if sy == 1 else 1)
        if sx == 0:
            src, dst = hb, hlr.at[b]
        elif sy == 0:
            src, dst = inp.at[:, :, 7 if sx == 1 else 0], hx.at[a]
        else:
            src, dst = hb.at[7 if sx == 1 else 0], hc.at[a, b]
        first.append(remote(src, dst, k, at(sx, sy)))
        first[-1].start()

    small = dot_nt(eye[:32, :32], w1t[...]).astype(BF16)
    small = jnp.concatenate([small, jnp.zeros((32, 128 - 108), BF16)], axis=1)

    def fill(r, _):
        w1[pl.ds(pl.multiple_of(r * 32, 32), 32), :] = dot(small, toeplitz[r]).astype(BF16)
        return 0

    lax.fori_loop(0, 16, fill, 0)
    for b in range(6):
        width = min(128, 720 - b * 128)
        w1tr[b * 128:b * 128 + width] = dot_nt(eye[:width, :width], w1[:, b * 128:b * 128 + width]).astype(BF16)
    w2[...] = dot_nt(eye[:64, :64], w2t[...]).astype(BF16)
    for dx in range(3):
        for dy in range(3):
            at_lane = ((2 - dx) * 3 + 2 - dy) * 64
            row = (dx * 3 + dy) * 96
            w2b[:, at_lane:at_lane + 64] = w2t[row:row + 96, :]
    bias1[...] = jnp.zeros_like(bias1)
    bias1[:, 0:32] = jnp.broadcast_to(b1r[...], (128, 32))
    bias2[...] = jnp.zeros_like(bias2)
    bias2[:, 0:64] = jnp.broadcast_to(b2r[...], (128, 64))
    b1 = jnp.transpose(bias1[...])[:32]
    b2 = jnp.transpose(bias2[...])[:64]
    b1 = jnp.concatenate([b1, b1], axis=1)
    b2 = jnp.concatenate([b2, b2], axis=1)
    for q in range(4):
        part = jnp.concatenate(
            [cot[(n * 8 + h * 4 + q) * 32:(n * 8 + h * 4 + q) * 32 + 32, :] for n in range(2) for h in range(2)], axis=0
        )
        turned = dot_nt(eye[:64, :64], part).astype(BF16)
        cots[q * 64:q * 64 + 64] = dot(turned, cot_map[...]) * 0.125

    def slab(index, rows):
        spread = dot(rows, depth_map[...]).astype(BF16)
        for t in range(3):
            xs[index, t * 80:t * 80 + 64] = spread[:, t * 256:t * 256 + 256]

    for x in range(8):
        slab(x + 1, raw(x))
    acc2[...] = jnp.zeros_like(acc2)
    gi[...] = jnp.zeros_like(gi)
    acc1[...] = jnp.zeros_like(acc1)
    for copy in first:
        copy.wait()

    left, right = gy > 0, gy < gyn - 1
    up, down = gx > 0, gx < gxn - 1
    row16 = lax.broadcasted_iota(jnp.int32, (16, 256), 0)
    from_left = jnp.logical_and(row16 < 4, left)
    from_right = jnp.logical_and(jnp.logical_and(row16 >= 4, row16 < 8), right)

    def halo(index, left_rows, right_rows, ok):
        rows = jnp.where(from_left, left_rows.astype(F32), jnp.where(from_right, right_rows.astype(F32), 0.0))
        if ok is not None:
            rows = jnp.where(ok, rows, 0.0)
        spread = dot(rows.astype(BF16), depth_map[...]).astype(BF16)
        for t in range(3):
            xs[index, t * 80 + 64:t * 80 + 80] = spread[:, t * 256:t * 256 + 256]

    for x in range(8):
        halo(x + 1, hlr[0, x], hlr[1, x], None)
    for a, ok in ((0, up), (1, down)):
        index = 0 if a == 0 else 9
        rows = jnp.concatenate([hx[a, n].reshape(64, 128) for n in range(2)], axis=1)
        slab(index, jnp.where(ok, rows.astype(F32), 0.0).astype(BF16))
        halo(index, hc[a, 0], hc[a, 1], ok)

    b1all = jnp.concatenate([b1] * 16, axis=0)

    def layer1(j, _):
        total = None
        for px in range(2):
            x = 2 * j + px
            pre = dot(w1[...], xs[pl.ds(x, 3)].reshape(720, 256)) + b1all
            t = jnp.tanh(0.5 * pre)
            value = pre * (0.65 + 0.35 * t)
            sl[x] = 0.65 + 0.35 * t + 0.175 * pre * (1.0 - t * t)
            value = value[:256] + value[256:]
            value = value[:, :128] + value[:, 128:]
            total = value if total is None else total + value
        pool[j + 1, 1, 32:288] = (total * 0.125).astype(BF16)
        return 0

    lax.fori_loop(0, 4, layer1, 0)

    def exchange(ref, where, unit, base):
        copies = []
        for k, (sx, sy) in enumerate(DIRS):
            src_x, dst_x = {0: (pl.ds(1, 4),) * 2, 1: (4, 0), -1: (1, 5)}[sx]
            src_y, dst_y = {0: (pl.ds(unit, 8 * unit),) * 2, 1: (pl.ds(8 * unit, unit), pl.ds(0, unit)),
                            -1: (pl.ds(unit, unit), pl.ds(9 * unit, unit))}[sy]
            copies.append(
                remote(ref.at[(src_x,) + where + (src_y,)], ref.at[(dst_x,) + where + (dst_y,)], base + k, at(sx, sy))
            )
            copies[-1].start()
        return copies

    def clear(ref, where, unit):
        for ok, index in ((up, 0), (down, 5)):
            @pl.when(jnp.logical_not(ok))
            def _(index=index):
                ref[(index,) + where] = jnp.zeros((10 * unit, 128), BF16)
        for ok, index in ((left, 0), (right, 9 * unit)):
            @pl.when(jnp.logical_not(ok))
            def _(index=index):
                ref[(slice(None),) + where + (slice(index, index + unit),)] = jnp.zeros((6, unit, 128), BF16)

    for copy in exchange(pool, (1,), 32, 8):
        copy.wait()
    clear(pool, (1,), 32)
    for i in range(6):
        spread = dot(pool[i, 1], pool_map[...]).astype(BF16)
        pool[i, 0] = spread[:, :128]
        pool[i, 2] = spread[:, 128:]

    def cell(ref, i, where, start, size):
        rows = pl.ds(start, size)
        return jnp.concatenate([ref[(i,) + where + (rows,)], ref[(i + 2,) + where + (rows,)]], axis=1)

    for j in range(2):
        def layer2(y, _, j=j):
            patch = jnp.concatenate(
                [cell(pool, j + dx, (dz,), pl.multiple_of((y + dy) * 32, 32), 32)
                 for dx in range(3) for dy in range(3) for dz in range(3)], axis=0)
            pre = dot(w2[...], patch) + b2
            t = jnp.tanh(0.5 * pre)
            slope = 0.65 + 0.35 * t + 0.175 * pre * (1.0 - t * t)
            grad = (slope * cots[pl.ds(pl.multiple_of((y // 2) * 64, 64), 64), :]).astype(BF16)
            rows = pl.ds(pl.multiple_of((y + 1) * 64, 64), 64)
            gs[j + 1, rows] = grad[:, :128]
            gs[j + 3, rows] = grad[:, 128:]
            return 0

        lax.fori_loop(0, 8, layer2, 0)

    third = exchange(gs, (), 64, 16)

    for j in range(2):
        def weights2(y, _, j=j):
            grad = cell(gs, j + 1, (), pl.multiple_of((y + 1) * 64, 64), 64)
            for half in range(2):
                patch = jnp.concatenate(
                    [cell(pool, j + dx, (dz,), pl.multiple_of((y + dy) * 32 + half * 16, 16), 16)
                     for dx in range(3) for dy in range(3) for dz in range(3)], axis=0)
                acc2[half, :, 0:432] += dot_nt(grad, patch)
            return 0

        lax.fori_loop(0, 8, weights2, 0)
    pair2 = remote(acc2.at[1 - dp], r2dp, 24, (gx, gy, 1 - dp))
    pair2.start()
    for copy in third:
        copy.wait()
    clear(gs, (), 64)

    for j in range(2):
        def back2(y, _, j=j):
            patch = jnp.concatenate(
                [cell(gs, j + u, (), pl.multiple_of(y * 64, 64), 192) for u in range(3)], axis=0)
            terms = dot(w2b[...], patch) * 0.125
            rows = pl.ds(pl.multiple_of(y * 32, 32), 32)
            for h in range(2):
                part = terms[:, h * 128:h * 128 + 128]
                gp[j + 2 * h, rows] = part[32:64] + before2(part[64:96]) + after2(part[0:32])
            return 0

        lax.fori_loop(0, 8, back2, 0)

    pair2.wait()
    s2a[...] = (acc2[dp] + r2dp[...]).reshape(gxn, 8, 512)
    along2 = []
    for d in range(1, gxn):
        along2.append(remote(s2a.at[lax.rem(gx + d, gxn)], r2gx.at[d - 1], 24 + d, at(d, 0)))
        along2[-1].start()

    def back1(x, _):
        spread = gp[x // 2]
        spread = jnp.concatenate([spread, spread], axis=1)
        spread = jnp.concatenate([spread, spread], axis=0)
        grad = (sl[x] * spread).astype(BF16)
        gf[x] = grad
        gi[pl.ds(x, 3)] += dot(w1tr[...], grad).reshape(3, 240, 256)
        return 0

    lax.fori_loop(0, 8, back1, 0)

    def combine(x):
        return gi[x, 80:152] + before(gi[x, 160:232]) + after(gi[x, 0:72])

    for i, x in ((0, 0), (1, 9)):
        edge = combine(x)
        sx_[i] = edge[:64]
        sc[i] = edge[64:]

    def sum_terms(x, _):
        inner = combine(x + 1)
        gi[x + 1, 80:144] = inner[:64]
        sby[x] = inner[64:]
        return 0

    lax.fori_loop(0, 8, sum_terms, 0)
    fourth = []
    for k, (sx, sy) in enumerate(DIRS):
        a, b = (0 if sx == 1 else 1), (0 if sy == 1 else 1)
        if sx == 0:
            src, dst = sby, ry.at[b]
        elif sy == 0:
            src, dst = sx_.at[1 if sx == 1 else 0], rx.at[a]
        else:
            src, dst = sc.at[1 if sx == 1 else 0], rc.at[a, b]
        fourth.append(remote(src, dst, 40 + k, at(sx, sy)))
        fourth[-1].start()

    for copy in along2:
        copy.wait()
    total2 = s2a[gx]
    for d in range(1, gxn):
        total2 = total2 + r2gx[d - 1]
    for g in range(8):
        s2b[g] = total2[g:g + 1]
    across2 = []
    for d in range(1, gyn):
        across2.append(remote(s2b.at[lax.rem(gy + d, gyn)], r2gy.at[d - 1], 31 + d, at(0, d)))
        across2[-1].start()

    def weights1(x, _):
        acc1[...] += dot_nt(gf[x], xs[pl.ds(x, 3)].reshape(720, 256))
        return 0

    lax.fori_loop(0, 8, weights1, 0)
    taps = None
    for dy in range(3):
        kept = None
        for r in range(16):
            y = 2 * (r % 8) + r // 8
            term = jnp.where(place[...] == float(y + dy - 1), acc1[r * 32:r * 32 + 32], 0.0)
            kept = term if kept is None else kept + term
        high = kept.astype(BF16)
        rest = kept - high.astype(F32)
        mid = rest.astype(BF16)
        low = (rest - mid.astype(F32)).astype(BF16)
        parts = dot(jnp.concatenate([high, mid, low], axis=0), gather[dy])
        parts = parts[:32] + parts[32:64] + parts[64:]
        taps = parts if taps is None else taps + parts
    for g in range(8):
        s1[g] = taps[4 * g:4 * g + 4]
    pair1 = remote(s1, r1dp, 48, (gx, gy, 1 - dp))
    pair1.start()

    for copy in fourth:
        copy.wait()
    y16 = lax.broadcasted_iota(jnp.int32, (4, 16, 256), 1)

    def ends(low_rows, high_rows):
        low_part = jnp.where(jnp.logical_and(y16 == 0, left), low_rows[4:8][:, None, :], 0.0)
        high_part = jnp.where(jnp.logical_and(y16 == 15, right), high_rows[0:4][:, None, :], 0.0)
        return (low_part + high_part).reshape(64, 256)

    for a, ok, x in ((0, up, 1), (1, down, 8)):
        term = rx[a] + ends(rc[a, 0], rc[a, 1])
        gi[x, 80:144] += jnp.where(ok, term, 0.0)

    def finish(x, _):
        total = (gi[x + 1, 80:144] + ends(ry[0, x], ry[1, x])).astype(BF16)
        natural = dot(total, restore[...]).astype(BF16)
        for n in range(2):
            out[n, :, x] = natural[:, n * 128:n * 128 + 128].reshape(4, 16, 128)
        return 0

    lax.fori_loop(0, 8, finish, 0)

    pair1.wait()
    s1a[...] = s1[...] + r1dp[...]
    along1 = []
    for d in range(1, gxn):
        along1.append(remote(s1a.at[lax.rem(gx + d, gxn)], r1gx.at[d - 1], 48 + d, at(d, 0)))
        along1[-1].start()
    for copy in across2:
        copy.wait()
    total2 = s2b[gy]
    for d in range(1, gyn):
        total2 = total2 + r2gy[d - 1]
    gw2[...] = total2 * (1.0 / (CELLS / 8) ** 0.5)
    for copy in along1:
        copy.wait()
    total1 = s1a[gx]
    for d in range(1, gxn):
        total1 = total1 + r1gx[d - 1]
    s1b[...] = total1
    across1 = []
    for d in range(1, gyn):
        across1.append(remote(s1b, r1gy.at[d - 1], 55 + d, at(0, d)))
        across1[-1].start()
    for copy in across1:
        copy.wait()
    total1 = s1b[...]
    for d in range(1, gyn):
        total1 = total1 + r1gy[d - 1]
    mine = None
    for q in range(4):
        for c in range(4):
            ok = jnp.logical_and(gy // 2 == q, (gy % 2) * 2 + dp == c)
            term = jnp.where(ok, total1[q:q + 1, c * 32:c * 32 + 32], 0.0)
            mine = term if mine is None else mine + term
    gw1[:, 0:32] = mine * (1.0 / CELLS ** 0.5)


def on_device(gxn, gyn, consts, inputs, cotangent, w_first, w_second, b_first, b_second):
    cot = jnp.transpose(cotangent, (0, 2, 3, 4, 1)).reshape(512, 64)
    w1t = jnp.transpose(w_first, (2, 3, 4, 1, 0)).reshape(108, 32)
    w2t = jnp.transpose(w_second, (2, 3, 4, 1, 0)).reshape(864, 64)
    vmem = pl.BlockSpec(memory_space=pltpu.VMEM)
    operands = (inputs, cot, w1t, w2t, b_first.reshape(1, 32), b_second.reshape(1, 64), *consts)
    scratch = [
        ((10, 240, 256), BF16), ((8, 16, 256), BF16), ((2, 8, 16, 256), BF16), ((2, 2, 4, 16, 128), BF16),
        ((2, 2, 16, 256), BF16), ((512, 720), BF16), ((720, 512), BF16), ((64, 864), BF16), ((96, 576), BF16),
        ((128, 128), F32), ((128, 128), F32), ((8, 512, 256), F32), ((8, 512, 256), BF16), ((6, 3, 320, 128), BF16),
        ((256, 256), F32), ((6, 640, 128), BF16), ((4, 256, 128), F32),
        ((2, 64, 512), F32), ((64, 512), F32), ((gxn, 8, 512), F32), ((gxn - 1, 8, 512), F32), ((gyn, 1, 512), F32),
        ((gyn - 1, 1, 512), F32), ((10, 240, 256), F32), ((8, 8, 256), F32), ((2, 8, 8, 256), F32),
        ((2, 64, 256), F32), ((2, 64, 256), F32), ((2, 8, 256), F32), ((2, 2, 8, 256), F32), ((512, 720), F32),
        ((gxn, 4, 128), F32), ((gxn, 4, 128), F32), ((gxn, 4, 128), F32), ((gxn - 1, 4, 128), F32), ((4, 128), F32),
        ((gyn - 1, 4, 128), F32),
    ]
    result, part1, part2 = pl.pallas_call(
        functools.partial(kernel, gxn, gyn),
        out_shape=(
            jax.ShapeDtypeStruct(inputs.shape, BF16),
            jax.ShapeDtypeStruct((1, 128), F32),
            jax.ShapeDtypeStruct((1, 512), F32),
        ),
        in_specs=[vmem] * len(operands),
        out_specs=(vmem, vmem, vmem),
        scratch_shapes=[pltpu.VMEM(s, d) for s, d in scratch]
        + [pltpu.SemaphoreType.DMA((63,)), pltpu.SemaphoreType.DMA((63,))],
        compiler_params=pltpu.CompilerParams(
            collective_id=0, has_side_effects=True, vmem_limit_bytes=60 * 1024 * 1024
        ),
    )(*operands)
    grad_w2 = jnp.transpose(part2[0, :432].reshape(27, 16)).reshape(432)
    return result, part1[0, :27], grad_w2


def solution(mesh):
    consts = constants()
    return jax.shard_map(
        functools.partial(on_device, mesh.shape["gx"], mesh.shape["gy"], consts),
        mesh=mesh,
        in_specs=(P("dp", None, "gx", "gy", None), P("dp", None, "gx", "gy", None), P(), P(), P(), P()),
        out_specs=(P("dp", None, "gx", "gy", None), P(("gx", "gy", "dp")), P(("gx", "gy", "dp"))),
        check_vma=False,
    )
```

```python
import functools

import jax
import jax.numpy as jnp
import ml_dtypes
import numpy as np
from jax import lax
from jax.experimental import pallas as pl
from jax.experimental.pallas import tpu as pltpu
from jax.sharding import PartitionSpec as P

MESH = pl.DeviceIdType.MESH
F32 = jnp.float32
BF16 = jnp.bfloat16
DIRS = [(0, 1), (0, -1), (1, 0), (-1, 0), (1, 1), (1, -1), (-1, 1), (-1, -1)]
CELLS = 4194304
NCONST = 10


def constants():
    depth_map = np.zeros((256, 768), np.float32)
    for n in range(2):
        for z in range(128):
            lane = (z % 2) * 128 + (z // 2 % 2) * 64 + n * 32 + z // 4
            for t in range(3):
                src = z + t - 1
                if 0 <= src < 128:
                    depth_map[n * 128 + src, t * 256 + lane] = 1
    restore = depth_map[:, 256:512].T.copy()
    pool_map = np.zeros((128, 256), np.float32)
    for n in range(2):
        for z in range(64):
            lane = (z % 2) * 64 + n * 32 + z // 2
            for half, src in ((0, z - 1), (1, z + 1)):
                if 0 <= src < 64:
                    pool_map[(src % 2) * 64 + n * 32 + src // 2, half * 128 + lane] = 1
    cot_map = np.zeros((128, 256), np.float32)
    for h in range(2):
        for b in range(2):
            for n in range(2):
                for k in range(32):
                    cot_map[n * 64 + h * 32 + k, h * 128 + b * 64 + n * 32 + k] = 1
    place = np.full((80,), -100.0, np.float32)
    chan = np.full((80,), -1)
    for c in range(4):
        for y in range(-1, 17):
            row = 64 + c if y < 0 else 68 + c if y > 15 else c * 16 + y
            place[row] = y
            chan[row] = c
    toeplitz = np.zeros((128, 3 * 768), np.float32)
    gather = np.zeros((720, 128), np.float32)
    for dx in range(3):
        for dz in range(3):
            group = dx * 240 + dz * 80
            for c in range(4):
                for dy in range(3):
                    toeplitz[((dx * 3 + dy) * 3 + dz) * 4 + c, (group + c * 16 + dy - 1) % 768] = 1
                toeplitz[((dx * 3 + 0) * 3 + dz) * 4 + c, 768 + group + 64 + c] = 1
                toeplitz[((dx * 3 + 2) * 3 + dz) * 4 + c, 1536 + group + 68 + c] = 1
            for row in range(72):
                gather[group + row, chan[row] * 32 + dx * 9 + dz] = 1
    reorder = np.zeros((432, 432), np.float32)
    for tap in range(27):
        for c in range(16):
            reorder[tap * 16 + c, c * 27 + tap] = 1
    select = np.zeros((16, 64), np.float32)
    for c in range(4):
        select[c, c * 16 + 15] = 1
        select[4 + c, c * 16] = 1
    b16 = lambda v: v.astype(ml_dtypes.bfloat16)
    return (
        b16(depth_map), b16(restore), b16(pool_map), b16(cot_map), b16(toeplitz), b16(gather), b16(select),
        b16(np.eye(128, dtype=np.float32)), b16(reorder), np.pad(np.tile(place, 9), (0, 48), constant_values=-100)[None, :],
    )


def dot(a, b):
    return jnp.dot(a, b, preferred_element_type=F32)


def dot_nt(a, b):
    return lax.dot_general(a, b, (((1,), (1,)), ((), ())), preferred_element_type=F32)


def split_dot(a, b):
    high = a.astype(BF16)
    rest = a - high.astype(F32)
    mid = rest.astype(BF16)
    low = (rest - mid.astype(F32)).astype(BF16)
    parts = dot(jnp.concatenate([high.astype(F32), mid.astype(F32), low.astype(F32)], axis=0).astype(BF16), b)
    rows = a.shape[0]
    return parts[:rows] + parts[rows:2 * rows] + parts[2 * rows:]


def before2(u):
    lane = lax.broadcasted_iota(jnp.int32, u.shape, 1)
    return jnp.where(
        lane < 64, jnp.where(lane % 32 != 0, pltpu.roll(u, 65, 1), 0.0), pltpu.roll(u, 64, 1)
    )


def after2(u):
    lane = lax.broadcasted_iota(jnp.int32, u.shape, 1)
    return jnp.where(
        lane >= 64, jnp.where(lane % 32 != 31, pltpu.roll(u, 63, 1), 0.0), pltpu.roll(u, 64, 1)
    )


def before(v):
    return jnp.concatenate([before2(v[:, 128:]), v[:, :128]], axis=1)


def after(v):
    return jnp.concatenate([v[:, 128:], after2(v[:, :128])], axis=1)


def kernel(
    gxn, gyn,
    inp, cot, w1t, w2t, b1r, b2r, *rest):
    fixed, rest = rest[:NCONST], rest[NCONST:]
    out, gw1, gw2 = rest[:3]
    kept, rest = rest[3:3 + NCONST], rest[3 + NCONST:]
    (xs, hb, hlr, hx, hc, w1, w1tr, w2, w2b, bias1, bias2, sl, gf, pool, cots, gs, gp,
    acc2, r2dp, s2a, r2gx, s2b, r2gy, gi, sby, ry, sx_, rx, sc, rc, acc1, s1, r1dp, s1a, r1gx, s1b, r1gy,
    w1f, ssem, rsem, lsem) = rest
    depth_map, restore, pool_map, cot_map, toeplitz, gather, select, eye, reorder, place = kept
    loads = [pltpu.make_async_copy(fixed[i], kept[i], lsem.at[i]) for i in range(NCONST)]
    for load in loads:
        load.start()
    gx, gy, dp = lax.axis_index("gx"), lax.axis_index("gy"), lax.axis_index("dp")

    def at(sx, sy):
        return (lax.rem(gx + sx + gxn, gxn), lax.rem(gy + sy + gyn, gyn), dp)

    def remote(src, dst, k, device):
        return pltpu.make_async_remote_copy(
            src_ref=src, dst_ref=dst, send_sem=ssem.at[k], recv_sem=rsem.at[k], device_id=device, device_id_type=MESH
        )

    barrier = pltpu.get_barrier_semaphore()
    peers = [at(*d) for d in DIRS]
    peers += [at(d, 0) for d in range(2, gxn - 1)] + [at(0, d) for d in range(2, gyn - 1)]
    peers += [(gx, gy, 1 - dp)]
    for peer in peers:
        pl.semaphore_signal(barrier, inc=1, device_id=peer, device_id_type=MESH)

    def raw(x):
        halves = [inp[n, :, x].reshape(64, 128) for n in range(2)]
        return jnp.concatenate(halves, axis=1)

    loads[6].wait()
    for x in range(8):
        hb[x] = dot(select[...], raw(x)).astype(BF16)
    pl.semaphore_wait(barrier, len(peers))
    first = []
    for k, (sx, sy) in enumerate(DIRS):
        a, b = (0 if sx == 1 else 1), (0 if sy == 1 else 1)
        if sx == 0:
            src, dst = hb, hlr.at[b]
        elif sy == 0:
            src, dst = inp.at[:, :, 7 if sx == 1 else 0], hx.at[a]
        else:
            src, dst = hb.at[7 if sx == 1 else 0], hc.at[a, b]
        first.append(remote(src, dst, k, at(sx, sy)))
        first[-1].start()

    for i, load in enumerate(loads):
        if i != 6:
            load.wait()
    w1f[...] = jnp.zeros_like(w1f)
    for tap in range(27):
        w1f[tap * 4:tap * 4 + 4] = w1t[tap].astype(F32)
    small = dot_nt(eye[:32, :32], w1f[...].astype(BF16)).astype(BF16)
    base = dot(small, toeplitz[...])
    for r in range(16):
        y = 2 * (r % 8) + r // 8
        block = base[:, :768] if y == 0 else pltpu.roll(base[:, :768], y, 1)
        block = jnp.where(jnp.abs(place[...] - float(y)) < 1.5, block, 0.0)
        if y == 0:
            block = block + base[:, 768:1536]
        if y == 15:
            block = block + base[:, 1536:]
        w1[r * 32:r * 32 + 32, :] = block[:, :720].astype(BF16)
    for b in range(6):
        width = min(128, 720 - b * 128)
        w1tr[b * 128:b * 128 + width] = dot_nt(eye[:width, :width], w1[:, b * 128:b * 128 + width]).astype(BF16)
    w2[...] = dot_nt(eye[:64, :64], w2t[...]).astype(BF16)
    for dx in range(3):
        for dy in range(3):
            at_lane = ((2 - dx) * 3 + 2 - dy) * 64
            row = (dx * 3 + dy) * 96
            w2b[:, at_lane:at_lane + 64] = w2t[row:row + 96, :]
    bias1[...] = jnp.zeros_like(bias1)
    bias1[:, 0:32] = jnp.broadcast_to(b1r[...], (128, 32))
    bias2[...] = jnp.zeros_like(bias2)
    bias2[:, 0:64] = jnp.broadcast_to(b2r[...], (128, 64))
    b1 = jnp.transpose(bias1[...])[:32]
    b2 = jnp.transpose(bias2[...])[:64]
    b1 = jnp.concatenate([b1, b1], axis=1)
    b2 = jnp.concatenate([b2, b2], axis=1)
    for q in range(4):
        part = jnp.concatenate(
            [cot[(n * 8 + h * 4 + q) * 32:(n * 8 + h * 4 + q) * 32 + 32, :] for n in range(2) for h in range(2)], axis=0
        )
        turned = dot_nt(eye[:64, :64], part).astype(BF16)
        cots[q * 64:q * 64 + 64] = dot(turned, cot_map[...]) * 0.125

    def slab(index, rows):
        spread = dot(rows, depth_map[...]).astype(BF16)
        for t in range(3):
            xs[index, t * 80:t * 80 + 64] = spread[:, t * 256:t * 256 + 256]

    for x in range(8):
        slab(x + 1, raw(x))
    acc2[...] = jnp.zeros_like(acc2)
    for copy in first:
        copy.wait()

    left, right = gy > 0, gy < gyn - 1
    up, down = gx > 0, gx < gxn - 1
    row16 = lax.broadcasted_iota(jnp.int32, (16, 256), 0)
    from_left = jnp.logical_and(row16 < 4, left)
    from_right = jnp.logical_and(jnp.logical_and(row16 >= 4, row16 < 8), right)

    def halo(index, left_rows, right_rows, ok):
        rows = jnp.where(from_left, left_rows.astype(F32), jnp.where(from_right, right_rows.astype(F32), 0.0))
        if ok is not None:
            rows = jnp.where(ok, rows, 0.0)
        spread = dot(rows.astype(BF16), depth_map[...]).astype(BF16)
        for t in range(3):
            xs[index, t * 80 + 64:t * 80 + 80] = spread[:, t * 256:t * 256 + 256]

    for x in range(8):
        halo(x + 1, hlr[0, x], hlr[1, x], None)
    for a, ok in ((0, up), (1, down)):
        index = 0 if a == 0 else 9
        rows = jnp.concatenate([hx[a, n].reshape(64, 128) for n in range(2)], axis=1)
        slab(index, jnp.where(ok, rows.astype(F32), 0.0).astype(BF16))
        halo(index, hc[a, 0], hc[a, 1], ok)

    b1all = jnp.concatenate([b1] * 16, axis=0)

    def layer1(j, _):
        total = None
        for px in range(2):
            x = 2 * j + px
            pre = dot(w1[...], xs[pl.ds(x, 3)].reshape(720, 256)) + b1all
            t = jnp.tanh(0.5 * pre)
            value = pre * (0.65 + 0.35 * t)
            sl[x] = 0.65 + 0.35 * t + 0.175 * pre * (1.0 - t * t)
            value = value[:256] + value[256:]
            value = value[:, :128] + value[:, 128:]
            total = value if total is None else total + value
        pool[j + 1, 1, 32:288] = (total * 0.125).astype(BF16)
        return 0

    lax.fori_loop(0, 4, layer1, 0, unroll=True)

    def exchange(ref, where, unit, base):
        copies = []
        for k, (sx, sy) in enumerate(DIRS):
            src_x, dst_x = {0: (pl.ds(1, 4),) * 2, 1: (4, 0), -1: (1, 5)}[sx]
            src_y, dst_y = {0: (pl.ds(unit, 8 * unit),) * 2, 1: (pl.ds(8 * unit, unit), pl.ds(0, unit)),
                            -1: (pl.ds(unit, unit), pl.ds(9 * unit, unit))}[sy]
            copies.append(
                remote(ref.at[(src_x,) + where + (src_y,)], ref.at[(dst_x,) + where + (dst_y,)], base + k, at(sx, sy))
            )
            copies[-1].start()
        return copies

    def clear(ref, where, unit):
        for ok, index in ((up, 0), (down, 5)):
            @pl.when(jnp.logical_not(ok))
            def _(index=index):
                ref[(index,) + where] = jnp.zeros((10 * unit, 128), BF16)
        for ok, index in ((left, 0), (right, 9 * unit)):
            @pl.when(jnp.logical_not(ok))
            def _(index=index):
                ref[(slice(None),) + where + (slice(index, index + unit),)] = jnp.zeros((6, unit, 128), BF16)

    for copy in exchange(pool, (1,), 32, 8):
        copy.wait()
    clear(pool, (1,), 32)
    for i in range(6):
        spread = dot(pool[i, 1], pool_map[...]).astype(BF16)
        pool[i, 0] = spread[:, :128]
        pool[i, 2] = spread[:, 128:]

    def cell(ref, i, where, start, size):
        rows = pl.ds(start, size)
        return jnp.concatenate([ref[(i,) + where + (rows,)], ref[(i + 2,) + where + (rows,)]], axis=1)

    for j in range(2):
        def layer2(y, _, j=j):
            patch = jnp.concatenate(
                [cell(pool, j + dx, (dz,), pl.multiple_of((y + dy) * 32, 32), 32)
                 for dx in range(3) for dy in range(3) for dz in range(3)], axis=0)
            pre = dot(w2[...], patch) + b2
            t = jnp.tanh(0.5 * pre)
            slope = 0.65 + 0.35 * t + 0.175 * pre * (1.0 - t * t)
            grad = (slope * cots[pl.ds(pl.multiple_of((y // 2) * 64, 64), 64), :]).astype(BF16)
            rows = pl.ds(pl.multiple_of((y + 1) * 64, 64), 64)
            gs[j + 1, rows] = grad[:, :128]
            gs[j + 3, rows] = grad[:, 128:]
            return 0

        lax.fori_loop(0, 8, layer2, 0, unroll=True)

    third = exchange(gs, (), 64, 16)

    for j in range(2):
        def weights2(y, _, j=j):
            grad = cell(gs, j + 1, (), pl.multiple_of((y + 1) * 64, 64), 64)
            for half in range(2):
                patch = jnp.concatenate(
                    [cell(pool, j + dx, (dz,), pl.multiple_of((y + dy) * 32 + half * 16, 16), 16)
                     for dx in range(3) for dy in range(3) for dz in range(3)], axis=0)
                acc2[half, :, 0:432] += dot_nt(grad, patch)
            return 0

        lax.fori_loop(0, 8, weights2, 0, unroll=True)
    pair2 = remote(acc2.at[1 - dp], r2dp, 24, (gx, gy, 1 - dp))
    pair2.start()
    for copy in third:
        copy.wait()
    clear(gs, (), 64)

    for j in range(2):
        def back2(y, _, j=j):
            patch = jnp.concatenate(
                [cell(gs, j + u, (), pl.multiple_of(y * 64, 64), 192) for u in range(3)], axis=0)
            terms = dot(w2b[...], patch) * 0.125
            rows = pl.ds(pl.multiple_of(y * 32, 32), 32)
            for h in range(2):
                part = terms[:, h * 128:h * 128 + 128]
                gp[j + 2 * h, rows] = part[32:64] + before2(part[64:96]) + after2(part[0:32])
            return 0

        lax.fori_loop(0, 8, back2, 0, unroll=True)

    pair2.wait()
    s2a[...] = (acc2[dp] + r2dp[...]).reshape(gxn, 8, 512)
    along2 = []
    for d in range(1, gxn):
        along2.append(remote(s2a.at[lax.rem(gx + d, gxn)], r2gx.at[d - 1], 24 + d, at(d, 0)))
        along2[-1].start()

    for x in range(8):
        spread = gp[x // 2]
        spread = jnp.concatenate([spread, spread], axis=1)
        spread = jnp.concatenate([spread, spread], axis=0)
        gf[x] = (sl[x] * spread).astype(BF16)
    for x in range(8):
        term = dot_nt(gf[x], xs[x:x + 3].reshape(720, 256))
        acc1[...] = term if x == 0 else acc1[...] + term

    taps = None
    for dy in range(3):
        kept = None
        for r in range(16):
            y = 2 * (r % 8) + r // 8
            term = jnp.where(place[:, :720] == float(y + dy - 1), acc1[r * 32:r * 32 + 32], 0.0)
            kept = term if kept is None else kept + term
        parts = split_dot(kept, gather[...])
        if dy:
            parts = pltpu.roll(parts, 3 * dy, 1)
        taps = parts if taps is None else taps + parts
    for g in range(8):
        s1[g] = taps[4 * g:4 * g + 4]
    pair1 = remote(s1, r1dp, 48, (gx, gy, 1 - dp))
    pair1.start()
    for copy in along2:
        copy.wait()
    total2 = s2a[gx]
    for d in range(1, gxn):
        total2 = total2 + r2gx[d - 1]
    for g in range(8):
        s2b[g] = total2[g:g + 1]
    across2 = []
    for d in range(1, gyn):
        across2.append(remote(s2b.at[lax.rem(gy + d, gyn)], r2gy.at[d - 1], 31 + d, at(0, d)))
        across2[-1].start()

    for x in range(8):
        term = dot(w1tr[...], gf[x]).reshape(3, 240, 256)
        if x == 0:
            gi[0:3] = term
        else:
            gi[x:x + 2] += term[:2]
            gi[x + 2] = term[2]
        if x == 3:
            pair1.wait()
            s1a[...] = s1[...] + r1dp[...]
            along1 = []
            for d in range(1, gxn):
                along1.append(remote(s1a.at[lax.rem(gx + d, gxn)], r1gx.at[d - 1], 48 + d, at(d, 0)))
                along1[-1].start()

    def combine(x):
        return gi[x, 80:152] + before(gi[x, 160:232]) + after(gi[x, 0:72])

    for i, x in ((0, 0), (1, 9)):
        edge = combine(x)
        sx_[i] = edge[:64]
        sc[i] = edge[64:]
    for x in range(8):
        inner = combine(x + 1)
        gi[x + 1, 80:144] = inner[:64]
        sby[x] = inner[64:]
    fourth = []
    for k, (sx, sy) in enumerate(DIRS):
        a, b = (0 if sx == 1 else 1), (0 if sy == 1 else 1)
        if sx == 0:
            src, dst = sby, ry.at[b]
        elif sy == 0:
            src, dst = sx_.at[1 if sx == 1 else 0], rx.at[a]
        else:
            src, dst = sc.at[1 if sx == 1 else 0], rc.at[a, b]
        fourth.append(remote(src, dst, 40 + k, at(sx, sy)))
        fourth[-1].start()
    for copy in along1:
        copy.wait()
    total1 = s1a[gx]
    for d in range(1, gxn):
        total1 = total1 + r1gx[d - 1]
    s1b[...] = total1
    across1 = []
    for d in range(1, gyn):
        across1.append(remote(s1b, r1gy.at[d - 1], 55 + d, at(0, d)))
        across1[-1].start()
    for copy in across2:
        copy.wait()
    total2 = s2b[gy]
    for d in range(1, gyn):
        total2 = total2 + r2gy[d - 1]
    total2 = jnp.concatenate([total2 * (1.0 / (CELLS / 8) ** 0.5)] * 8, axis=0)[:, :432]
    gw2[...] = split_dot(total2, reorder[...])[0:1]

    for copy in fourth:
        copy.wait()
    y16 = lax.broadcasted_iota(jnp.int32, (4, 16, 256), 1)

    def ends(low_rows, high_rows):
        low_part = jnp.where(jnp.logical_and(y16 == 0, left), low_rows[4:8][:, None, :], 0.0)
        high_part = jnp.where(jnp.logical_and(y16 == 15, right), high_rows[0:4][:, None, :], 0.0)
        return (low_part + high_part).reshape(64, 256)

    for a, ok, x in ((0, up, 1), (1, down, 8)):
        term = rx[a] + ends(rc[a, 0], rc[a, 1])
        gi[x, 80:144] += jnp.where(ok, term, 0.0)

    def finish(x, _):
        total = (gi[x + 1, 80:144] + ends(ry[0, x], ry[1, x])).astype(BF16)
        natural = dot(total, restore[...]).astype(BF16)
        for n in range(2):
            out[n, :, x] = natural[:, n * 128:n * 128 + 128].reshape(4, 16, 128)
        return 0

    lax.fori_loop(0, 8, finish, 0, unroll=True)

    for copy in across1:
        copy.wait()
    total1 = s1b[...]
    for d in range(1, gyn):
        total1 = total1 + r1gy[d - 1]
    mine = None
    for q in range(4):
        for c in range(4):
            ok = jnp.logical_and(gy // 2 == q, (gy % 2) * 2 + dp == c)
            term = jnp.where(ok, total1[q:q + 1, c * 32:c * 32 + 32], 0.0)
            mine = term if mine is None else mine + term
    gw1[...] = mine[:, 0:27] * (1.0 / CELLS ** 0.5)


def on_device(gxn, gyn, consts, inputs, cotangent, w_first, w_second, b_first, b_second):
    cot = jnp.transpose(cotangent, (0, 2, 3, 4, 1)).reshape(512, 64)
    w1t = jnp.transpose(w_first, (2, 3, 4, 1, 0)).reshape(27, 4, 32)
    w2t = jnp.transpose(w_second, (2, 3, 4, 1, 0)).reshape(864, 64)
    vmem = pl.BlockSpec(memory_space=pltpu.VMEM)
    operands = (inputs, cot, w1t, w2t, b_first.reshape(1, 32), b_second.reshape(1, 64), *consts)
    scratch = [
        ((10, 240, 256), BF16), ((8, 16, 256), BF16), ((2, 8, 16, 256), BF16), ((2, 2, 4, 16, 128), BF16),
        ((2, 2, 16, 256), BF16), ((512, 720), BF16), ((720, 512), BF16), ((64, 864), BF16), ((96, 576), BF16),
        ((128, 128), F32), ((128, 128), F32), ((8, 512, 256), F32), ((8, 512, 256), BF16), ((6, 3, 320, 128), BF16),
        ((256, 256), F32), ((6, 640, 128), BF16), ((4, 256, 128), F32),
        ((2, 64, 512), F32), ((64, 512), F32), ((gxn, 8, 512), F32), ((gxn - 1, 8, 512), F32), ((gyn, 1, 512), F32),
        ((gyn - 1, 1, 512), F32), ((10, 240, 256), F32), ((8, 8, 256), F32), ((2, 8, 8, 256), F32),
        ((2, 64, 256), F32), ((2, 64, 256), F32), ((2, 8, 256), F32), ((2, 2, 8, 256), F32), ((512, 720), F32),
        ((gxn, 4, 128), F32), ((gxn, 4, 128), F32), ((gxn, 4, 128), F32), ((gxn - 1, 4, 128), F32), ((4, 128), F32),
        ((gyn - 1, 4, 128), F32), ((128, 32), F32),
    ]
    result, part1, part2 = pl.pallas_call(
        functools.partial(kernel, gxn, gyn),
        out_shape=(
            jax.ShapeDtypeStruct(inputs.shape, BF16),
            jax.ShapeDtypeStruct((1, 27), F32),
            jax.ShapeDtypeStruct((1, 432), F32),
        ),
        in_specs=[vmem] * 6 + [pl.BlockSpec(memory_space=pl.ANY)] * NCONST,
        out_specs=(vmem, vmem, vmem),
        scratch_shapes=[pltpu.VMEM(c.shape, c.dtype) for c in consts]
        + [pltpu.VMEM(s, d) for s, d in scratch]
        + [pltpu.SemaphoreType.DMA((63,)), pltpu.SemaphoreType.DMA((63,)), pltpu.SemaphoreType.DMA((NCONST,))],
        compiler_params=pltpu.CompilerParams(
            collective_id=0, has_side_effects=True, vmem_limit_bytes=60 * 1024 * 1024
        ),
    )(*operands)
    return result, part1.reshape(27), part2.reshape(432)


def solution(mesh):
    consts = constants()
    return jax.shard_map(
        functools.partial(on_device, mesh.shape["gx"], mesh.shape["gy"], consts),
        mesh=mesh,
        in_specs=(P("dp", None, "gx", "gy", None), P("dp", None, "gx", "gy", None), P(), P(), P(), P()),
        out_specs=(P("dp", None, "gx", "gy", None), P(("gx", "gy", "dp")), P(("gx", "gy", "dp"))),
        check_vma=False,
    )
```

```python
import functools

import jax
import jax.numpy as jnp
import ml_dtypes
import numpy as np
from jax import lax
from jax.experimental import pallas as pl
from jax.experimental.pallas import tpu as pltpu
from jax.sharding import PartitionSpec as P

MESH = pl.DeviceIdType.MESH
F32 = jnp.float32
BF16 = jnp.bfloat16
DIRS = [(0, 1), (0, -1), (1, 0), (-1, 0), (1, 1), (1, -1), (-1, 1), (-1, -1)]
CELLS = 4194304
NCONST = 10


def constants():
    depth_map = np.zeros((256, 768), np.float32)
    for n in range(2):
        for z in range(128):
            lane = (z % 2) * 128 + (z // 2 % 2) * 64 + n * 32 + z // 4
            for t in range(3):
                src = z + t - 1
                if 0 <= src < 128:
                    depth_map[n * 128 + src, t * 256 + lane] = 1
    restore = depth_map[:, 256:512].T.copy()
    pool_map = np.zeros((128, 256), np.float32)
    for n in range(2):
        for z in range(64):
            lane = (z % 2) * 64 + n * 32 + z // 2
            for half, src in ((0, z - 1), (1, z + 1)):
                if 0 <= src < 64:
                    pool_map[(src % 2) * 64 + n * 32 + src // 2, half * 128 + lane] = 1
    cot_map = np.zeros((128, 256), np.float32)
    for h in range(2):
        for b in range(2):
            for n in range(2):
                for k in range(32):
                    cot_map[n * 64 + h * 32 + k, h * 128 + b * 64 + n * 32 + k] = 1
    place = np.full((80,), -100.0, np.float32)
    chan = np.full((80,), -1)
    for c in range(4):
        for y in range(-1, 17):
            row = 64 + c if y < 0 else 68 + c if y > 15 else c * 16 + y
            place[row] = y
            chan[row] = c
    toeplitz = np.zeros((128, 3 * 768), np.float32)
    gather = np.zeros((720, 128), np.float32)
    for dx in range(3):
        for dz in range(3):
            group = dx * 240 + dz * 80
            for c in range(4):
                for dy in range(3):
                    toeplitz[((dx * 3 + dy) * 3 + dz) * 4 + c, (group + c * 16 + dy - 1) % 768] = 1
                toeplitz[((dx * 3 + 0) * 3 + dz) * 4 + c, 768 + group + 64 + c] = 1
                toeplitz[((dx * 3 + 2) * 3 + dz) * 4 + c, 1536 + group + 68 + c] = 1
            for row in range(72):
                gather[group + row, chan[row] * 32 + dx * 9 + dz] = 1
    reorder = np.zeros((432, 432), np.float32)
    for tap in range(27):
        for c in range(16):
            reorder[tap * 16 + c, c * 27 + tap] = 1
    select = np.zeros((16, 64), np.float32)
    for c in range(4):
        select[c, c * 16 + 15] = 1
        select[4 + c, c * 16] = 1
    b16 = lambda v: v.astype(ml_dtypes.bfloat16)
    return (
        b16(depth_map), b16(restore), b16(pool_map), b16(cot_map), b16(toeplitz), b16(gather), b16(select),
        b16(np.eye(128, dtype=np.float32)), b16(reorder), np.pad(np.tile(place, 9), (0, 48), constant_values=-100)[None, :],
    )


def dot(a, b):
    return jnp.dot(a, b, preferred_element_type=F32)


def dot_nt(a, b):
    return lax.dot_general(a, b, (((1,), (1,)), ((), ())), preferred_element_type=F32)


def split_dot(a, b):
    high = a.astype(BF16)
    rest = a - high.astype(F32)
    mid = rest.astype(BF16)
    low = (rest - mid.astype(F32)).astype(BF16)
    parts = dot(jnp.concatenate([high.astype(F32), mid.astype(F32), low.astype(F32)], axis=0).astype(BF16), b)
    rows = a.shape[0]
    return parts[:rows] + parts[rows:2 * rows] + parts[2 * rows:]


def before2(u):
    lane = lax.broadcasted_iota(jnp.int32, u.shape, 1)
    return jnp.where(
        lane < 64, jnp.where(lane % 32 != 0, pltpu.roll(u, 65, 1), 0.0), pltpu.roll(u, 64, 1)
    )


def after2(u):
    lane = lax.broadcasted_iota(jnp.int32, u.shape, 1)
    return jnp.where(
        lane >= 64, jnp.where(lane % 32 != 31, pltpu.roll(u, 63, 1), 0.0), pltpu.roll(u, 64, 1)
    )


def before(v):
    return jnp.concatenate([before2(v[:, 128:]), v[:, :128]], axis=1)


def after(v):
    return jnp.concatenate([v[:, 128:], after2(v[:, :128])], axis=1)


def kernel(
    gxn, gyn,
    inp, cot, w1t, w2t, b1r, b2r, *rest):
    fixed, rest = rest[:NCONST], rest[NCONST:]
    out, gw1, gw2 = rest[:3]
    kept, rest = rest[3:3 + NCONST], rest[3 + NCONST:]
    (xs, hb, hlr, hx, hc, w1, w1tr, w2, w2b, bias1, bias2, sl, gf, pool, cots, gs, gp,
    acc2, r2dp, s2a, r2gx, s2b, r2gy, gi, sby, ry, sx_, rx, sc, rc, acc1, s1, r1gx, s1b, r1gy,
    w1f, w2e, pre2, xe, ye, rxe, rye, rce, ssem, rsem, lsem) = rest
    depth_map, restore, pool_map, cot_map, toeplitz, gather, select, eye, reorder, place = kept
    loads = [pltpu.make_async_copy(fixed[i], kept[i], lsem.at[i]) for i in range(NCONST)]
    for load in loads:
        load.start()
    gx, gy, dp = lax.axis_index("gx"), lax.axis_index("gy"), lax.axis_index("dp")

    def at(sx, sy):
        return (lax.rem(gx + sx + gxn, gxn), lax.rem(gy + sy + gyn, gyn), dp)

    def remote(src, dst, k, device):
        return pltpu.make_async_remote_copy(
            src_ref=src, dst_ref=dst, send_sem=ssem.at[k], recv_sem=rsem.at[k], device_id=device, device_id_type=MESH
        )

    left, right = gy > 0, gy < gyn - 1
    up, down = gx > 0, gx < gxn - 1

    def start(copies, which):
        for sx in which:
            picked = [c for c, d in zip(copies, DIRS) if d[0] == sx]
            if sx == 0:
                for copy in picked:
                    copy.start()
            else:
                @pl.when(down if sx == 1 else up)
                def _(picked=picked):
                    for copy in picked:
                        copy.start()

    def finish_all(copies):
        by = {sx: [c for c, d in zip(copies, DIRS) if d[0] == sx] for sx in (0, 1, -1)}
        for sx in (1, -1):
            @pl.when(down if sx == 1 else up)
            def _(sx=sx):
                for copy in by[sx]:
                    copy.wait_send()
                for copy in by[-sx]:
                    copy.wait_recv()
        for copy in by[0]:
            copy.wait()

    barrier = pltpu.get_barrier_semaphore()
    peers = [at(*d) for d in DIRS]
    peers += [at(d, 0) for d in range(2, gxn - 1)] + [at(0, d) for d in range(2, gyn - 1)]
    peers += [(lax.rem(gx + d, gxn), gy, 1 - dp) for d in range(gxn)]
    for peer in peers:
        pl.semaphore_signal(barrier, inc=1, device_id=peer, device_id_type=MESH)

    def raw(x):
        halves = [inp[n, :, x].reshape(64, 128) for n in range(2)]
        return jnp.concatenate(halves, axis=1)

    loads[6].wait()
    for x in range(8):
        hb[x] = dot(select[...], raw(x)).astype(BF16)
    pl.semaphore_wait(barrier, len(peers))
    first = []
    for k, (sx, sy) in enumerate(DIRS):
        a, b = (0 if sx == 1 else 1), (0 if sy == 1 else 1)
        if sx == 0:
            src, dst = hb, hlr.at[b]
        elif sy == 0:
            src, dst = inp.at[:, :, 7 if sx == 1 else 0], hx.at[a]
        else:
            src, dst = hb.at[7 if sx == 1 else 0], hc.at[a, b]
        first.append(remote(src, dst, k, at(sx, sy)))
    start(first, (1, -1, 0))

    for i, load in enumerate(loads):
        if i != 6:
            load.wait()
    w1f[...] = jnp.zeros_like(w1f)
    for tap in range(27):
        w1f[tap * 4:tap * 4 + 4] = w1t[tap].astype(F32)
    small = dot_nt(eye[:32, :32], w1f[...].astype(BF16)).astype(BF16)
    base = dot(small, toeplitz[...])
    for r in range(16):
        y = 2 * (r % 8) + r // 8
        block = base[:, :768] if y == 0 else pltpu.roll(base[:, :768], y, 1)
        block = jnp.where(jnp.abs(place[...] - float(y)) < 1.5, block, 0.0)
        if y == 0:
            block = block + base[:, 768:1536]
        if y == 15:
            block = block + base[:, 1536:]
        w1[r * 32:r * 32 + 32, :] = block[:, :720].astype(BF16)
    for b in range(6):
        width = min(128, 720 - b * 128)
        w1tr[b * 128:b * 128 + width] = dot_nt(eye[:width, :width], w1[:, b * 128:b * 128 + width]).astype(BF16)
    w2[...] = dot_nt(eye[:64, :64], w2t[...]).astype(BF16)
    for dx in range(3):
        for dy in range(3):
            at_lane = ((2 - dx) * 3 + 2 - dy) * 64
            row = (dx * 3 + dy) * 96
            w2b[:, at_lane:at_lane + 64] = w2t[row:row + 96, :]
    bias1[...] = jnp.zeros_like(bias1)
    bias1[:, 0:32] = jnp.broadcast_to(b1r[...], (128, 32))
    bias2[...] = jnp.zeros_like(bias2)
    bias2[:, 0:64] = jnp.broadcast_to(b2r[...], (128, 64))
    b1 = jnp.transpose(bias1[...])[:32]
    b2 = jnp.transpose(bias2[...])[:64]
    b1 = jnp.concatenate([b1, b1], axis=1)
    b2 = jnp.concatenate([b2, b2], axis=1)
    for q in range(4):
        part = jnp.concatenate(
            [cot[(n * 8 + h * 4 + q) * 32:(n * 8 + h * 4 + q) * 32 + 32, :] for n in range(2) for h in range(2)], axis=0
        )
        turned = dot_nt(eye[:64, :64], part).astype(BF16)
        cots[q * 64:q * 64 + 64] = dot(turned, cot_map[...]) * 0.125

    def slab(index, rows):
        spread = dot(rows, depth_map[...]).astype(BF16)
        for t in range(3):
            xs[index, t * 80:t * 80 + 64] = spread[:, t * 256:t * 256 + 256]

    for x in range(8):
        slab(x + 1, raw(x))
    acc2[...] = jnp.zeros_like(acc2)
    for i in (0, 5):
        gs[i] = jnp.zeros((768, 128), BF16)
    for i in range(1, 5):
        gs[i, 0:128] = jnp.zeros((128, 128), BF16)
        gs[i, 640:768] = jnp.zeros((128, 128), BF16)
    for i, picked in enumerate((
        [(0, dy) for dy in range(3)], [(2, dy) for dy in range(3)], [(dx, 0) for dx in range(3)], [(dx, 2) for dx in range(3)]
    )):
        rows = [w2t[(dx * 3 + dy) * 96:(dx * 3 + dy) * 96 + 96, :] for dx, dy in picked]
        w2e[i] = dot_nt(eye[:64, :64], jnp.concatenate(rows, axis=0)).astype(BF16)
    finish_all(first)
    row16 = lax.broadcasted_iota(jnp.int32, (16, 256), 0)
    from_left = jnp.logical_and(row16 < 4, left)
    from_right = jnp.logical_and(jnp.logical_and(row16 >= 4, row16 < 8), right)

    def halo(index, left_rows, right_rows, ok):
        rows = jnp.where(from_left, left_rows.astype(F32), jnp.where(from_right, right_rows.astype(F32), 0.0))
        if ok is not None:
            rows = jnp.where(ok, rows, 0.0)
        spread = dot(rows.astype(BF16), depth_map[...]).astype(BF16)
        for t in range(3):
            xs[index, t * 80 + 64:t * 80 + 80] = spread[:, t * 256:t * 256 + 256]

    for x in range(8):
        halo(x + 1, hlr[0, x], hlr[1, x], None)
    for a, ok in ((0, up), (1, down)):
        index = 0 if a == 0 else 9
        rows = jnp.concatenate([hx[a, n].reshape(64, 128) for n in range(2)], axis=1)
        slab(index, jnp.where(ok, rows.astype(F32), 0.0).astype(BF16))
        halo(index, hc[a, 0], hc[a, 1], ok)

    b1all = jnp.concatenate([b1] * 16, axis=0)

    def layer1(j):
        total = None
        for px in range(2):
            x = 2 * j + px
            pre = dot(w1[...], xs[x:x + 3].reshape(720, 256)) + b1all
            t = jnp.tanh(0.5 * pre)
            value = pre * (0.65 + 0.35 * t)
            sl[x] = 0.65 + 0.35 * t + 0.175 * pre * (1.0 - t * t)
            value = value[:256] + value[256:]
            value = value[:, :128] + value[:, 128:]
            total = value if total is None else total + value
        pool[j + 1, 1, 32:288] = (total * 0.125).astype(BF16)

    second = []
    for k, (sx, sy) in enumerate(DIRS):
        src_x, dst_x = {0: (pl.ds(1, 4),) * 2, 1: (4, 0), -1: (1, 5)}[sx]
        src_y, dst_y = {0: (pl.ds(32, 256),) * 2, 1: (pl.ds(256, 32), pl.ds(0, 32)), -1: (pl.ds(32, 32), pl.ds(288, 32))}[sy]
        second.append(remote(pool.at[src_x, 1, src_y], pool.at[dst_x, 1, dst_y], 8 + k, at(sx, sy)))
    layer1(0)
    layer1(3)
    start(second, (1, -1))
    layer1(1)
    layer1(2)
    start(second, (0,))

    for i in range(1, 5):
        spread = dot(pool[i, 1, 32:288], pool_map[...]).astype(BF16)
        pool[i, 0, 32:288] = spread[:, :128]
        pool[i, 2, 32:288] = spread[:, 128:]
    none = jnp.zeros((32, 128), BF16)

    def piece(i, dz, r):
        return none if i in (0, 5) or r in (0, 9) else pool[i, dz, r * 32:r * 32 + 32]

    def pair(i, dz, r):
        return jnp.concatenate([piece(i, dz, r), piece(i + 2, dz, r)], axis=1)

    for j in range(2):
        for y in range(8):
            patch = jnp.concatenate(
                [pair(j + dx, dz, y + dy) for dx in range(3) for dy in range(3) for dz in range(3)], axis=0)
            pre2[j, y] = dot(w2[...], patch) + b2

    finish_all(second)
    for ok, index in ((up, 0), (down, 5)):
        @pl.when(jnp.logical_not(ok))
        def _(index=index):
            pool[index, 1] = jnp.zeros((320, 128), BF16)
    for ok, index in ((left, 0), (right, 288)):
        @pl.when(jnp.logical_not(ok))
        def _(index=index):
            pool[:, 1, index:index + 32] = jnp.zeros((6, 32, 128), BF16)

    for i in (0, 5):
        spread = dot(pool[i, 1], pool_map[...]).astype(BF16)
        pool[i, 0] = spread[:, :128]
        pool[i, 2] = spread[:, 128:]
    rims = [(i, r) for i in range(1, 5) for r in (0, 288)]
    spread = dot(jnp.concatenate([pool[i, 1, r:r + 32] for i, r in rims], axis=0), pool_map[...]).astype(BF16)
    for q, (i, r) in enumerate(rims):
        pool[i, 0, r:r + 32] = spread[q * 32:q * 32 + 32, :128]
        pool[i, 2, r:r + 32] = spread[q * 32:q * 32 + 32, 128:]
    for side, i in ((0, 0), (1, 5)):
        for y in range(4):
            patch = jnp.concatenate(
                [jnp.concatenate([pool[i, dz, (q + dy) * 32:(q + dy) * 32 + 32] for q in (y, y + 4)], axis=1)
                 for dy in range(3) for dz in range(3)], axis=0)
            term = dot(w2e[side], patch)
            lanes = slice(side * 128, side * 128 + 128)
            pre2[side, y, :, lanes] += term[:, :128]
            pre2[side, y + 4, :, lanes] += term[:, 128:]
    for side, y, r in ((2, 0, 0), (3, 7, 288)):
        for j in range(2):
            patch = jnp.concatenate(
                [jnp.concatenate([none if i in (0, 5) else pool[i, dz, r:r + 32] for i in (j + dx, j + dx + 2)], axis=1)
                 for dx in range(3) for dz in range(3)], axis=0)
            pre2[j, y] += dot(w2e[side], patch)
    for j in range(2):
        for y in range(8):
            pre = pre2[j, y]
            t = jnp.tanh(0.5 * pre)
            slope = 0.65 + 0.35 * t + 0.175 * pre * (1.0 - t * t)
            grad = (slope * cots[(y // 2) * 64:(y // 2) * 64 + 64, :]).astype(BF16)
            gs[j + 1, (y + 2) * 64:(y + 3) * 64] = grad[:, :128]
            gs[j + 3, (y + 2) * 64:(y + 3) * 64] = grad[:, 128:]

    def depth_terms(part):
        return part[32:64] + before2(part[64:96]) + after2(part[0:32])

    for side, i, u in ((0, 1, 2), (1, 4, 0)):
        for y in range(5):
            patch = jnp.concatenate([gs[i, q * 64:q * 64 + 192] for q in (y, y + 5)], axis=1)
            terms = dot(w2b[:, u * 192:u * 192 + 192], patch) * 0.125
            xe[side, y * 32:y * 32 + 32] = depth_terms(terms[:, :128]).astype(BF16)
            xe[side, (y + 5) * 32:(y + 6) * 32] = depth_terms(terms[:, 128:]).astype(BF16)

    def back2(j, y):
        patch = jnp.concatenate(
            [jnp.concatenate([gs[i, (y + 1) * 64:(y + 4) * 64] for i in (j + u, j + u + 2)], axis=1) for u in range(3)],
            axis=0)
        terms = dot(w2b[...], patch) * 0.125
        return depth_terms(terms[:, :128]), depth_terms(terms[:, 128:])

    for side, y in ((0, -1), (1, 8)):
        for j in range(2):
            one, two = back2(j, y)
            ye[side, j] = one.astype(BF16)
            ye[side, j + 2] = two.astype(BF16)
    third = []
    for k, (sx, sy) in enumerate(DIRS):
        a, b = (0 if sx == 1 else 1), (0 if sy == 1 else 1)
        if sx == 0:
            src, dst = ye.at[1 - b], rye.at[b]
        elif sy == 0:
            src, dst = xe.at[1 - a, pl.ds(32, 256)], rxe.at[a]
        else:
            src, dst = xe.at[1 - a, pl.ds(288 if sy == 1 else 0, 32)], rce.at[a, b]
        third.append(remote(src, dst, 16 + k, at(sx, sy)))
    start(third, (1, -1, 0))

    def cell(ref, i, where, start, size):
        rows = slice(start, start + size)
        return jnp.concatenate([ref[(i,) + where + (rows,)], ref[(i + 2,) + where + (rows,)]], axis=1)

    for j in range(2):
        for y in range(8):
            grad = cell(gs, j + 1, (), (y + 2) * 64, 64)
            for half in range(2):
                patch = jnp.concatenate(
                    [cell(pool, j + dx, (dz,), (y + dy) * 32 + half * 16, 16)
                     for dx in range(3) for dy in range(3) for dz in range(3)], axis=0)
                acc2[half, :, 0:432] += dot_nt(grad, patch)
    pair2 = remote(acc2.at[1 - dp], r2dp, 24, (gx, gy, 1 - dp))
    pair2.start()
    for j in range(2):
        for y in range(8):
            one, two = back2(j, y)
            gp[j, y * 32:y * 32 + 32] = one
            gp[j + 2, y * 32:y * 32 + 32] = two
    finish_all(third)

    for a, ok, i in ((0, up, 0), (1, down, 3)):
        gp[i] += jnp.where(ok, rxe[a].astype(F32), 0.0)
        for b, ok2, r in ((0, left, 0), (1, right, 224)):
            gp[i, r:r + 32] += jnp.where(jnp.logical_and(ok, ok2), rce[a, b].astype(F32), 0.0)
    for b, ok, r in ((0, left, 0), (1, right, 224)):
        for i in range(4):
            gp[i, r:r + 32] += jnp.where(ok, rye[b, i].astype(F32), 0.0)

    for x in range(8):
        spread = gp[x // 2]
        spread = jnp.concatenate([spread, spread], axis=1)
        spread = jnp.concatenate([spread, spread], axis=0)
        gf[x] = (sl[x] * spread).astype(BF16)
    for x in range(8):
        term = dot_nt(gf[x], xs[x:x + 3].reshape(720, 256))
        acc1[...] = term if x == 0 else acc1[...] + term

    pair2.wait()
    s2a[...] = (acc2[dp] + r2dp[...]).reshape(gxn, 8, 512)
    along2 = []
    for d in range(1, gxn):
        along2.append(remote(s2a.at[lax.rem(gx + d, gxn)], r2gx.at[d - 1], 24 + d, at(d, 0)))
        along2[-1].start()

    taps = None
    for dy in range(3):
        kept = None
        for r in range(16):
            y = 2 * (r % 8) + r // 8
            term = jnp.where(place[:, :720] == float(y + dy - 1), acc1[r * 32:r * 32 + 32], 0.0)
            kept = term if kept is None else kept + term
        parts = split_dot(kept, gather[...])
        if dy:
            parts = pltpu.roll(parts, 3 * dy, 1)
        taps = parts if taps is None else taps + parts
    for g in range(8):
        s1[g] = taps[4 * g:4 * g + 4]
    along1 = []
    for d in range(gxn):
        for e in range(2):
            if d + e:
                peer = (lax.rem(gx + d, gxn), gy, lax.rem(dp + e, 2))
                along1.append(remote(s1.at[peer[0]], r1gx.at[2 * d + e - 1], 47 + 2 * d + e, peer))
                along1[-1].start()

    for x in range(8):
        term = dot(w1tr[...], gf[x]).reshape(3, 240, 256)
        if x == 0:
            gi[0:3] = term
        else:
            gi[x:x + 2] += term[:2]
            gi[x + 2] = term[2]

    def combine(x):
        return gi[x, 80:152] + before(gi[x, 160:232]) + after(gi[x, 0:72])

    for i, x in ((0, 0), (1, 9)):
        edge = combine(x)
        sx_[i] = edge[:64]
        sc[i] = edge[64:]
    for x in range(8):
        inner = combine(x + 1)
        gi[x + 1, 80:144] = inner[:64]
        sby[x] = inner[64:]
    fourth = []
    for k, (sx, sy) in enumerate(DIRS):
        a, b = (0 if sx == 1 else 1), (0 if sy == 1 else 1)
        if sx == 0:
            src, dst = sby, ry.at[b]
        elif sy == 0:
            src, dst = sx_.at[1 if sx == 1 else 0], rx.at[a]
        else:
            src, dst = sc.at[1 if sx == 1 else 0], rc.at[a, b]
        fourth.append(remote(src, dst, 40 + k, at(sx, sy)))
    start(fourth, (1, -1, 0))
    for copy in along1:
        copy.wait()
    total1 = s1[gx]
    for i in range(2 * gxn - 1):
        total1 = total1 + r1gx[i]
    s1b[...] = total1
    across1 = []
    for d in range(1, gyn):
        across1.append(remote(s1b, r1gy.at[d - 1], 62 + d, at(0, d)))
        across1[-1].start()
    for copy in along2:
        copy.wait()
    total2 = s2a[gx]
    for d in range(1, gxn):
        total2 = total2 + r2gx[d - 1]
    for g in range(8):
        s2b[g] = total2[g:g + 1]
    across2 = []
    for d in range(1, gyn):
        across2.append(remote(s2b.at[lax.rem(gy + d, gyn)], r2gy.at[d - 1], 31 + d, at(0, d)))
        across2[-1].start()
    finish_all(fourth)
    y16 = lax.broadcasted_iota(jnp.int32, (4, 16, 256), 1)

    def ends(low_rows, high_rows):
        low_part = jnp.where(jnp.logical_and(y16 == 0, left), low_rows[4:8][:, None, :], 0.0)
        high_part = jnp.where(jnp.logical_and(y16 == 15, right), high_rows[0:4][:, None, :], 0.0)
        return (low_part + high_part).reshape(64, 256)

    for a, ok, x in ((0, up, 1), (1, down, 8)):
        term = rx[a] + ends(rc[a, 0], rc[a, 1])
        gi[x, 80:144] += jnp.where(ok, term, 0.0)

    def finish(x, _):
        total = (gi[x + 1, 80:144] + ends(ry[0, x], ry[1, x])).astype(BF16)
        natural = dot(total, restore[...]).astype(BF16)
        for n in range(2):
            out[n, :, x] = natural[:, n * 128:n * 128 + 128].reshape(4, 16, 128)
        return 0

    lax.fori_loop(0, 8, finish, 0, unroll=True)

    for copy in across2:
        copy.wait()
    total2 = s2b[gy]
    for d in range(1, gyn):
        total2 = total2 + r2gy[d - 1]
    total2 = jnp.concatenate([total2 * (1.0 / (CELLS / 8) ** 0.5)] * 8, axis=0)[:, :432]
    gw2[...] = split_dot(total2, reorder[...])[0:1]
    for copy in across1:
        copy.wait()
    total1 = s1b[...]
    for d in range(1, gyn):
        total1 = total1 + r1gy[d - 1]
    mine = None
    for q in range(4):
        for c in range(4):
            ok = jnp.logical_and(gy // 2 == q, (gy % 2) * 2 + dp == c)
            term = jnp.where(ok, total1[q:q + 1, c * 32:c * 32 + 32], 0.0)
            mine = term if mine is None else mine + term
    gw1[...] = mine[:, 0:27] * (1.0 / CELLS ** 0.5)


def on_device(gxn, gyn, consts, inputs, cotangent, w_first, w_second, b_first, b_second):
    cot = jnp.transpose(cotangent, (0, 2, 3, 4, 1)).reshape(512, 64)
    w1t = jnp.transpose(w_first, (2, 3, 4, 1, 0)).reshape(27, 4, 32)
    w2t = jnp.transpose(w_second, (2, 3, 4, 1, 0)).reshape(864, 64)
    vmem = pl.BlockSpec(memory_space=pltpu.VMEM)
    operands = (inputs, cot, w1t, w2t, b_first.reshape(1, 32), b_second.reshape(1, 64), *consts)
    scratch = [
        ((10, 240, 256), BF16), ((8, 16, 256), BF16), ((2, 8, 16, 256), BF16), ((2, 2, 4, 16, 128), BF16),
        ((2, 2, 16, 256), BF16), ((512, 720), BF16), ((720, 512), BF16), ((64, 864), BF16), ((96, 576), BF16),
        ((128, 128), F32), ((128, 128), F32), ((8, 512, 256), F32), ((8, 512, 256), BF16), ((6, 3, 320, 128), BF16),
        ((256, 256), F32), ((6, 768, 128), BF16), ((4, 256, 128), F32),
        ((2, 64, 512), F32), ((64, 512), F32), ((gxn, 8, 512), F32), ((gxn - 1, 8, 512), F32), ((gyn, 1, 512), F32),
        ((gyn - 1, 1, 512), F32), ((10, 240, 256), F32), ((8, 8, 256), F32), ((2, 8, 8, 256), F32),
        ((2, 64, 256), F32), ((2, 64, 256), F32), ((2, 8, 256), F32), ((2, 2, 8, 256), F32), ((512, 720), F32),
        ((gxn, 4, 128), F32), ((2 * gxn - 1, 4, 128), F32), ((4, 128), F32),
        ((gyn - 1, 4, 128), F32), ((128, 32), F32), ((4, 64, 288), BF16), ((2, 8, 64, 256), F32),
        ((2, 320, 128), BF16), ((2, 4, 32, 128), BF16), ((2, 256, 128), BF16), ((2, 4, 32, 128), BF16),
        ((2, 2, 32, 128), BF16),
    ]
    result, part1, part2 = pl.pallas_call(
        functools.partial(kernel, gxn, gyn),
        out_shape=(
            jax.ShapeDtypeStruct(inputs.shape, BF16),
            jax.ShapeDtypeStruct((1, 27), F32),
            jax.ShapeDtypeStruct((1, 432), F32),
        ),
        in_specs=[vmem] * 6 + [pl.BlockSpec(memory_space=pl.ANY)] * NCONST,
        out_specs=(vmem, vmem, vmem),
        scratch_shapes=[pltpu.VMEM(c.shape, c.dtype) for c in consts]
        + [pltpu.VMEM(s, d) for s, d in scratch]
        + [pltpu.SemaphoreType.DMA((70,)), pltpu.SemaphoreType.DMA((70,)), pltpu.SemaphoreType.DMA((NCONST,))],
        compiler_params=pltpu.CompilerParams(
            collective_id=0, has_side_effects=True, vmem_limit_bytes=60 * 1024 * 1024
        ),
    )(*operands)
    return result, part1.reshape(27), part2.reshape(432)


def solution(mesh):
    consts = constants()
    return jax.shard_map(
        functools.partial(on_device, mesh.shape["gx"], mesh.shape["gy"], consts),
        mesh=mesh,
        in_specs=(P("dp", None, "gx", "gy", None), P("dp", None, "gx", "gy", None), P(), P(), P(), P()),
        out_specs=(P("dp", None, "gx", "gy", None), P(("gx", "gy", "dp")), P(("gx", "gy", "dp"))),
        check_vma=False,
    )
```

```python
import functools

import jax
import jax.numpy as jnp
import ml_dtypes
import numpy as np
from jax import lax
from jax.experimental import pallas as pl
from jax.experimental.pallas import tpu as pltpu
from jax.sharding import PartitionSpec as P

MESH = pl.DeviceIdType.MESH
F32 = jnp.float32
BF16 = jnp.bfloat16
DIRS = [(0, 1), (0, -1), (1, 0), (-1, 0), (1, 1), (1, -1), (-1, 1), (-1, -1)]
CELLS = 4194304
NLOAD = 15


def constants():
    depth_map = np.zeros((256, 768), np.float32)
    for n in range(2):
        for z in range(128):
            lane = (z % 2) * 128 + (z // 2 % 2) * 64 + n * 32 + z // 4
            for t in range(3):
                src = z + t - 1
                if 0 <= src < 128:
                    depth_map[n * 128 + src, t * 256 + lane] = 1
    restore = depth_map[:, 256:512].T.copy()
    pool_map = np.zeros((128, 256), np.float32)
    for n in range(2):
        for z in range(64):
            lane = (z % 2) * 64 + n * 32 + z // 2
            for half, src in ((0, z - 1), (1, z + 1)):
                if 0 <= src < 64:
                    pool_map[(src % 2) * 64 + n * 32 + src // 2, half * 128 + lane] = 1
    cot_map = np.zeros((128, 256), np.float32)
    for h in range(2):
        for b in range(2):
            for n in range(2):
                for k in range(32):
                    cot_map[n * 64 + h * 32 + k, h * 128 + b * 64 + n * 32 + k] = 1
    place = np.full((80,), -100.0, np.float32)
    chan = np.full((80,), -1)
    for c in range(4):
        for y in range(-1, 17):
            row = 64 + c if y < 0 else 68 + c if y > 15 else c * 16 + y
            place[row] = y
            chan[row] = c
    toeplitz = np.zeros((128, 3 * 768), np.float32)
    gather = np.zeros((720, 128), np.float32)
    for dx in range(3):
        for dz in range(3):
            group = dx * 240 + dz * 80
            for c in range(4):
                for dy in range(3):
                    toeplitz[((dx * 3 + dy) * 3 + dz) * 4 + c, (group + c * 16 + dy - 1) % 768] = 1
                toeplitz[((dx * 3 + 0) * 3 + dz) * 4 + c, 768 + group + 64 + c] = 1
                toeplitz[((dx * 3 + 2) * 3 + dz) * 4 + c, 1536 + group + 68 + c] = 1
            for row in range(72):
                gather[group + row, chan[row] * 32 + dx * 9 + dz] = 1
    reorder = np.zeros((432, 432), np.float32)
    for tap in range(27):
        for c in range(16):
            reorder[tap * 16 + c, c * 27 + tap] = 1
    select = np.zeros((16, 64), np.float32)
    for c in range(4):
        select[c, c * 16 + 15] = 1
        select[4 + c, c * 16] = 1
    b16 = lambda v: v.astype(ml_dtypes.bfloat16)
    place = np.pad(np.tile(place, 9), (0, 48), constant_values=-100)[None, :]
    return {
        "depth_map": b16(depth_map), "restore": b16(restore), "pool_map": b16(pool_map), "cot_map": b16(cot_map),
        "toeplitz": b16(toeplitz), "gather": b16(gather), "select": b16(select), "reorder": b16(reorder),
        "eye": b16(np.eye(128, dtype=np.float32)), "place": place,
    }


def dot(a, b):
    return jnp.dot(a, b, preferred_element_type=F32)


def dot_nt(a, b):
    return lax.dot_general(a, b, (((1,), (1,)), ((), ())), preferred_element_type=F32)


def split_dot(a, b):
    high = a.astype(BF16)
    rest = a - high.astype(F32)
    mid = rest.astype(BF16)
    low = (rest - mid.astype(F32)).astype(BF16)
    parts = dot(jnp.concatenate([high.astype(F32), mid.astype(F32), low.astype(F32)], axis=0).astype(BF16), b)
    rows = a.shape[0]
    return parts[:rows] + parts[rows:2 * rows] + parts[2 * rows:]


def before2(u):
    lane = lax.broadcasted_iota(jnp.int32, u.shape, 1)
    return jnp.where(
        lane < 64, jnp.where(lane % 32 != 0, pltpu.roll(u, 65, 1), 0.0), pltpu.roll(u, 64, 1)
    )


def after2(u):
    lane = lax.broadcasted_iota(jnp.int32, u.shape, 1)
    return jnp.where(
        lane >= 64, jnp.where(lane % 32 != 31, pltpu.roll(u, 63, 1), 0.0), pltpu.roll(u, 64, 1)
    )


def before(v):
    return jnp.concatenate([before2(v[:, 128:]), v[:, :128]], axis=1)


def after(v):
    return jnp.concatenate([v[:, 128:], after2(v[:, :128])], axis=1)


def kernel(
    gxn, gyn,
    *rest):
    fixed, rest = rest[:NLOAD], rest[NLOAD:]
    out, gw1, gw2 = rest[:3]
    kept, rest = rest[3:3 + NLOAD], rest[3 + NLOAD:]
    (xs, hb, hlr, hx, hc, w1, w1tr, w2, w2b, bias1, bias2, sl, gf, pool, cots, gs, gp,
    acc2, r2dp, s2a, r2gx, s2b, r2gy, gi, sby, ry, sx_, rx, sc, rc, acc1, s1, r1gx, s1b, r1gy,
    w1f, w2e, pre2, xe, ye, rxe, rye, rce, ssem, rsem, lsem) = rest
    inp, select, w1t, eye, toeplitz, place, depth_map, b1r, w2t, cot, b2r, pool_map, cot_map, gather, reorder = kept
    loads = [pltpu.make_async_copy(fixed[i], kept[i], lsem.at[i]) for i in range(NLOAD)]
    for load in loads:
        load.start()
    gx, gy, dp = lax.axis_index("gx"), lax.axis_index("gy"), lax.axis_index("dp")

    def at(sx, sy):
        return (lax.rem(gx + sx + gxn, gxn), lax.rem(gy + sy + gyn, gyn), dp)

    def remote(src, dst, k, device):
        return pltpu.make_async_remote_copy(
            src_ref=src, dst_ref=dst, send_sem=ssem.at[k], recv_sem=rsem.at[k], device_id=device, device_id_type=MESH
        )

    left, right = gy > 0, gy < gyn - 1
    up, down = gx > 0, gx < gxn - 1

    def start(copies, which):
        for sx in which:
            picked = [c for c, d in zip(copies, DIRS) if d[0] == sx]
            if sx == 0:
                for copy in picked:
                    copy.start()
            else:
                @pl.when(down if sx == 1 else up)
                def _(picked=picked):
                    for copy in picked:
                        copy.start()

    def finish_all(copies):
        by = {sx: [c for c, d in zip(copies, DIRS) if d[0] == sx] for sx in (0, 1, -1)}
        for sx in (1, -1):
            @pl.when(down if sx == 1 else up)
            def _(sx=sx):
                for copy in by[sx]:
                    copy.wait_send()
                for copy in by[-sx]:
                    copy.wait_recv()
        for copy in by[0]:
            copy.wait()

    barrier = pltpu.get_barrier_semaphore()
    peers = [at(*d) for d in DIRS]
    peers += [at(d, 0) for d in range(2, gxn - 1)] + [at(0, d) for d in range(2, gyn - 1)]
    peers += [(lax.rem(gx + d, gxn), gy, 1 - dp) for d in range(gxn)]
    for peer in peers:
        pl.semaphore_signal(barrier, inc=1, device_id=peer, device_id_type=MESH)

    def raw(x):
        halves = [inp[n, :, x].reshape(64, 128) for n in range(2)]
        return jnp.concatenate(halves, axis=1)

    loads[0].wait()
    loads[1].wait()
    for x in range(8):
        hb[x] = dot(select[...], raw(x)).astype(BF16)
    pl.semaphore_wait(barrier, len(peers))
    first = []
    for k, (sx, sy) in enumerate(DIRS):
        a, b = (0 if sx == 1 else 1), (0 if sy == 1 else 1)
        if sx == 0:
            src, dst = hb, hlr.at[b]
        elif sy == 0:
            src, dst = inp.at[:, :, 7 if sx == 1 else 0], hx.at[a]
        else:
            src, dst = hb.at[7 if sx == 1 else 0], hc.at[a, b]
        first.append(remote(src, dst, k, at(sx, sy)))
    start(first, (1, -1, 0))

    for load in loads[2:8]:
        load.wait()
    w1f[...] = jnp.zeros_like(w1f)
    for tap in range(27):
        w1f[tap * 4:tap * 4 + 4] = w1t[tap].astype(F32)
    small = dot_nt(eye[:32, :32], w1f[...].astype(BF16)).astype(BF16)
    base = dot(small, toeplitz[...])
    for r in range(16):
        y = 2 * (r % 8) + r // 8
        block = base[:, :768] if y == 0 else pltpu.roll(base[:, :768], y, 1)
        block = jnp.where(jnp.abs(place[...] - float(y)) < 1.5, block, 0.0)
        if y == 0:
            block = block + base[:, 768:1536]
        if y == 15:
            block = block + base[:, 1536:]
        w1[r * 32:r * 32 + 32, :] = block[:, :720].astype(BF16)
    bias1[...] = jnp.zeros_like(bias1)
    bias1[:, 0:32] = jnp.broadcast_to(b1r[...], (128, 32))
    b1 = jnp.transpose(bias1[...])[:32]
    b1 = jnp.concatenate([b1, b1], axis=1)
    spread = dot(jnp.concatenate([raw(x) for x in range(8)], axis=0), depth_map[...]).astype(BF16)
    for x in range(8):
        for t in range(3):
            xs[x + 1, t * 80:t * 80 + 64] = spread[x * 64:x * 64 + 64, t * 256:t * 256 + 256]
    finish_all(first)
    row16 = lax.broadcasted_iota(jnp.int32, (16, 256), 0)
    from_left = jnp.logical_and(row16 < 4, left)
    from_right = jnp.logical_and(jnp.logical_and(row16 >= 4, row16 < 8), right)

    def halo(left_rows, right_rows):
        return jnp.where(from_left, left_rows.astype(F32), jnp.where(from_right, right_rows.astype(F32), 0.0))

    blocks = [halo(hlr[0, x], hlr[1, x]) for x in range(8)]
    for a, ok in ((0, up), (1, down)):
        rows = [hx[a, n].reshape(64, 128) for n in range(2)]
        blocks.append(jnp.where(ok, jnp.concatenate(rows, axis=1).astype(F32), 0.0))
        blocks.append(jnp.where(ok, halo(hc[a, 0], hc[a, 1]), 0.0))
    spread = dot(jnp.concatenate(blocks, axis=0).astype(BF16), depth_map[...]).astype(BF16)
    pieces = [(x + 1, 64, x * 16, 16) for x in range(8)]
    pieces += [(0, 0, 128, 64), (0, 64, 192, 16), (9, 0, 208, 64), (9, 64, 272, 16)]
    for index, row, at_row, size in pieces:
        for t in range(3):
            xs[index, t * 80 + row:t * 80 + row + size] = spread[at_row:at_row + size, t * 256:t * 256 + 256]

    b1all = jnp.concatenate([b1] * 16, axis=0)

    def layer1(j):
        total = None
        for px in range(2):
            x = 2 * j + px
            pre = dot(w1[...], xs[x:x + 3].reshape(720, 256)) + b1all
            t = jnp.tanh(0.5 * pre)
            value = pre * (0.65 + 0.35 * t)
            sl[x] = 0.65 + 0.35 * t + 0.175 * pre * (1.0 - t * t)
            value = value[:256] + value[256:]
            value = value[:, :128] + value[:, 128:]
            total = value if total is None else total + value
        pool[j + 1, 1, 32:288] = (total * 0.125).astype(BF16)

    second = []
    for k, (sx, sy) in enumerate(DIRS):
        src_x, dst_x = {0: (pl.ds(1, 4),) * 2, 1: (4, 0), -1: (1, 5)}[sx]
        src_y, dst_y = {0: (pl.ds(32, 256),) * 2, 1: (pl.ds(256, 32), pl.ds(0, 32)), -1: (pl.ds(32, 32), pl.ds(288, 32))}[sy]
        second.append(remote(pool.at[src_x, 1, src_y], pool.at[dst_x, 1, dst_y], 8 + k, at(sx, sy)))
    layer1(0)
    layer1(3)
    start(second, (1, -1))
    layer1(1)
    layer1(2)
    start(second, (0,))

    for load in loads[8:]:
        load.wait()
    w2[...] = dot_nt(eye[:64, :64], w2t[...]).astype(BF16)
    for dx in range(3):
        for dy in range(3):
            at_lane = ((2 - dx) * 3 + 2 - dy) * 64
            row = (dx * 3 + dy) * 96
            w2b[:, at_lane:at_lane + 64] = w2t[row:row + 96, :]
    bias2[...] = jnp.zeros_like(bias2)
    bias2[:, 0:64] = jnp.broadcast_to(b2r[...], (128, 64))
    b2 = jnp.transpose(bias2[...])[:64]
    b2 = jnp.concatenate([b2, b2], axis=1)
    for i in range(1, 5):
        spread = dot(pool[i, 1, 32:288], pool_map[...]).astype(BF16)
        pool[i, 0, 32:288] = spread[:, :128]
        pool[i, 2, 32:288] = spread[:, 128:]
    none = jnp.zeros((32, 128), BF16)

    def piece(i, dz, r):
        return none if i in (0, 5) or r in (0, 9) else pool[i, dz, r * 32:r * 32 + 32]

    def pair(i, dz, r):
        return jnp.concatenate([piece(i, dz, r), piece(i + 2, dz, r)], axis=1)

    for j in range(2):
        for y in range(8):
            patch = jnp.concatenate(
                [pair(j + dx, dz, y + dy) for dx in range(3) for dy in range(3) for dz in range(3)], axis=0)
            pre2[j, y] = dot(w2[...], patch) + b2

    for q in range(4):
        part = jnp.concatenate(
            [cot[(n * 8 + h * 4 + q) * 32:(n * 8 + h * 4 + q) * 32 + 32, :] for n in range(2) for h in range(2)], axis=0
        )
        turned = dot_nt(eye[:64, :64], part).astype(BF16)
        cots[q * 64:q * 64 + 64] = dot(turned, cot_map[...]) * 0.125

    acc2[...] = jnp.zeros_like(acc2)
    for i in (0, 5):
        gs[i] = jnp.zeros((768, 128), BF16)
    for i in range(1, 5):
        gs[i, 0:128] = jnp.zeros((128, 128), BF16)
        gs[i, 640:768] = jnp.zeros((128, 128), BF16)
    for i, picked in enumerate((
        [(0, dy) for dy in range(3)], [(2, dy) for dy in range(3)], [(dx, 0) for dx in range(3)], [(dx, 2) for dx in range(3)]
    )):
        rows = [w2t[(dx * 3 + dy) * 96:(dx * 3 + dy) * 96 + 96, :] for dx, dy in picked]
        w2e[i] = dot_nt(eye[:64, :64], jnp.concatenate(rows, axis=0)).astype(BF16)
    finish_all(second)
    for ok, index in ((up, 0), (down, 5)):
        @pl.when(jnp.logical_not(ok))
        def _(index=index):
            pool[index, 1] = jnp.zeros((320, 128), BF16)
    for ok, index in ((left, 0), (right, 288)):
        @pl.when(jnp.logical_not(ok))
        def _(index=index):
            pool[:, 1, index:index + 32] = jnp.zeros((6, 32, 128), BF16)

    for i in (0, 5):
        spread = dot(pool[i, 1], pool_map[...]).astype(BF16)
        pool[i, 0] = spread[:, :128]
        pool[i, 2] = spread[:, 128:]
    rims = [(i, r) for i in range(1, 5) for r in (0, 288)]
    spread = dot(jnp.concatenate([pool[i, 1, r:r + 32] for i, r in rims], axis=0), pool_map[...]).astype(BF16)
    for q, (i, r) in enumerate(rims):
        pool[i, 0, r:r + 32] = spread[q * 32:q * 32 + 32, :128]
        pool[i, 2, r:r + 32] = spread[q * 32:q * 32 + 32, 128:]
    for side, i in ((0, 0), (1, 5)):
        for y in range(4):
            patch = jnp.concatenate(
                [jnp.concatenate([pool[i, dz, (q + dy) * 32:(q + dy) * 32 + 32] for q in (y, y + 4)], axis=1)
                 for dy in range(3) for dz in range(3)], axis=0)
            term = dot(w2e[side], patch)
            lanes = slice(side * 128, side * 128 + 128)
            pre2[side, y, :, lanes] += term[:, :128]
            pre2[side, y + 4, :, lanes] += term[:, 128:]
    for side, y, r in ((2, 0, 0), (3, 7, 288)):
        for j in range(2):
            patch = jnp.concatenate(
                [jnp.concatenate([none if i in (0, 5) else pool[i, dz, r:r + 32] for i in (j + dx, j + dx + 2)], axis=1)
                 for dx in range(3) for dz in range(3)], axis=0)
            pre2[j, y] += dot(w2e[side], patch)
    for j in range(2):
        for y in range(8):
            pre = pre2[j, y]
            t = jnp.tanh(0.5 * pre)
            slope = 0.65 + 0.35 * t + 0.175 * pre * (1.0 - t * t)
            grad = (slope * cots[(y // 2) * 64:(y // 2) * 64 + 64, :]).astype(BF16)
            gs[j + 1, (y + 2) * 64:(y + 3) * 64] = grad[:, :128]
            gs[j + 3, (y + 2) * 64:(y + 3) * 64] = grad[:, 128:]

    def depth_terms(part):
        return part[32:64] + before2(part[64:96]) + after2(part[0:32])

    for side, i, u in ((0, 1, 2), (1, 4, 0)):
        for y in range(5):
            patch = jnp.concatenate([gs[i, q * 64:q * 64 + 192] for q in (y, y + 5)], axis=1)
            terms = dot(w2b[:, u * 192:u * 192 + 192], patch) * 0.125
            xe[side, y * 32:y * 32 + 32] = depth_terms(terms[:, :128]).astype(BF16)
            xe[side, (y + 5) * 32:(y + 6) * 32] = depth_terms(terms[:, 128:]).astype(BF16)

    def back2(j, y):
        patch = jnp.concatenate(
            [jnp.concatenate([gs[i, (y + 1) * 64:(y + 4) * 64] for i in (j + u, j + u + 2)], axis=1) for u in range(3)],
            axis=0)
        terms = dot(w2b[...], patch) * 0.125
        return depth_terms(terms[:, :128]), depth_terms(terms[:, 128:])

    for side, y in ((0, -1), (1, 8)):
        for j in range(2):
            one, two = back2(j, y)
            ye[side, j] = one.astype(BF16)
            ye[side, j + 2] = two.astype(BF16)
    third = []
    for k, (sx, sy) in enumerate(DIRS):
        a, b = (0 if sx == 1 else 1), (0 if sy == 1 else 1)
        if sx == 0:
            src, dst = ye.at[1 - b], rye.at[b]
        elif sy == 0:
            src, dst = xe.at[1 - a, pl.ds(32, 256)], rxe.at[a]
        else:
            src, dst = xe.at[1 - a, pl.ds(288 if sy == 1 else 0, 32)], rce.at[a, b]
        third.append(remote(src, dst, 16 + k, at(sx, sy)))
    start(third, (1, -1, 0))

    def cell(ref, i, where, start, size):
        rows = slice(start, start + size)
        return jnp.concatenate([ref[(i,) + where + (rows,)], ref[(i + 2,) + where + (rows,)]], axis=1)

    for j in range(2):
        for y in range(8):
            grad = cell(gs, j + 1, (), (y + 2) * 64, 64)
            for half in range(2):
                patch = jnp.concatenate(
                    [cell(pool, j + dx, (dz,), (y + dy) * 32 + half * 16, 16)
                     for dx in range(3) for dy in range(3) for dz in range(3)], axis=0)
                acc2[half, :, 0:432] += dot_nt(grad, patch)
    pair2 = remote(acc2.at[1 - dp], r2dp, 24, (gx, gy, 1 - dp))
    pair2.start()
    for j in range(2):
        for y in range(8):
            one, two = back2(j, y)
            gp[j, y * 32:y * 32 + 32] = one
            gp[j + 2, y * 32:y * 32 + 32] = two
    for b in range(6):
        width = min(128, 720 - b * 128)
        w1tr[b * 128:b * 128 + width] = dot_nt(eye[:width, :width], w1[:, b * 128:b * 128 + width]).astype(BF16)
    finish_all(third)

    for a, ok, i in ((0, up, 0), (1, down, 3)):
        gp[i] += jnp.where(ok, rxe[a].astype(F32), 0.0)
        for b, ok2, r in ((0, left, 0), (1, right, 224)):
            gp[i, r:r + 32] += jnp.where(jnp.logical_and(ok, ok2), rce[a, b].astype(F32), 0.0)
    for b, ok, r in ((0, left, 0), (1, right, 224)):
        for i in range(4):
            gp[i, r:r + 32] += jnp.where(ok, rye[b, i].astype(F32), 0.0)

    for x in range(8):
        spread = gp[x // 2]
        spread = jnp.concatenate([spread, spread], axis=1)
        spread = jnp.concatenate([spread, spread], axis=0)
        gf[x] = (sl[x] * spread).astype(BF16)
    for x in range(8):
        term = dot_nt(gf[x], xs[x:x + 3].reshape(720, 256))
        acc1[...] = term if x == 0 else acc1[...] + term

    pair2.wait()
    s2a[...] = (acc2[dp] + r2dp[...]).reshape(gxn, 8, 512)
    along2 = []
    for d in range(1, gxn):
        along2.append(remote(s2a.at[lax.rem(gx + d, gxn)], r2gx.at[d - 1], 24 + d, at(d, 0)))
        along2[-1].start()

    taps = None
    for dy in range(3):
        kept = None
        for r in range(16):
            y = 2 * (r % 8) + r // 8
            term = jnp.where(place[:, :720] == float(y + dy - 1), acc1[r * 32:r * 32 + 32], 0.0)
            kept = term if kept is None else kept + term
        parts = split_dot(kept, gather[...])
        if dy:
            parts = pltpu.roll(parts, 3 * dy, 1)
        taps = parts if taps is None else taps + parts
    for g in range(8):
        s1[g] = taps[4 * g:4 * g + 4]
    along1 = []
    for d in range(gxn):
        for e in range(2):
            if d + e:
                peer = (lax.rem(gx + d, gxn), gy, lax.rem(dp + e, 2))
                along1.append(remote(s1.at[peer[0]], r1gx.at[2 * d + e - 1], 47 + 2 * d + e, peer))
                along1[-1].start()

    for x in range(8):
        term = dot(w1tr[...], gf[x]).reshape(3, 240, 256)
        if x == 0:
            gi[0:3] = term
        else:
            gi[x:x + 2] += term[:2]
            gi[x + 2] = term[2]

    def combine(x):
        return gi[x, 80:152] + before(gi[x, 160:232]) + after(gi[x, 0:72])

    for i, x in ((0, 0), (1, 9)):
        edge = combine(x)
        sx_[i] = edge[:64]
        sc[i] = edge[64:]
    for x in range(8):
        inner = combine(x + 1)
        gi[x + 1, 80:144] = inner[:64]
        sby[x] = inner[64:]
    fourth = []
    for k, (sx, sy) in enumerate(DIRS):
        a, b = (0 if sx == 1 else 1), (0 if sy == 1 else 1)
        if sx == 0:
            src, dst = sby, ry.at[b]
        elif sy == 0:
            src, dst = sx_.at[1 if sx == 1 else 0], rx.at[a]
        else:
            src, dst = sc.at[1 if sx == 1 else 0], rc.at[a, b]
        fourth.append(remote(src, dst, 40 + k, at(sx, sy)))
    start(fourth, (1, -1, 0))
    for copy in along1:
        copy.wait()
    total1 = s1[gx]
    for i in range(2 * gxn - 1):
        total1 = total1 + r1gx[i]
    s1b[...] = total1
    across1 = []
    for d in range(1, gyn):
        across1.append(remote(s1b, r1gy.at[d - 1], 62 + d, at(0, d)))
        across1[-1].start()
    for copy in along2:
        copy.wait()
    total2 = s2a[gx]
    for d in range(1, gxn):
        total2 = total2 + r2gx[d - 1]
    for g in range(8):
        s2b[g] = total2[g:g + 1]
    across2 = []
    for d in range(1, gyn):
        across2.append(remote(s2b.at[lax.rem(gy + d, gyn)], r2gy.at[d - 1], 31 + d, at(0, d)))
        across2[-1].start()
    finish_all(fourth)
    y16 = lax.broadcasted_iota(jnp.int32, (4, 16, 256), 1)

    def ends(low_rows, high_rows):
        low_part = jnp.where(jnp.logical_and(y16 == 0, left), low_rows[4:8][:, None, :], 0.0)
        high_part = jnp.where(jnp.logical_and(y16 == 15, right), high_rows[0:4][:, None, :], 0.0)
        return (low_part + high_part).reshape(64, 256)

    for a, ok, x in ((0, up, 1), (1, down, 8)):
        term = rx[a] + ends(rc[a, 0], rc[a, 1])
        gi[x, 80:144] += jnp.where(ok, term, 0.0)

    for x in range(8):
        out[x] = (gi[x + 1, 80:144] + ends(ry[0, x], ry[1, x])).astype(BF16)

    for copy in across2:
        copy.wait()
    total2 = s2b[gy]
    for d in range(1, gyn):
        total2 = total2 + r2gy[d - 1]
    total2 = jnp.concatenate([total2 * (1.0 / (CELLS / 8) ** 0.5)] * 8, axis=0)[:, :432]
    gw2[...] = split_dot(total2, reorder[...])[0:1]
    for copy in across1:
        copy.wait()
    total1 = s1b[...]
    for d in range(1, gyn):
        total1 = total1 + r1gy[d - 1]
    mine = None
    for q in range(4):
        for c in range(4):
            ok = jnp.logical_and(gy // 2 == q, (gy % 2) * 2 + dp == c)
            term = jnp.where(ok, total1[q:q + 1, c * 32:c * 32 + 32], 0.0)
            mine = term if mine is None else mine + term
    gw1[...] = mine[:, 0:27] * (1.0 / CELLS ** 0.5)


def write_back(total, restore, part1, part2, out, gw1, gw2):
    natural = dot(total[...].reshape(512, 256), restore[...]).astype(BF16)
    for x in range(8):
        for n in range(2):
            out[n, :, x] = natural[x * 64:x * 64 + 64, n * 128:n * 128 + 128].reshape(4, 16, 128)
    gw1[...] = part1[...]
    gw2[...] = part2[...]


def on_device(gxn, gyn, consts, inputs, cotangent, w_first, w_second, b_first, b_second):
    cot = jnp.transpose(cotangent, (0, 2, 3, 4, 1)).reshape(512, 64)
    w1t = jnp.transpose(w_first, (2, 3, 4, 1, 0)).reshape(27, 4, 32)
    w2t = jnp.transpose(w_second, (2, 3, 4, 1, 0)).reshape(864, 64)
    vmem = pl.BlockSpec(memory_space=pltpu.VMEM)
    b1, b2 = b_first.reshape(1, 32), b_second.reshape(1, 64)
    c = {name: jnp.asarray(value) for name, value in consts.items()}
    operands = (
        inputs, c["select"], w1t, c["eye"], c["toeplitz"], c["place"], c["depth_map"], b1, w2t, cot, b2,
        c["pool_map"], c["cot_map"], c["gather"], c["reorder"],
    )
    scratch = [
        ((10, 240, 256), BF16), ((8, 16, 256), BF16), ((2, 8, 16, 256), BF16), ((2, 2, 4, 16, 128), BF16),
        ((2, 2, 16, 256), BF16), ((512, 720), BF16), ((720, 512), BF16), ((64, 864), BF16), ((96, 576), BF16),
        ((128, 128), F32), ((128, 128), F32), ((8, 512, 256), F32), ((8, 512, 256), BF16), ((6, 3, 320, 128), BF16),
        ((256, 256), F32), ((6, 768, 128), BF16), ((4, 256, 128), F32),
        ((2, 64, 512), F32), ((64, 512), F32), ((gxn, 8, 512), F32), ((gxn - 1, 8, 512), F32), ((gyn, 1, 512), F32),
        ((gyn - 1, 1, 512), F32), ((10, 240, 256), F32), ((8, 8, 256), F32), ((2, 8, 8, 256), F32),
        ((2, 64, 256), F32), ((2, 64, 256), F32), ((2, 8, 256), F32), ((2, 2, 8, 256), F32), ((512, 720), F32),
        ((gxn, 4, 128), F32), ((2 * gxn - 1, 4, 128), F32), ((4, 128), F32),
        ((gyn - 1, 4, 128), F32), ((128, 32), F32), ((4, 64, 288), BF16), ((2, 8, 64, 256), F32),
        ((2, 320, 128), BF16), ((2, 4, 32, 128), BF16), ((2, 256, 128), BF16), ((2, 4, 32, 128), BF16),
        ((2, 2, 32, 128), BF16),
    ]
    total, part1, part2 = pl.pallas_call(
        functools.partial(kernel, gxn, gyn),
        out_shape=(
            jax.ShapeDtypeStruct((8, 64, 256), BF16),
            jax.ShapeDtypeStruct((1, 27), F32),
            jax.ShapeDtypeStruct((1, 432), F32),
        ),
        in_specs=[pl.BlockSpec(memory_space=pl.ANY)] * NLOAD,
        out_specs=(vmem, vmem, vmem),
        scratch_shapes=[pltpu.VMEM(v.shape, v.dtype) for v in operands]
        + [pltpu.VMEM(s, d) for s, d in scratch]
        + [pltpu.SemaphoreType.DMA((70,)), pltpu.SemaphoreType.DMA((70,)), pltpu.SemaphoreType.DMA((NLOAD,))],
        compiler_params=pltpu.CompilerParams(
            collective_id=0, has_side_effects=True, vmem_limit_bytes=60 * 1024 * 1024
        ),
    )(*operands)
    result, part1, part2 = pl.pallas_call(
        write_back,
        out_shape=(
            jax.ShapeDtypeStruct(inputs.shape, BF16),
            jax.ShapeDtypeStruct((1, 27), F32),
            jax.ShapeDtypeStruct((1, 432), F32),
        ),
        in_specs=[vmem] * 4,
        out_specs=(vmem, vmem, vmem),
    )(total, c["restore"], part1, part2)
    return result, part1.reshape(27), part2.reshape(432)


def solution(mesh):
    consts = constants()
    return jax.shard_map(
        functools.partial(on_device, mesh.shape["gx"], mesh.shape["gy"], consts),
        mesh=mesh,
        in_specs=(P("dp", None, "gx", "gy", None), P("dp", None, "gx", "gy", None), P(), P(), P(), P()),
        out_specs=(P("dp", None, "gx", "gy", None), P(("gx", "gy", "dp")), P(("gx", "gy", "dp"))),
        check_vma=False,
    )
```

```python
import functools

import jax
import jax.numpy as jnp
import ml_dtypes
import numpy as np
from jax import lax
from jax.experimental import pallas as pl
from jax.experimental.pallas import tpu as pltpu
from jax.sharding import PartitionSpec as P

MESH = pl.DeviceIdType.MESH
F32 = jnp.float32
BF16 = jnp.bfloat16
DIRS = [(0, 1), (0, -1), (1, 0), (-1, 0), (1, 1), (1, -1), (-1, 1), (-1, -1)]
CELLS = 4194304
NLOAD = 18


def constants():
    depth_map = np.zeros((256, 768), np.float32)
    for n in range(2):
        for z in range(128):
            lane = (z % 2) * 128 + (z // 2 % 2) * 64 + n * 32 + z // 4
            for t in range(3):
                src = z + t - 1
                if 0 <= src < 128:
                    depth_map[n * 128 + src, t * 256 + lane] = 1
    restore = depth_map[:, 256:512].T.copy()
    pool_map = np.zeros((128, 256), np.float32)
    for n in range(2):
        for z in range(64):
            lane = (z % 2) * 64 + n * 32 + z // 2
            for half, src in ((0, z - 1), (1, z + 1)):
                if 0 <= src < 64:
                    pool_map[(src % 2) * 64 + n * 32 + src // 2, half * 128 + lane] = 1
    cot_map = np.zeros((128, 256), np.float32)
    for h in range(2):
        for b in range(2):
            for n in range(2):
                for k in range(32):
                    cot_map[n * 64 + h * 32 + k, h * 128 + b * 64 + n * 32 + k] = 1
    place = np.full((80,), -100.0, np.float32)
    chan = np.full((80,), -1)
    for c in range(4):
        for y in range(-1, 17):
            row = 64 + c if y < 0 else 68 + c if y > 15 else c * 16 + y
            place[row] = y
            chan[row] = c
    toeplitz = np.zeros((128, 3 * 768), np.float32)
    gather = np.zeros((720, 128), np.float32)
    for dx in range(3):
        for dz in range(3):
            group = dx * 240 + dz * 80
            for c in range(4):
                for dy in range(3):
                    toeplitz[((dx * 3 + dy) * 3 + dz) * 4 + c, (group + c * 16 + dy - 1) % 768] = 1
                toeplitz[((dx * 3 + 0) * 3 + dz) * 4 + c, 768 + group + 64 + c] = 1
                toeplitz[((dx * 3 + 2) * 3 + dz) * 4 + c, 1536 + group + 68 + c] = 1
            for row in range(72):
                gather[group + row, chan[row] * 32 + dx * 9 + dz] = 1
    reorder = np.zeros((432, 432), np.float32)
    for tap in range(27):
        for c in range(16):
            reorder[tap * 16 + c, c * 27 + tap] = 1
    select = np.zeros((64, 512), np.float32)
    regroup = np.zeros((64, 64), np.float32)
    expand = np.zeros((160, 128), np.float32)
    for x in range(8):
        for c in range(4):
            select[x * 4 + c, x * 64 + c * 16 + 15] = 1
            select[32 + x * 4 + c, x * 64 + c * 16] = 1
            for side in range(2):
                regroup[side * 32 + x * 4 + c, x * 8 + side * 4 + c] = 1
                expand[x * 16 + side * 4 + c, side * 32 + x * 4 + c] = 1
    for a in range(2):
        for side in range(2):
            for c in range(4):
                expand[128 + a * 16 + side * 4 + c, 64 + a * 32 + side * 16 + (12 if a == 0 else 0) + c] = 1
    b16 = lambda v: v.astype(ml_dtypes.bfloat16)
    place = np.pad(np.tile(place, 9), (0, 48), constant_values=-100)[None, :]
    return {
        "depth_map": b16(depth_map), "restore": b16(restore), "pool_map": b16(pool_map), "cot_map": b16(cot_map),
        "toeplitz": b16(toeplitz), "gather": b16(gather), "select": b16(select), "reorder": b16(reorder),
        "scatter": b16(select.T.copy()), "regroup": b16(regroup), "expand": b16(expand),
        "eye": b16(np.eye(128, dtype=np.float32)), "place": place,
    }


def dot(a, b):
    return jnp.dot(a, b, preferred_element_type=F32)


def dot_nt(a, b):
    return lax.dot_general(a, b, (((1,), (1,)), ((), ())), preferred_element_type=F32)


def split_dot(a, b):
    high = a.astype(BF16)
    rest = a - high.astype(F32)
    mid = rest.astype(BF16)
    low = (rest - mid.astype(F32)).astype(BF16)
    parts = dot(jnp.concatenate([high.astype(F32), mid.astype(F32), low.astype(F32)], axis=0).astype(BF16), b)
    rows = a.shape[0]
    return parts[:rows] + parts[rows:2 * rows] + parts[2 * rows:]


def before2(u):
    lane = lax.broadcasted_iota(jnp.int32, u.shape, 1)
    return jnp.where(
        lane < 64, jnp.where(lane % 32 != 0, pltpu.roll(u, 65, 1), 0.0), pltpu.roll(u, 64, 1)
    )


def after2(u):
    lane = lax.broadcasted_iota(jnp.int32, u.shape, 1)
    return jnp.where(
        lane >= 64, jnp.where(lane % 32 != 31, pltpu.roll(u, 63, 1), 0.0), pltpu.roll(u, 64, 1)
    )


def before(v):
    return jnp.concatenate([before2(v[:, 128:]), v[:, :128]], axis=1)


def after(v):
    return jnp.concatenate([v[:, 128:], after2(v[:, :128])], axis=1)


def kernel(
    gxn, gyn,
    *rest):
    fixed, rest = rest[:NLOAD], rest[NLOAD:]
    out, gw1, gw2 = rest[:3]
    kept, rest = rest[3:3 + NLOAD], rest[3 + NLOAD:]
    (xs, hb, hlr, hx, hc, w1, w1tr, w2, w2b, bias1, bias2, sl, gf, pool, cots, gs, gp,
    acc2, r2dp, s2a, r2gx, s2b, r2gy, gi, sby, ry, sx_, rx, sc, rc, acc1, s1, r1gx, s1b, r1gy,
    w1f, w2e, pre2, xe, ye, rxe, rye, rce, ssem, rsem, lsem) = rest
    inp, select, w1t, eye, toeplitz, place, depth_map, b1r, expand, w2t, cot, b2r, pool_map, cot_map, *others = kept
    gather, reorder, regroup, scatter = others
    loads = [pltpu.make_async_copy(fixed[i], kept[i], lsem.at[i]) for i in range(NLOAD)]
    for load in loads:
        load.start()
    gx, gy, dp = lax.axis_index("gx"), lax.axis_index("gy"), lax.axis_index("dp")

    def at(sx, sy):
        return (lax.rem(gx + sx + gxn, gxn), lax.rem(gy + sy + gyn, gyn), dp)

    def remote(src, dst, k, device):
        return pltpu.make_async_remote_copy(
            src_ref=src, dst_ref=dst, send_sem=ssem.at[k], recv_sem=rsem.at[k], device_id=device, device_id_type=MESH
        )

    left, right = gy > 0, gy < gyn - 1
    up, down = gx > 0, gx < gxn - 1

    def start(copies, which):
        for sx in which:
            picked = [c for c, d in zip(copies, DIRS) if d[0] == sx]
            if sx == 0:
                for copy in picked:
                    copy.start()
            else:
                @pl.when(down if sx == 1 else up)
                def _(picked=picked):
                    for copy in picked:
                        copy.start()

    def finish_all(copies):
        by = {sx: [c for c, d in zip(copies, DIRS) if d[0] == sx] for sx in (0, 1, -1)}
        for sx in (1, -1):
            @pl.when(down if sx == 1 else up)
            def _(sx=sx):
                for copy in by[sx]:
                    copy.wait_send()
                for copy in by[-sx]:
                    copy.wait_recv()
        for copy in by[0]:
            copy.wait()

    barrier = pltpu.get_barrier_semaphore()
    peers = [at(*d) for d in DIRS]
    peers += [at(d, 0) for d in range(2, gxn - 1)] + [at(0, d) for d in range(2, gyn - 1)]
    peers += [(lax.rem(gx + d, gxn), gy, 1 - dp) for d in range(gxn)]
    for peer in peers:
        pl.semaphore_signal(barrier, inc=1, device_id=peer, device_id_type=MESH)

    def raw(x):
        halves = [inp[n, :, x].reshape(64, 128) for n in range(2)]
        return jnp.concatenate(halves, axis=1)

    loads[0].wait()
    loads[1].wait()
    own = jnp.concatenate([raw(x) for x in range(8)], axis=0)
    hb[...] = dot(select[...], own).astype(BF16)
    pl.semaphore_wait(barrier, len(peers))
    first = []
    for k, (sx, sy) in enumerate(DIRS):
        a, b = (0 if sx == 1 else 1), (0 if sy == 1 else 1)
        if sx == 0:
            src, dst = hb.at[pl.ds(b * 32, 32)], hlr.at[pl.ds(b * 32, 32)]
        elif sy == 0:
            src, dst = inp.at[:, :, 7 if sx == 1 else 0], hx.at[a]
        else:
            src, dst = hb.at[pl.ds(b * 32 + 16 - a * 16, 16)], hc.at[a, b]
        first.append(remote(src, dst, k, at(sx, sy)))
    start(first, (1, -1, 0))

    for load in loads[2:9]:
        load.wait()
    w1f[...] = jnp.zeros_like(w1f)
    for tap in range(27):
        w1f[tap * 4:tap * 4 + 4] = w1t[tap].astype(F32)
    small = dot_nt(eye[:32, :32], w1f[...].astype(BF16)).astype(BF16)
    base = dot(small, toeplitz[...])
    for r in range(16):
        y = 2 * (r % 8) + r // 8
        block = base[:, :768] if y == 0 else pltpu.roll(base[:, :768], y, 1)
        block = jnp.where(jnp.abs(place[...] - float(y)) < 1.5, block, 0.0)
        if y == 0:
            block = block + base[:, 768:1536]
        if y == 15:
            block = block + base[:, 1536:]
        w1[r * 32:r * 32 + 32, :] = block[:, :720].astype(BF16)
    bias1[...] = jnp.zeros_like(bias1)
    bias1[:, 0:32] = jnp.broadcast_to(b1r[...], (128, 32))
    b1 = jnp.transpose(bias1[...])[:32]
    b1 = jnp.concatenate([b1, b1], axis=1)
    spread = dot(own, depth_map[...]).astype(BF16)
    for x in range(8):
        for t in range(3):
            xs[x + 1, t * 80:t * 80 + 64] = spread[x * 64:x * 64 + 64, t * 256:t * 256 + 256]
    finish_all(first)
    sides = [jnp.where(left, hlr[0:32].astype(F32), 0.0), jnp.where(right, hlr[32:64].astype(F32), 0.0)]
    for a, ok in ((0, up), (1, down)):
        for b, ok2 in ((0, left), (1, right)):
            sides.append(jnp.where(jnp.logical_and(ok, ok2), hc[a, b].astype(F32), 0.0))
    rims = dot(expand[...], jnp.concatenate(sides, axis=0).astype(BF16))
    blocks = [rims[:128]]
    for a, ok in ((0, up), (1, down)):
        rows = [hx[a, n].reshape(64, 128) for n in range(2)]
        blocks.append(jnp.where(ok, jnp.concatenate(rows, axis=1).astype(F32), 0.0))
        blocks.append(rims[128 + a * 16:144 + a * 16])
    spread = dot(jnp.concatenate(blocks, axis=0).astype(BF16), depth_map[...]).astype(BF16)
    pieces = [(x + 1, 64, x * 16, 16) for x in range(8)]
    pieces += [(0, 0, 128, 64), (0, 64, 192, 16), (9, 0, 208, 64), (9, 64, 272, 16)]
    for index, row, at_row, size in pieces:
        for t in range(3):
            xs[index, t * 80 + row:t * 80 + row + size] = spread[at_row:at_row + size, t * 256:t * 256 + 256]

    b1all = jnp.concatenate([b1] * 16, axis=0)

    def layer1(j):
        total = None
        for px in range(2):
            x = 2 * j + px
            pre = dot(w1[...], xs[x:x + 3].reshape(720, 256)) + b1all
            t = jnp.tanh(0.5 * pre)
            value = pre * (0.65 + 0.35 * t)
            sl[x] = 0.65 + 0.35 * t + 0.175 * pre * (1.0 - t * t)
            value = value[:256] + value[256:]
            value = value[:, :128] + value[:, 128:]
            total = value if total is None else total + value
        pool[j + 1, 1, 32:288] = (total * 0.125).astype(BF16)

    second = []
    for k, (sx, sy) in enumerate(DIRS):
        src_x, dst_x = {0: (pl.ds(1, 4),) * 2, 1: (4, 0), -1: (1, 5)}[sx]
        src_y, dst_y = {0: (pl.ds(32, 256),) * 2, 1: (pl.ds(256, 32), pl.ds(0, 32)), -1: (pl.ds(32, 32), pl.ds(288, 32))}[sy]
        second.append(remote(pool.at[src_x, 1, src_y], pool.at[dst_x, 1, dst_y], 8 + k, at(sx, sy)))
    layer1(0)
    layer1(3)
    start(second, (1, -1))
    layer1(1)
    layer1(2)
    start(second, (0,))

    for load in loads[9:]:
        load.wait()
    w2[...] = dot_nt(eye[:64, :64], w2t[...]).astype(BF16)
    for dx in range(3):
        for dy in range(3):
            at_lane = ((2 - dx) * 3 + 2 - dy) * 64
            row = (dx * 3 + dy) * 96
            w2b[:, at_lane:at_lane + 64] = w2t[row:row + 96, :]
    bias2[...] = jnp.zeros_like(bias2)
    bias2[:, 0:64] = jnp.broadcast_to(b2r[...], (128, 64))
    b2 = jnp.transpose(bias2[...])[:64]
    b2 = jnp.concatenate([b2, b2], axis=1)
    for i in range(1, 5):
        spread = dot(pool[i, 1, 32:288], pool_map[...]).astype(BF16)
        pool[i, 0, 32:288] = spread[:, :128]
        pool[i, 2, 32:288] = spread[:, 128:]
    none = jnp.zeros((32, 128), BF16)

    def piece(i, dz, r):
        return none if i in (0, 5) or r in (0, 9) else pool[i, dz, r * 32:r * 32 + 32]

    def pair(i, dz, r):
        return jnp.concatenate([piece(i, dz, r), piece(i + 2, dz, r)], axis=1)

    for j in range(2):
        for y in range(8):
            patch = jnp.concatenate(
                [pair(j + dx, dz, y + dy) for dx in range(3) for dy in range(3) for dz in range(3)], axis=0)
            pre2[j, y] = dot(w2[...], patch) + b2

    for q in range(4):
        part = jnp.concatenate(
            [cot[(n * 8 + h * 4 + q) * 32:(n * 8 + h * 4 + q) * 32 + 32, :] for n in range(2) for h in range(2)], axis=0
        )
        turned = dot_nt(eye[:64, :64], part).astype(BF16)
        cots[q * 64:q * 64 + 64] = dot(turned, cot_map[...]) * 0.125

    acc2[...] = jnp.zeros_like(acc2)
    for i in (0, 5):
        gs[i] = jnp.zeros((768, 128), BF16)
    for i in range(1, 5):
        gs[i, 0:128] = jnp.zeros((128, 128), BF16)
        gs[i, 640:768] = jnp.zeros((128, 128), BF16)
    for i, picked in enumerate((
        [(0, dy) for dy in range(3)], [(2, dy) for dy in range(3)], [(dx, 0) for dx in range(3)], [(dx, 2) for dx in range(3)]
    )):
        rows = [w2t[(dx * 3 + dy) * 96:(dx * 3 + dy) * 96 + 96, :] for dx, dy in picked]
        w2e[i] = dot_nt(eye[:64, :64], jnp.concatenate(rows, axis=0)).astype(BF16)
    finish_all(second)
    for ok, index in ((up, 0), (down, 5)):
        @pl.when(jnp.logical_not(ok))
        def _(index=index):
            pool[index, 1] = jnp.zeros((320, 128), BF16)
    for ok, index in ((left, 0), (right, 288)):
        @pl.when(jnp.logical_not(ok))
        def _(index=index):
            pool[:, 1, index:index + 32] = jnp.zeros((6, 32, 128), BF16)

    for i in (0, 5):
        spread = dot(pool[i, 1], pool_map[...]).astype(BF16)
        pool[i, 0] = spread[:, :128]
        pool[i, 2] = spread[:, 128:]
    rims = [(i, r) for i in range(1, 5) for r in (0, 288)]
    spread = dot(jnp.concatenate([pool[i, 1, r:r + 32] for i, r in rims], axis=0), pool_map[...]).astype(BF16)
    for q, (i, r) in enumerate(rims):
        pool[i, 0, r:r + 32] = spread[q * 32:q * 32 + 32, :128]
        pool[i, 2, r:r + 32] = spread[q * 32:q * 32 + 32, 128:]
    for side, i in ((0, 0), (1, 5)):
        for y in range(4):
            patch = jnp.concatenate(
                [jnp.concatenate([pool[i, dz, (q + dy) * 32:(q + dy) * 32 + 32] for q in (y, y + 4)], axis=1)
                 for dy in range(3) for dz in range(3)], axis=0)
            term = dot(w2e[side], patch)
            lanes = slice(side * 128, side * 128 + 128)
            pre2[side, y, :, lanes] += term[:, :128]
            pre2[side, y + 4, :, lanes] += term[:, 128:]
    for side, y, r in ((2, 0, 0), (3, 7, 288)):
        for j in range(2):
            patch = jnp.concatenate(
                [jnp.concatenate([none if i in (0, 5) else pool[i, dz, r:r + 32] for i in (j + dx, j + dx + 2)], axis=1)
                 for dx in range(3) for dz in range(3)], axis=0)
            pre2[j, y] += dot(w2e[side], patch)
    for j in range(2):
        for y in range(8):
            pre = pre2[j, y]
            t = jnp.tanh(0.5 * pre)
            slope = 0.65 + 0.35 * t + 0.175 * pre * (1.0 - t * t)
            grad = (slope * cots[(y // 2) * 64:(y // 2) * 64 + 64, :]).astype(BF16)
            gs[j + 1, (y + 2) * 64:(y + 3) * 64] = grad[:, :128]
            gs[j + 3, (y + 2) * 64:(y + 3) * 64] = grad[:, 128:]

    def depth_terms(part):
        return part[32:64] + before2(part[64:96]) + after2(part[0:32])

    for side, i, u in ((0, 1, 2), (1, 4, 0)):
        for y in range(5):
            patch = jnp.concatenate([gs[i, q * 64:q * 64 + 192] for q in (y, y + 5)], axis=1)
            terms = dot(w2b[:, u * 192:u * 192 + 192], patch) * 0.125
            xe[side, y * 32:y * 32 + 32] = depth_terms(terms[:, :128]).astype(BF16)
            xe[side, (y + 5) * 32:(y + 6) * 32] = depth_terms(terms[:, 128:]).astype(BF16)

    def back2(j, y):
        patch = jnp.concatenate(
            [jnp.concatenate([gs[i, (y + 1) * 64:(y + 4) * 64] for i in (j + u, j + u + 2)], axis=1) for u in range(3)],
            axis=0)
        terms = dot(w2b[...], patch) * 0.125
        return depth_terms(terms[:, :128]), depth_terms(terms[:, 128:])

    for side, y in ((0, -1), (1, 8)):
        for j in range(2):
            one, two = back2(j, y)
            ye[side, j] = one.astype(BF16)
            ye[side, j + 2] = two.astype(BF16)
    third = []
    for k, (sx, sy) in enumerate(DIRS):
        a, b = (0 if sx == 1 else 1), (0 if sy == 1 else 1)
        if sx == 0:
            src, dst = ye.at[1 - b], rye.at[b]
        elif sy == 0:
            src, dst = xe.at[1 - a, pl.ds(32, 256)], rxe.at[a]
        else:
            src, dst = xe.at[1 - a, pl.ds(288 if sy == 1 else 0, 32)], rce.at[a, b]
        third.append(remote(src, dst, 16 + k, at(sx, sy)))
    start(third, (1, -1, 0))

    def cell(ref, i, where, start, size):
        rows = slice(start, start + size)
        return jnp.concatenate([ref[(i,) + where + (rows,)], ref[(i + 2,) + where + (rows,)]], axis=1)

    for j in range(2):
        for y in range(8):
            grad = cell(gs, j + 1, (), (y + 2) * 64, 64)
            for half in range(2):
                patch = jnp.concatenate(
                    [cell(pool, j + dx, (dz,), (y + dy) * 32 + half * 16, 16)
                     for dx in range(3) for dy in range(3) for dz in range(3)], axis=0)
                acc2[half, :, 0:432] += dot_nt(grad, patch)
    pair2 = remote(acc2.at[1 - dp], r2dp, 24, (gx, gy, 1 - dp))
    pair2.start()
    for j in range(2):
        for y in range(8):
            one, two = back2(j, y)
            gp[j, y * 32:y * 32 + 32] = one
            gp[j + 2, y * 32:y * 32 + 32] = two
    for b in range(6):
        width = min(128, 720 - b * 128)
        w1tr[b * 128:b * 128 + width] = dot_nt(eye[:width, :width], w1[:, b * 128:b * 128 + width]).astype(BF16)
    finish_all(third)

    for a, ok, i in ((0, up, 0), (1, down, 3)):
        gp[i] += jnp.where(ok, rxe[a].astype(F32), 0.0)
        for b, ok2, r in ((0, left, 0), (1, right, 224)):
            gp[i, r:r + 32] += jnp.where(jnp.logical_and(ok, ok2), rce[a, b].astype(F32), 0.0)
    for b, ok, r in ((0, left, 0), (1, right, 224)):
        for i in range(4):
            gp[i, r:r + 32] += jnp.where(ok, rye[b, i].astype(F32), 0.0)

    pair2.wait()
    s2a[...] = (acc2[dp] + r2dp[...]).reshape(gxn, 8, 512)
    along2 = []
    for d in range(1, gxn):
        along2.append(remote(s2a.at[lax.rem(gx + d, gxn)], r2gx.at[d - 1], 24 + d, at(d, 0)))
        along2[-1].start()

    for x in range(8):
        spread = gp[x // 2]
        spread = jnp.concatenate([spread, spread], axis=1)
        spread = jnp.concatenate([spread, spread], axis=0)
        gf[x] = (sl[x] * spread).astype(BF16)
    for x in range(8):
        term = dot_nt(gf[x], xs[x:x + 3].reshape(720, 256))
        acc1[...] = term if x == 0 else acc1[...] + term

    taps = None
    for dy in range(3):
        kept = None
        for r in range(16):
            y = 2 * (r % 8) + r // 8
            term = jnp.where(place[:, :720] == float(y + dy - 1), acc1[r * 32:r * 32 + 32], 0.0)
            kept = term if kept is None else kept + term
        parts = split_dot(kept, gather[...])
        if dy:
            parts = pltpu.roll(parts, 3 * dy, 1)
        taps = parts if taps is None else taps + parts
    for g in range(8):
        s1[g] = taps[4 * g:4 * g + 4]
    along1 = []
    for d in range(gxn):
        for e in range(2):
            if d + e:
                peer = (lax.rem(gx + d, gxn), gy, lax.rem(dp + e, 2))
                along1.append(remote(s1.at[peer[0]], r1gx.at[2 * d + e - 1], 47 + 2 * d + e, peer))
                along1[-1].start()

    for copy in along2:
        copy.wait()
    total2 = s2a[gx]
    for d in range(1, gxn):
        total2 = total2 + r2gx[d - 1]
    for g in range(8):
        s2b[g] = total2[g:g + 1]
    across2 = []
    for d in range(1, gyn):
        across2.append(remote(s2b.at[lax.rem(gy + d, gyn)], r2gy.at[d - 1], 31 + d, at(0, d)))
        across2[-1].start()
    for x in range(8):
        term = dot(w1tr[...], gf[x]).reshape(3, 240, 256)
        if x == 0:
            gi[0:3] = term
        else:
            gi[x:x + 2] += term[:2]
            gi[x + 2] = term[2]

    def combine(x):
        return gi[x, 80:152] + before(gi[x, 160:232]) + after(gi[x, 0:72])

    for i, x in ((0, 0), (1, 9)):
        edge = combine(x)
        sx_[i] = edge[:64].astype(BF16)
        sc[i] = jnp.concatenate([edge[64:], edge[64:]], axis=0).astype(BF16)
    outer = []
    for x in range(8):
        inner = combine(x + 1)
        gi[x + 1, 80:144] = inner[:64]
        outer.append(inner[64:])
    sby[...] = dot(regroup[...], jnp.concatenate(outer, axis=0).astype(BF16)).astype(BF16)
    fourth = []
    for k, (sx, sy) in enumerate(DIRS):
        a, b = (0 if sx == 1 else 1), (0 if sy == 1 else 1)
        if sx == 0:
            src, dst = sby.at[pl.ds(32 - b * 32, 32)], ry.at[pl.ds(32 - b * 32, 32)]
        elif sy == 0:
            src, dst = sx_.at[1 if sx == 1 else 0], rx.at[a]
        else:
            src, dst = sc.at[1 if sx == 1 else 0], rc.at[a, b]
        fourth.append(remote(src, dst, 40 + k, at(sx, sy)))
    start(fourth, (1, -1, 0))
    for copy in along1:
        copy.wait()
    total1 = s1[gx]
    for i in range(2 * gxn - 1):
        total1 = total1 + r1gx[i]
    s1b[...] = total1
    across1 = []
    for d in range(1, gyn):
        across1.append(remote(s1b, r1gy.at[d - 1], 62 + d, at(0, d)))
        across1[-1].start()
    for copy in across2:
        copy.wait()
    total2 = s2b[gy]
    for d in range(1, gyn):
        total2 = total2 + r2gy[d - 1]
    total2 = jnp.concatenate([total2 * (1.0 / (CELLS / 8) ** 0.5)] * 8, axis=0)[:, :432]
    gw2[...] = split_dot(total2, reorder[...])[0:1]
    finish_all(fourth)
    y16 = lax.broadcasted_iota(jnp.int32, (4, 16, 256), 1)

    def ends(low_rows, high_rows):
        low_part = jnp.where(jnp.logical_and(y16 == 0, left), low_rows[4:8][:, None, :], 0.0)
        high_part = jnp.where(jnp.logical_and(y16 == 15, right), high_rows[0:4][:, None, :], 0.0)
        return (low_part + high_part).reshape(64, 256)

    for a, ok, x in ((0, up, 1), (1, down, 8)):
        term = rx[a].astype(F32) + ends(rc[a, 0].astype(F32), rc[a, 1].astype(F32))
        gi[x, 80:144] += jnp.where(ok, term, 0.0)
    sides = [jnp.where(right, ry[0:32].astype(F32), 0.0), jnp.where(left, ry[32:64].astype(F32), 0.0)]
    extra = dot(scatter[...], jnp.concatenate(sides, axis=0).astype(BF16))
    for x in range(8):
        out[x] = (gi[x + 1, 80:144] + extra[x * 64:x * 64 + 64]).astype(BF16)

    for copy in across1:
        copy.wait()
    total1 = s1b[...]
    for d in range(1, gyn):
        total1 = total1 + r1gy[d - 1]
    mine = None
    for q in range(4):
        for c in range(4):
            ok = jnp.logical_and(gy // 2 == q, (gy % 2) * 2 + dp == c)
            term = jnp.where(ok, total1[q:q + 1, c * 32:c * 32 + 32], 0.0)
            mine = term if mine is None else mine + term
    gw1[...] = mine[:, 0:27] * (1.0 / CELLS ** 0.5)


def write_back(total, restore, part1, part2, out, gw1, gw2):
    natural = dot(total[...].reshape(512, 256), restore[...]).astype(BF16)
    for x in range(8):
        for n in range(2):
            out[n, :, x] = natural[x * 64:x * 64 + 64, n * 128:n * 128 + 128].reshape(4, 16, 128)
    gw1[...] = part1[...]
    gw2[...] = part2[...]


def on_device(gxn, gyn, consts, inputs, cotangent, w_first, w_second, b_first, b_second):
    cot = jnp.transpose(cotangent, (0, 2, 3, 4, 1)).reshape(512, 64)
    w1t = jnp.transpose(w_first, (2, 3, 4, 1, 0)).reshape(27, 4, 32)
    w2t = jnp.transpose(w_second, (2, 3, 4, 1, 0)).reshape(864, 64)
    vmem = pl.BlockSpec(memory_space=pltpu.VMEM)
    b1, b2 = b_first.reshape(1, 32), b_second.reshape(1, 64)
    c = {name: jnp.asarray(value) for name, value in consts.items()}
    operands = (
        inputs, c["select"], w1t, c["eye"], c["toeplitz"], c["place"], c["depth_map"], b1, c["expand"], w2t, cot, b2,
        c["pool_map"], c["cot_map"], c["gather"], c["reorder"], c["regroup"], c["scatter"],
    )
    scratch = [
        ((10, 240, 256), BF16), ((64, 256), BF16), ((64, 256), BF16), ((2, 2, 4, 16, 128), BF16),
        ((2, 2, 16, 256), BF16), ((512, 720), BF16), ((720, 512), BF16), ((64, 864), BF16), ((96, 576), BF16),
        ((128, 128), F32), ((128, 128), F32), ((8, 512, 256), F32), ((8, 512, 256), BF16), ((6, 3, 320, 128), BF16),
        ((256, 256), F32), ((6, 768, 128), BF16), ((4, 256, 128), F32),
        ((2, 64, 512), F32), ((64, 512), F32), ((gxn, 8, 512), F32), ((gxn - 1, 8, 512), F32), ((gyn, 1, 512), F32),
        ((gyn - 1, 1, 512), F32), ((10, 240, 256), F32), ((64, 256), BF16), ((64, 256), BF16),
        ((2, 64, 256), BF16), ((2, 64, 256), BF16), ((2, 16, 256), BF16), ((2, 2, 16, 256), BF16), ((512, 720), F32),
        ((gxn, 4, 128), F32), ((2 * gxn - 1, 4, 128), F32), ((4, 128), F32),
        ((gyn - 1, 4, 128), F32), ((128, 32), F32), ((4, 64, 288), BF16), ((2, 8, 64, 256), F32),
        ((2, 320, 128), BF16), ((2, 4, 32, 128), BF16), ((2, 256, 128), BF16), ((2, 4, 32, 128), BF16),
        ((2, 2, 32, 128), BF16),
    ]
    total, part1, part2 = pl.pallas_call(
        functools.partial(kernel, gxn, gyn),
        out_shape=(
            jax.ShapeDtypeStruct((8, 64, 256), BF16),
            jax.ShapeDtypeStruct((1, 27), F32),
            jax.ShapeDtypeStruct((1, 432), F32),
        ),
        in_specs=[pl.BlockSpec(memory_space=pl.ANY)] * NLOAD,
        out_specs=(vmem, vmem, vmem),
        scratch_shapes=[pltpu.VMEM(v.shape, v.dtype) for v in operands]
        + [pltpu.VMEM(s, d) for s, d in scratch]
        + [pltpu.SemaphoreType.DMA((70,)), pltpu.SemaphoreType.DMA((70,)), pltpu.SemaphoreType.DMA((NLOAD,))],
        compiler_params=pltpu.CompilerParams(
            collective_id=0, has_side_effects=True, vmem_limit_bytes=60 * 1024 * 1024
        ),
    )(*operands)
    result, part1, part2 = pl.pallas_call(
        write_back,
        out_shape=(
            jax.ShapeDtypeStruct(inputs.shape, BF16),
            jax.ShapeDtypeStruct((1, 27), F32),
            jax.ShapeDtypeStruct((1, 432), F32),
        ),
        in_specs=[vmem] * 4,
        out_specs=(vmem, vmem, vmem),
    )(total, c["restore"], part1, part2)
    return result, part1.reshape(27), part2.reshape(432)


def solution(mesh):
    consts = constants()
    return jax.shard_map(
        functools.partial(on_device, mesh.shape["gx"], mesh.shape["gy"], consts),
        mesh=mesh,
        in_specs=(P("dp", None, "gx", "gy", None), P("dp", None, "gx", "gy", None), P(), P(), P(), P()),
        out_specs=(P("dp", None, "gx", "gy", None), P(("gx", "gy", "dp")), P(("gx", "gy", "dp"))),
        check_vma=False,
    )
```

```python
import functools

import jax
import jax.numpy as jnp
import ml_dtypes
import numpy as np
from jax import lax
from jax.experimental import pallas as pl
from jax.experimental.pallas import tpu as pltpu
from jax.sharding import PartitionSpec as P

MESH = pl.DeviceIdType.MESH
F32 = jnp.float32
BF16 = jnp.bfloat16
DIRS = [(0, 1), (0, -1), (1, 0), (-1, 0), (1, 1), (1, -1), (-1, 1), (-1, -1)]
CELLS = 4194304
NLOAD = 18


def constants():
    depth_map = np.zeros((256, 768), np.float32)
    for n in range(2):
        for z in range(128):
            lane = (z % 2) * 128 + (z // 2 % 2) * 64 + n * 32 + z // 4
            for t in range(3):
                src = z + t - 1
                if 0 <= src < 128:
                    depth_map[n * 128 + src, t * 256 + lane] = 1
    restore = depth_map[:, 256:512].T.copy()
    pool_map = np.zeros((128, 256), np.float32)
    for n in range(2):
        for z in range(64):
            lane = (z % 2) * 64 + n * 32 + z // 2
            for half, src in ((0, z - 1), (1, z + 1)):
                if 0 <= src < 64:
                    pool_map[(src % 2) * 64 + n * 32 + src // 2, half * 128 + lane] = 1
    cot_map = np.zeros((128, 256), np.float32)
    for h in range(2):
        for b in range(2):
            for n in range(2):
                for k in range(32):
                    cot_map[n * 64 + h * 32 + k, h * 128 + b * 64 + n * 32 + k] = 1
    place = np.full((80,), -100.0, np.float32)
    chan = np.full((80,), -1)
    for c in range(4):
        for y in range(-1, 17):
            row = 64 + c if y < 0 else 68 + c if y > 15 else c * 16 + y
            place[row] = y
            chan[row] = c
    toeplitz = np.zeros((128, 3 * 768), np.float32)
    gather = np.zeros((720, 128), np.float32)
    for dx in range(3):
        for dz in range(3):
            group = dx * 240 + dz * 80
            for c in range(4):
                for dy in range(3):
                    toeplitz[((dx * 3 + dy) * 3 + dz) * 4 + c, (group + c * 16 + dy - 1) % 768] = 1
                toeplitz[((dx * 3 + 0) * 3 + dz) * 4 + c, 768 + group + 64 + c] = 1
                toeplitz[((dx * 3 + 2) * 3 + dz) * 4 + c, 1536 + group + 68 + c] = 1
            for row in range(72):
                gather[group + row, chan[row] * 32 + dx * 9 + dz] = 1
    reorder = np.zeros((432, 432), np.float32)
    for tap in range(27):
        for c in range(16):
            reorder[tap * 16 + c, c * 27 + tap] = 1
    select = np.zeros((64, 512), np.float32)
    regroup = np.zeros((64, 64), np.float32)
    expand = np.zeros((160, 128), np.float32)
    for x in range(8):
        for c in range(4):
            select[x * 4 + c, x * 64 + c * 16 + 15] = 1
            select[32 + x * 4 + c, x * 64 + c * 16] = 1
            for side in range(2):
                regroup[side * 32 + x * 4 + c, x * 8 + side * 4 + c] = 1
                expand[x * 16 + side * 4 + c, side * 32 + x * 4 + c] = 1
    for a in range(2):
        for side in range(2):
            for c in range(4):
                expand[128 + a * 16 + side * 4 + c, 64 + a * 32 + side * 16 + (12 if a == 0 else 0) + c] = 1
    b16 = lambda v: v.astype(ml_dtypes.bfloat16)
    place = np.pad(np.tile(place, 9), (0, 48), constant_values=-100)[None, :]
    return {
        "depth_map": b16(depth_map), "restore": b16(restore), "pool_map": b16(pool_map), "cot_map": b16(cot_map),
        "toeplitz": b16(toeplitz), "gather": b16(gather), "select": b16(select), "reorder": b16(reorder),
        "scatter": b16(select.T.copy()), "regroup": b16(regroup), "expand": b16(expand),
        "eye": b16(np.eye(128, dtype=np.float32)), "place": place,
    }


def dot(a, b):
    return jnp.dot(a, b, preferred_element_type=F32)


def dot_nt(a, b):
    return lax.dot_general(a, b, (((1,), (1,)), ((), ())), preferred_element_type=F32)


def split_dot(a, b):
    high = a.astype(BF16)
    rest = a - high.astype(F32)
    mid = rest.astype(BF16)
    low = (rest - mid.astype(F32)).astype(BF16)
    parts = dot(jnp.concatenate([high.astype(F32), mid.astype(F32), low.astype(F32)], axis=0).astype(BF16), b)
    rows = a.shape[0]
    return parts[:rows] + parts[rows:2 * rows] + parts[2 * rows:]


def before2(u):
    lane = lax.broadcasted_iota(jnp.int32, u.shape, 1)
    return jnp.where(
        lane < 64, jnp.where(lane % 32 != 0, pltpu.roll(u, 65, 1), 0.0), pltpu.roll(u, 64, 1)
    )


def after2(u):
    lane = lax.broadcasted_iota(jnp.int32, u.shape, 1)
    return jnp.where(
        lane >= 64, jnp.where(lane % 32 != 31, pltpu.roll(u, 63, 1), 0.0), pltpu.roll(u, 64, 1)
    )


def before(v):
    return jnp.concatenate([before2(v[:, 128:]), v[:, :128]], axis=1)


def after(v):
    return jnp.concatenate([v[:, 128:], after2(v[:, :128])], axis=1)


def kernel(
    gxn, gyn,
    *rest):
    fixed, rest = rest[:NLOAD], rest[NLOAD:]
    out, gw1, gw2 = rest[:3]
    kept, rest = rest[3:3 + NLOAD], rest[3 + NLOAD:]
    (xs, hb, hlr, hx, hc, w1, w1tr, w2, w2b, bias1, bias2, sl, gf, pool, cots, gs, gp,
    acc2, r2dp, s2a, r2gx, s2b, r2gy, gi, sby, ry, sx_, rx, sc, rc, acc1, s1, r1gx, s1b, r1gy,
    w1f, w2e, pre2, xe, ye, rxe, rye, rce, ssem, rsem, lsem) = rest
    inp, select, w1t, eye, toeplitz, place, depth_map, b1r, expand, w2t, cot, b2r, pool_map, cot_map, *others = kept
    gather, reorder, regroup, scatter = others
    loads = [pltpu.make_async_copy(fixed[i], kept[i], lsem.at[i]) for i in range(NLOAD)]
    for load in loads[:2]:
        load.start()
    gx, gy, dp = lax.axis_index("gx"), lax.axis_index("gy"), lax.axis_index("dp")

    def at(sx, sy):
        return (lax.rem(gx + sx + gxn, gxn), lax.rem(gy + sy + gyn, gyn), dp)

    def remote(src, dst, k, device):
        return pltpu.make_async_remote_copy(
            src_ref=src, dst_ref=dst, send_sem=ssem.at[k], recv_sem=rsem.at[k], device_id=device, device_id_type=MESH
        )

    left, right = gy > 0, gy < gyn - 1
    up, down = gx > 0, gx < gxn - 1

    def start(copies, which):
        for sx in which:
            picked = [c for c, d in zip(copies, DIRS) if d[0] == sx]
            if sx == 0:
                for copy in picked:
                    copy.start()
            else:
                @pl.when(down if sx == 1 else up)
                def _(picked=picked):
                    for copy in picked:
                        copy.start()

    def finish_all(copies):
        by = {sx: [c for c, d in zip(copies, DIRS) if d[0] == sx] for sx in (0, 1, -1)}
        for sx in (1, -1):
            @pl.when(down if sx == 1 else up)
            def _(sx=sx):
                for copy in by[sx]:
                    copy.wait_send()
                for copy in by[-sx]:
                    copy.wait_recv()
        for copy in by[0]:
            copy.wait()

    barrier = pltpu.get_barrier_semaphore()
    peers = [at(*d) for d in DIRS]
    peers += [at(d, 0) for d in range(2, gxn - 1)] + [at(0, d) for d in range(2, gyn - 1)]
    peers += [(lax.rem(gx + d, gxn), gy, 1 - dp) for d in range(gxn)]
    for peer in peers:
        pl.semaphore_signal(barrier, inc=1, device_id=peer, device_id_type=MESH)
    for load in loads[2:]:
        load.start()

    def raw(x):
        halves = [inp[n, :, x].reshape(64, 128) for n in range(2)]
        return jnp.concatenate(halves, axis=1)

    pl.semaphore_wait(barrier, len(peers))
    faces = []
    for k, sx in ((2, 1), (3, -1)):
        faces.append(remote(fixed[0].at[:, :, 7 if sx == 1 else 0], hx.at[0 if sx == 1 else 1], k, at(sx, 0)))
    for copy, ok in zip(faces, (down, up)):
        @pl.when(ok)
        def _(copy=copy):
            copy.start()
    loads[0].wait()
    loads[1].wait()
    own = jnp.concatenate([raw(x) for x in range(8)], axis=0)
    hb[...] = dot(select[...], own).astype(BF16)
    first = []
    for k, (sx, sy) in enumerate(DIRS):
        a, b = (0 if sx == 1 else 1), (0 if sy == 1 else 1)
        if sx == 0:
            src, dst = hb.at[pl.ds(b * 32, 32)], hlr.at[pl.ds(b * 32, 32)]
        elif sy == 0:
            first.append(faces[a])
            continue
        else:
            src, dst = hb.at[pl.ds(b * 32 + 16 - a * 16, 16)], hc.at[a, b]
        first.append(remote(src, dst, k, at(sx, sy)))
    start(first, (0,))
    for sx, ok in ((1, down), (-1, up)):
        @pl.when(ok)
        def _(sx=sx):
            for copy, d in zip(first, DIRS):
                if d[0] == sx and d[1]:
                    copy.start()

    for load in loads[2:9]:
        load.wait()
    w1f[...] = jnp.zeros_like(w1f)
    for tap in range(27):
        w1f[tap * 4:tap * 4 + 4] = w1t[tap].astype(F32)
    small = dot_nt(eye[:32, :32], w1f[...].astype(BF16)).astype(BF16)
    base = dot(small, toeplitz[...])
    for r in range(16):
        y = 2 * (r % 8) + r // 8
        block = base[:, :768] if y == 0 else pltpu.roll(base[:, :768], y, 1)
        block = jnp.where(jnp.abs(place[...] - float(y)) < 1.5, block, 0.0)
        if y == 0:
            block = block + base[:, 768:1536]
        if y == 15:
            block = block + base[:, 1536:]
        w1[r * 32:r * 32 + 32, :] = block[:, :720].astype(BF16)
    bias1[...] = jnp.zeros_like(bias1)
    bias1[:, 0:32] = jnp.broadcast_to(b1r[...], (128, 32))
    b1 = jnp.transpose(bias1[...])[:32]
    b1 = jnp.concatenate([b1, b1], axis=1)
    spread = dot(own, depth_map[...]).astype(BF16)
    for x in range(8):
        for t in range(3):
            xs[x + 1, t * 80:t * 80 + 64] = spread[x * 64:x * 64 + 64, t * 256:t * 256 + 256]
    finish_all(first)
    sides = [jnp.where(left, hlr[0:32].astype(F32), 0.0), jnp.where(right, hlr[32:64].astype(F32), 0.0)]
    for a, ok in ((0, up), (1, down)):
        for b, ok2 in ((0, left), (1, right)):
            sides.append(jnp.where(jnp.logical_and(ok, ok2), hc[a, b].astype(F32), 0.0))
    rims = dot(expand[...], jnp.concatenate(sides, axis=0).astype(BF16))
    blocks = [rims[:128]]
    for a, ok in ((0, up), (1, down)):
        rows = [hx[a, n].reshape(64, 128) for n in range(2)]
        blocks.append(jnp.where(ok, jnp.concatenate(rows, axis=1).astype(F32), 0.0))
        blocks.append(rims[128 + a * 16:144 + a * 16])
    spread = dot(jnp.concatenate(blocks, axis=0).astype(BF16), depth_map[...]).astype(BF16)
    pieces = [(x + 1, 64, x * 16, 16) for x in range(8)]
    pieces += [(0, 0, 128, 64), (0, 64, 192, 16), (9, 0, 208, 64), (9, 64, 272, 16)]
    for index, row, at_row, size in pieces:
        for t in range(3):
            xs[index, t * 80 + row:t * 80 + row + size] = spread[at_row:at_row + size, t * 256:t * 256 + 256]

    b1all = jnp.concatenate([b1] * 16, axis=0)

    def layer1(j):
        total = None
        for px in range(2):
            x = 2 * j + px
            pre = dot(w1[...], xs[x:x + 3].reshape(720, 256)) + b1all
            t = jnp.tanh(0.5 * pre)
            value = pre * (0.65 + 0.35 * t)
            sl[x] = 0.65 + 0.35 * t + 0.175 * pre * (1.0 - t * t)
            value = value[:256] + value[256:]
            value = value[:, :128] + value[:, 128:]
            total = value if total is None else total + value
        pool[j + 1, 1, 32:288] = (total * 0.125).astype(BF16)

    second = []
    for k, (sx, sy) in enumerate(DIRS):
        src_x, dst_x = {0: (pl.ds(1, 4),) * 2, 1: (4, 0), -1: (1, 5)}[sx]
        src_y, dst_y = {0: (pl.ds(32, 256),) * 2, 1: (pl.ds(256, 32), pl.ds(0, 32)), -1: (pl.ds(32, 32), pl.ds(288, 32))}[sy]
        second.append(remote(pool.at[src_x, 1, src_y], pool.at[dst_x, 1, dst_y], 8 + k, at(sx, sy)))
    layer1(0)
    layer1(3)
    start(second, (1, -1))
    layer1(1)
    layer1(2)
    start(second, (0,))

    for load in loads[9:]:
        load.wait()
    w2[...] = dot_nt(eye[:64, :64], w2t[...]).astype(BF16)
    for dx in range(3):
        for dy in range(3):
            at_lane = ((2 - dx) * 3 + 2 - dy) * 64
            row = (dx * 3 + dy) * 96
            w2b[:, at_lane:at_lane + 64] = w2t[row:row + 96, :]
    bias2[...] = jnp.zeros_like(bias2)
    bias2[:, 0:64] = jnp.broadcast_to(b2r[...], (128, 64))
    b2 = jnp.transpose(bias2[...])[:64]
    b2 = jnp.concatenate([b2, b2], axis=1)
    for i in range(1, 5):
        spread = dot(pool[i, 1, 32:288], pool_map[...]).astype(BF16)
        pool[i, 0, 32:288] = spread[:, :128]
        pool[i, 2, 32:288] = spread[:, 128:]
    none = jnp.zeros((32, 128), BF16)

    def piece(i, dz, r):
        return none if i in (0, 5) or r in (0, 9) else pool[i, dz, r * 32:r * 32 + 32]

    def pair(i, dz, r):
        return jnp.concatenate([piece(i, dz, r), piece(i + 2, dz, r)], axis=1)

    for j in range(2):
        for y in range(8):
            patch = jnp.concatenate(
                [pair(j + dx, dz, y + dy) for dx in range(3) for dy in range(3) for dz in range(3)], axis=0)
            pre2[j, y] = dot(w2[...], patch) + b2

    for q in range(4):
        part = jnp.concatenate(
            [cot[(n * 8 + h * 4 + q) * 32:(n * 8 + h * 4 + q) * 32 + 32, :] for n in range(2) for h in range(2)], axis=0
        )
        turned = dot_nt(eye[:64, :64], part).astype(BF16)
        cots[q * 64:q * 64 + 64] = dot(turned, cot_map[...]) * 0.125

    acc2[...] = jnp.zeros_like(acc2)
    for i in (0, 5):
        gs[i] = jnp.zeros((768, 128), BF16)
    for i in range(1, 5):
        gs[i, 0:128] = jnp.zeros((128, 128), BF16)
        gs[i, 640:768] = jnp.zeros((128, 128), BF16)
    for i, picked in enumerate((
        [(0, dy) for dy in range(3)], [(2, dy) for dy in range(3)], [(dx, 0) for dx in range(3)], [(dx, 2) for dx in range(3)]
    )):
        rows = [w2t[(dx * 3 + dy) * 96:(dx * 3 + dy) * 96 + 96, :] for dx, dy in picked]
        w2e[i] = dot_nt(eye[:64, :64], jnp.concatenate(rows, axis=0)).astype(BF16)
    finish_all(second)
    for ok, index in ((up, 0), (down, 5)):
        @pl.when(jnp.logical_not(ok))
        def _(index=index):
            pool[index, 1] = jnp.zeros((320, 128), BF16)
    for ok, index in ((left, 0), (right, 288)):
        @pl.when(jnp.logical_not(ok))
        def _(index=index):
            pool[:, 1, index:index + 32] = jnp.zeros((6, 32, 128), BF16)

    for i in (0, 5):
        spread = dot(pool[i, 1], pool_map[...]).astype(BF16)
        pool[i, 0] = spread[:, :128]
        pool[i, 2] = spread[:, 128:]
    rims = [(i, r) for i in range(1, 5) for r in (0, 288)]
    spread = dot(jnp.concatenate([pool[i, 1, r:r + 32] for i, r in rims], axis=0), pool_map[...]).astype(BF16)
    for q, (i, r) in enumerate(rims):
        pool[i, 0, r:r + 32] = spread[q * 32:q * 32 + 32, :128]
        pool[i, 2, r:r + 32] = spread[q * 32:q * 32 + 32, 128:]
    for side, i in ((0, 0), (1, 5)):
        for y in range(4):
            patch = jnp.concatenate(
                [jnp.concatenate([pool[i, dz, (q + dy) * 32:(q + dy) * 32 + 32] for q in (y, y + 4)], axis=1)
                 for dy in range(3) for dz in range(3)], axis=0)
            term = dot(w2e[side], patch)
            lanes = slice(side * 128, side * 128 + 128)
            pre2[side, y, :, lanes] += term[:, :128]
            pre2[side, y + 4, :, lanes] += term[:, 128:]
    for side, y, r in ((2, 0, 0), (3, 7, 288)):
        for j in range(2):
            patch = jnp.concatenate(
                [jnp.concatenate([none if i in (0, 5) else pool[i, dz, r:r + 32] for i in (j + dx, j + dx + 2)], axis=1)
                 for dx in range(3) for dz in range(3)], axis=0)
            pre2[j, y] += dot(w2e[side], patch)
    for j in range(2):
        for y in range(8):
            pre = pre2[j, y]
            t = jnp.tanh(0.5 * pre)
            slope = 0.65 + 0.35 * t + 0.175 * pre * (1.0 - t * t)
            grad = (slope * cots[(y // 2) * 64:(y // 2) * 64 + 64, :]).astype(BF16)
            gs[j + 1, (y + 2) * 64:(y + 3) * 64] = grad[:, :128]
            gs[j + 3, (y + 2) * 64:(y + 3) * 64] = grad[:, 128:]

    def depth_terms(part):
        return part[32:64] + before2(part[64:96]) + after2(part[0:32])

    for side, i, u in ((0, 1, 2), (1, 4, 0)):
        for y in range(5):
            patch = jnp.concatenate([gs[i, q * 64:q * 64 + 192] for q in (y, y + 5)], axis=1)
            terms = dot(w2b[:, u * 192:u * 192 + 192], patch) * 0.125
            xe[side, y * 32:y * 32 + 32] = depth_terms(terms[:, :128]).astype(BF16)
            xe[side, (y + 5) * 32:(y + 6) * 32] = depth_terms(terms[:, 128:]).astype(BF16)

    def back2(j, y):
        patch = jnp.concatenate(
            [jnp.concatenate([gs[i, (y + 1) * 64:(y + 4) * 64] for i in (j + u, j + u + 2)], axis=1) for u in range(3)],
            axis=0)
        terms = dot(w2b[...], patch) * 0.125
        return depth_terms(terms[:, :128]), depth_terms(terms[:, 128:])

    for side, y in ((0, -1), (1, 8)):
        for j in range(2):
            one, two = back2(j, y)
            ye[side, j] = one.astype(BF16)
            ye[side, j + 2] = two.astype(BF16)
    third = []
    for k, (sx, sy) in enumerate(DIRS):
        a, b = (0 if sx == 1 else 1), (0 if sy == 1 else 1)
        if sx == 0:
            src, dst = ye.at[1 - b], rye.at[b]
        elif sy == 0:
            src, dst = xe.at[1 - a, pl.ds(32, 256)], rxe.at[a]
        else:
            src, dst = xe.at[1 - a, pl.ds(288 if sy == 1 else 0, 32)], rce.at[a, b]
        third.append(remote(src, dst, 16 + k, at(sx, sy)))
    start(third, (1, -1, 0))

    def cell(ref, i, where, start, size):
        rows = slice(start, start + size)
        return jnp.concatenate([ref[(i,) + where + (rows,)], ref[(i + 2,) + where + (rows,)]], axis=1)

    for j in range(2):
        for y in range(8):
            grad = cell(gs, j + 1, (), (y + 2) * 64, 64)
            for half in range(2):
                patch = jnp.concatenate(
                    [cell(pool, j + dx, (dz,), (y + dy) * 32 + half * 16, 16)
                     for dx in range(3) for dy in range(3) for dz in range(3)], axis=0)
                acc2[half, :, 0:432] += dot_nt(grad, patch)
    pair2 = remote(acc2.at[1 - dp], r2dp, 24, (gx, gy, 1 - dp))
    pair2.start()
    for j in range(2):
        for y in range(8):
            one, two = back2(j, y)
            gp[j, y * 32:y * 32 + 32] = one
            gp[j + 2, y * 32:y * 32 + 32] = two
    for b in range(6):
        width = min(128, 720 - b * 128)
        w1tr[b * 128:b * 128 + width] = dot_nt(eye[:width, :width], w1[:, b * 128:b * 128 + width]).astype(BF16)
    finish_all(third)

    for a, ok, i in ((0, up, 0), (1, down, 3)):
        gp[i] += jnp.where(ok, rxe[a].astype(F32), 0.0)
        for b, ok2, r in ((0, left, 0), (1, right, 224)):
            gp[i, r:r + 32] += jnp.where(jnp.logical_and(ok, ok2), rce[a, b].astype(F32), 0.0)
    for b, ok, r in ((0, left, 0), (1, right, 224)):
        for i in range(4):
            gp[i, r:r + 32] += jnp.where(ok, rye[b, i].astype(F32), 0.0)

    pair2.wait()
    s2a[...] = (acc2[dp] + r2dp[...]).reshape(gxn, 8, 512)
    along2 = []
    for d in range(1, gxn):
        along2.append(remote(s2a.at[lax.rem(gx + d, gxn)], r2gx.at[d - 1], 24 + d, at(d, 0)))
        along2[-1].start()

    for x in range(8):
        spread = gp[x // 2]
        spread = jnp.concatenate([spread, spread], axis=1)
        spread = jnp.concatenate([spread, spread], axis=0)
        gf[x] = (sl[x] * spread).astype(BF16)
    for x in range(8):
        term = dot_nt(gf[x], xs[x:x + 3].reshape(720, 256))
        acc1[...] = term if x == 0 else acc1[...] + term

    taps = None
    for dy in range(3):
        kept = None
        for r in range(16):
            y = 2 * (r % 8) + r // 8
            term = jnp.where(place[:, :720] == float(y + dy - 1), acc1[r * 32:r * 32 + 32], 0.0)
            kept = term if kept is None else kept + term
        parts = split_dot(kept, gather[...])
        if dy:
            parts = pltpu.roll(parts, 3 * dy, 1)
        taps = parts if taps is None else taps + parts
    for g in range(8):
        s1[g] = taps[4 * g:4 * g + 4]
    along1 = []
    for d in range(gxn):
        for e in range(2):
            if d + e:
                peer = (lax.rem(gx + d, gxn), gy, lax.rem(dp + e, 2))
                along1.append(remote(s1.at[peer[0]], r1gx.at[2 * d + e - 1], 47 + 2 * d + e, peer))
                along1[-1].start()

    for x in range(8):
        term = dot(w1tr[...], gf[x]).reshape(3, 240, 256)
        if x == 0:
            gi[0:3] = term
        else:
            gi[x:x + 2] += term[:2]
            gi[x + 2] = term[2]

    def combine(x):
        return gi[x, 80:152] + before(gi[x, 160:232]) + after(gi[x, 0:72])

    for i, x in ((0, 0), (1, 9)):
        edge = combine(x)
        sx_[i] = edge[:64].astype(BF16)
        sc[i] = jnp.concatenate([edge[64:], edge[64:]], axis=0).astype(BF16)
    outer = []
    for x in range(8):
        inner = combine(x + 1)
        gi[x + 1, 80:144] = inner[:64]
        outer.append(inner[64:])
    sby[...] = dot(regroup[...], jnp.concatenate(outer, axis=0).astype(BF16)).astype(BF16)
    fourth = []
    for k, (sx, sy) in enumerate(DIRS):
        a, b = (0 if sx == 1 else 1), (0 if sy == 1 else 1)
        if sx == 0:
            src, dst = sby.at[pl.ds(32 - b * 32, 32)], ry.at[pl.ds(32 - b * 32, 32)]
        elif sy == 0:
            src, dst = sx_.at[1 if sx == 1 else 0], rx.at[a]
        else:
            src, dst = sc.at[1 if sx == 1 else 0], rc.at[a, b]
        fourth.append(remote(src, dst, 40 + k, at(sx, sy)))
    start(fourth, (1, -1, 0))
    for copy in along1:
        copy.wait()
    total1 = s1[gx]
    for i in range(2 * gxn - 1):
        total1 = total1 + r1gx[i]
    s1b[...] = total1
    across1 = []
    for d in range(1, gyn):
        across1.append(remote(s1b, r1gy.at[d - 1], 62 + d, at(0, d)))
        across1[-1].start()
    for copy in along2:
        copy.wait()
    total2 = s2a[gx]
    for d in range(1, gxn):
        total2 = total2 + r2gx[d - 1]
    for g in range(8):
        s2b[g] = total2[g:g + 1]
    across2 = []
    for d in range(1, gyn):
        across2.append(remote(s2b.at[lax.rem(gy + d, gyn)], r2gy.at[d - 1], 31 + d, at(0, d)))
        across2[-1].start()
    finish_all(fourth)
    y16 = lax.broadcasted_iota(jnp.int32, (4, 16, 256), 1)

    def ends(low_rows, high_rows):
        low_part = jnp.where(jnp.logical_and(y16 == 0, left), low_rows[4:8][:, None, :], 0.0)
        high_part = jnp.where(jnp.logical_and(y16 == 15, right), high_rows[0:4][:, None, :], 0.0)
        return (low_part + high_part).reshape(64, 256)

    for a, ok, x in ((0, up, 1), (1, down, 8)):
        term = rx[a].astype(F32) + ends(rc[a, 0].astype(F32), rc[a, 1].astype(F32))
        gi[x, 80:144] += jnp.where(ok, term, 0.0)
    sides = [jnp.where(right, ry[0:32].astype(F32), 0.0), jnp.where(left, ry[32:64].astype(F32), 0.0)]
    extra = dot(scatter[...], jnp.concatenate(sides, axis=0).astype(BF16))
    for x in range(8):
        out[x] = (gi[x + 1, 80:144] + extra[x * 64:x * 64 + 64]).astype(BF16)

    for copy in across2:
        copy.wait()
    total2 = s2b[gy]
    for d in range(1, gyn):
        total2 = total2 + r2gy[d - 1]
    total2 = jnp.concatenate([total2 * (1.0 / (CELLS / 8) ** 0.5)] * 8, axis=0)[:, :432]
    gw2[...] = split_dot(total2, reorder[...])[0:1]
    for copy in across1:
        copy.wait()
    total1 = s1b[...]
    for d in range(1, gyn):
        total1 = total1 + r1gy[d - 1]
    mine = None
    for q in range(4):
        for c in range(4):
            ok = jnp.logical_and(gy // 2 == q, (gy % 2) * 2 + dp == c)
            term = jnp.where(ok, total1[q:q + 1, c * 32:c * 32 + 32], 0.0)
            mine = term if mine is None else mine + term
    gw1[...] = mine[:, 0:27] * (1.0 / CELLS ** 0.5)


def write_back(total, restore, part1, part2, out, gw1, gw2):
    natural = dot(total[...].reshape(512, 256), restore[...]).astype(BF16)
    for x in range(8):
        for n in range(2):
            out[n, :, x] = natural[x * 64:x * 64 + 64, n * 128:n * 128 + 128].reshape(4, 16, 128)
    gw1[...] = part1[...]
    gw2[...] = part2[...]


def on_device(gxn, gyn, consts, inputs, cotangent, w_first, w_second, b_first, b_second):
    cot = jnp.transpose(cotangent, (0, 2, 3, 4, 1)).reshape(512, 64)
    w1t = jnp.transpose(w_first, (2, 3, 4, 1, 0)).reshape(27, 4, 32)
    w2t = jnp.transpose(w_second, (2, 3, 4, 1, 0)).reshape(864, 64)
    vmem = pl.BlockSpec(memory_space=pltpu.VMEM)
    b1, b2 = b_first.reshape(1, 32), b_second.reshape(1, 64)
    c = {name: jnp.asarray(value) for name, value in consts.items()}
    operands = (
        inputs, c["select"], w1t, c["eye"], c["toeplitz"], c["place"], c["depth_map"], b1, c["expand"], w2t, cot, b2,
        c["pool_map"], c["cot_map"], c["gather"], c["reorder"], c["regroup"], c["scatter"],
    )
    scratch = [
        ((10, 240, 256), BF16), ((64, 256), BF16), ((64, 256), BF16), ((2, 2, 4, 16, 128), BF16),
        ((2, 2, 16, 256), BF16), ((512, 720), BF16), ((720, 512), BF16), ((64, 864), BF16), ((96, 576), BF16),
        ((128, 128), F32), ((128, 128), F32), ((8, 512, 256), F32), ((8, 512, 256), BF16), ((6, 3, 320, 128), BF16),
        ((256, 256), F32), ((6, 768, 128), BF16), ((4, 256, 128), F32),
        ((2, 64, 512), F32), ((64, 512), F32), ((gxn, 8, 512), F32), ((gxn - 1, 8, 512), F32), ((gyn, 1, 512), F32),
        ((gyn - 1, 1, 512), F32), ((10, 240, 256), F32), ((64, 256), BF16), ((64, 256), BF16),
        ((2, 64, 256), BF16), ((2, 64, 256), BF16), ((2, 16, 256), BF16), ((2, 2, 16, 256), BF16), ((512, 720), F32),
        ((gxn, 4, 128), F32), ((2 * gxn - 1, 4, 128), F32), ((4, 128), F32),
        ((gyn - 1, 4, 128), F32), ((128, 32), F32), ((4, 64, 288), BF16), ((2, 8, 64, 256), F32),
        ((2, 320, 128), BF16), ((2, 4, 32, 128), BF16), ((2, 256, 128), BF16), ((2, 4, 32, 128), BF16),
        ((2, 2, 32, 128), BF16),
    ]
    total, part1, part2 = pl.pallas_call(
        functools.partial(kernel, gxn, gyn),
        out_shape=(
            jax.ShapeDtypeStruct((8, 64, 256), BF16),
            jax.ShapeDtypeStruct((1, 27), F32),
            jax.ShapeDtypeStruct((1, 432), F32),
        ),
        in_specs=[pl.BlockSpec(memory_space=pl.ANY)] * NLOAD,
        out_specs=(vmem, vmem, vmem),
        scratch_shapes=[pltpu.VMEM(v.shape, v.dtype) for v in operands]
        + [pltpu.VMEM(s, d) for s, d in scratch]
        + [pltpu.SemaphoreType.DMA((70,)), pltpu.SemaphoreType.DMA((70,)), pltpu.SemaphoreType.DMA((NLOAD,))],
        compiler_params=pltpu.CompilerParams(
            collective_id=0, has_side_effects=True, vmem_limit_bytes=60 * 1024 * 1024
        ),
    )(*operands)
    result, part1, part2 = pl.pallas_call(
        write_back,
        out_shape=(
            jax.ShapeDtypeStruct(inputs.shape, BF16),
            jax.ShapeDtypeStruct((1, 27), F32),
            jax.ShapeDtypeStruct((1, 432), F32),
        ),
        in_specs=[vmem] * 4,
        out_specs=(vmem, vmem, vmem),
    )(total, c["restore"], part1, part2)
    return result, part1.reshape(27), part2.reshape(432)


def solution(mesh):
    consts = constants()
    return jax.shard_map(
        functools.partial(on_device, mesh.shape["gx"], mesh.shape["gy"], consts),
        mesh=mesh,
        in_specs=(P("dp", None, "gx", "gy", None), P("dp", None, "gx", "gy", None), P(), P(), P(), P()),
        out_specs=(P("dp", None, "gx", "gy", None), P(("gx", "gy", "dp")), P(("gx", "gy", "dp"))),
        check_vma=False,
    )
```

```python
import functools

import jax
import jax.numpy as jnp
import ml_dtypes
import numpy as np
from jax import lax
from jax.experimental import pallas as pl
from jax.experimental.pallas import tpu as pltpu
from jax.sharding import PartitionSpec as P

MESH = pl.DeviceIdType.MESH
F32 = jnp.float32
BF16 = jnp.bfloat16
DIRS = [(0, 1), (0, -1), (1, 0), (-1, 0), (1, 1), (1, -1), (-1, 1), (-1, -1)]
CELLS = 4194304
NLOAD = 18


def constants():
    depth_map = np.zeros((256, 768), np.float32)
    for n in range(2):
        for z in range(128):
            lane = (z % 2) * 128 + (z // 2 % 2) * 64 + n * 32 + z // 4
            for t in range(3):
                src = z + t - 1
                if 0 <= src < 128:
                    depth_map[n * 128 + src, t * 256 + lane] = 1
    restore = depth_map[:, 256:512].T.copy()
    pool_map = np.zeros((128, 256), np.float32)
    for n in range(2):
        for z in range(64):
            lane = (z % 2) * 64 + n * 32 + z // 2
            for half, src in ((0, z - 1), (1, z + 1)):
                if 0 <= src < 64:
                    pool_map[(src % 2) * 64 + n * 32 + src // 2, half * 128 + lane] = 1
    cot_map = np.zeros((128, 256), np.float32)
    for h in range(2):
        for b in range(2):
            for n in range(2):
                for k in range(32):
                    cot_map[n * 64 + h * 32 + k, h * 128 + b * 64 + n * 32 + k] = 1
    place = np.full((80,), -100.0, np.float32)
    chan = np.full((80,), -1)
    for c in range(4):
        for y in range(-1, 17):
            row = 64 + c if y < 0 else 68 + c if y > 15 else c * 16 + y
            place[row] = y
            chan[row] = c
    toeplitz = np.zeros((128, 3 * 768), np.float32)
    gather = np.zeros((720, 128), np.float32)
    for dx in range(3):
        for dz in range(3):
            group = dx * 240 + dz * 80
            for c in range(4):
                for dy in range(3):
                    toeplitz[((dx * 3 + dy) * 3 + dz) * 4 + c, (group + c * 16 + dy - 1) % 768] = 1
                toeplitz[((dx * 3 + 0) * 3 + dz) * 4 + c, 768 + group + 64 + c] = 1
                toeplitz[((dx * 3 + 2) * 3 + dz) * 4 + c, 1536 + group + 68 + c] = 1
            for row in range(72):
                gather[group + row, chan[row] * 32 + dx * 9 + dz] = 1
    reorder = np.zeros((432, 432), np.float32)
    for tap in range(27):
        for c in range(16):
            reorder[tap * 16 + c, c * 27 + tap] = 1
    select = np.zeros((64, 512), np.float32)
    regroup = np.zeros((64, 64), np.float32)
    expand = np.zeros((160, 128), np.float32)
    for x in range(8):
        for c in range(4):
            select[x * 4 + c, x * 64 + c * 16 + 15] = 1
            select[32 + x * 4 + c, x * 64 + c * 16] = 1
            for side in range(2):
                regroup[side * 32 + x * 4 + c, x * 8 + side * 4 + c] = 1
                expand[x * 16 + side * 4 + c, side * 32 + x * 4 + c] = 1
    for a in range(2):
        for side in range(2):
            for c in range(4):
                expand[128 + a * 16 + side * 4 + c, 64 + a * 32 + side * 16 + (12 if a == 0 else 0) + c] = 1
    b16 = lambda v: v.astype(ml_dtypes.bfloat16)
    place = np.pad(np.tile(place, 9), (0, 48), constant_values=-100)[None, :]
    return {
        "depth_map": b16(depth_map), "restore": b16(restore), "pool_map": b16(pool_map), "cot_map": b16(cot_map),
        "toeplitz": b16(toeplitz), "gather": b16(gather), "select": b16(select), "reorder": b16(reorder),
        "scatter": b16(select.T.copy()), "regroup": b16(regroup), "expand": b16(expand),
        "eye": b16(np.eye(128, dtype=np.float32)), "place": place,
    }


def dot(a, b):
    return jnp.dot(a, b, preferred_element_type=F32)


def dot_nt(a, b):
    return lax.dot_general(a, b, (((1,), (1,)), ((), ())), preferred_element_type=F32)


def split_dot(a, b):
    high = a.astype(BF16)
    rest = a - high.astype(F32)
    mid = rest.astype(BF16)
    low = (rest - mid.astype(F32)).astype(BF16)
    parts = dot(jnp.concatenate([high.astype(F32), mid.astype(F32), low.astype(F32)], axis=0).astype(BF16), b)
    rows = a.shape[0]
    return parts[:rows] + parts[rows:2 * rows] + parts[2 * rows:]


def before2(u):
    lane = lax.broadcasted_iota(jnp.int32, u.shape, 1)
    return jnp.where(
        lane < 64, jnp.where(lane % 32 != 0, pltpu.roll(u, 65, 1), 0.0), pltpu.roll(u, 64, 1)
    )


def after2(u):
    lane = lax.broadcasted_iota(jnp.int32, u.shape, 1)
    return jnp.where(
        lane >= 64, jnp.where(lane % 32 != 31, pltpu.roll(u, 63, 1), 0.0), pltpu.roll(u, 64, 1)
    )


def before(v):
    return jnp.concatenate([before2(v[:, 128:]), v[:, :128]], axis=1)


def after(v):
    return jnp.concatenate([v[:, 128:], after2(v[:, :128])], axis=1)


def kernel(
    gxn, gyn,
    *rest):
    fixed, rest = rest[:NLOAD], rest[NLOAD:]
    out, gw1, gw2 = rest[:3]
    kept, rest = rest[3:3 + NLOAD], rest[3 + NLOAD:]
    (xs, hb, hlr, hx, hc, w1, w1tr, w2, w2b, bias1, bias2, sl, gf, pool, cots, gs, gp,
    acc2, r2dp, s2a, r2gx, s2b, r2gy, gi, sby, ry, sx_, rx, sc, rc, acc1, s1, r1gx, s1b, r1gy,
    w1f, w2e, pre2, xe, ye, rxe, rye, rce, ssem, rsem, lsem) = rest
    inp, select, w1t, eye, toeplitz, place, depth_map, b1r, expand, w2t, cot, b2r, pool_map, cot_map, *others = kept
    gather, reorder, regroup, scatter = others
    loads = [pltpu.make_async_copy(fixed[i], kept[i], lsem.at[i]) for i in range(NLOAD)]
    for load in loads[:2]:
        load.start()
    gx, gy, dp = lax.axis_index("gx"), lax.axis_index("gy"), lax.axis_index("dp")

    def at(sx, sy):
        return (lax.rem(gx + sx + gxn, gxn), lax.rem(gy + sy + gyn, gyn), dp)

    def remote(src, dst, k, device):
        return pltpu.make_async_remote_copy(
            src_ref=src, dst_ref=dst, send_sem=ssem.at[k], recv_sem=rsem.at[k], device_id=device, device_id_type=MESH
        )

    left, right = gy > 0, gy < gyn - 1
    up, down = gx > 0, gx < gxn - 1

    def start(copies, which):
        for sx in which:
            picked = [c for c, d in zip(copies, DIRS) if d[0] == sx]
            if sx == 0:
                for copy in picked:
                    copy.start()
            else:
                @pl.when(down if sx == 1 else up)
                def _(picked=picked):
                    for copy in picked:
                        copy.start()

    def finish_all(copies):
        by = {sx: [c for c, d in zip(copies, DIRS) if d[0] == sx] for sx in (0, 1, -1)}
        for sx in (1, -1):
            @pl.when(down if sx == 1 else up)
            def _(sx=sx):
                for copy in by[sx]:
                    copy.wait_send()
                for copy in by[-sx]:
                    copy.wait_recv()
        for copy in by[0]:
            copy.wait()

    barrier = pltpu.get_barrier_semaphore()
    peers = [at(*d) for d in DIRS]
    peers += [at(d, 0) for d in range(2, gxn - 1)] + [at(0, d) for d in range(2, gyn - 1)]
    peers += [(lax.rem(gx + d, gxn), gy, 1 - dp) for d in range(gxn)]
    for peer in peers:
        pl.semaphore_signal(barrier, inc=1, device_id=peer, device_id_type=MESH)
    for load in loads[2:]:
        load.start()

    def raw(x):
        halves = [inp[n, :, x].reshape(64, 128) for n in range(2)]
        return jnp.concatenate(halves, axis=1)

    pl.semaphore_wait(barrier, len(peers))
    faces = []
    for k, sx in ((2, 1), (3, -1)):
        faces.append(remote(fixed[0].at[:, :, 7 if sx == 1 else 0], hx.at[0 if sx == 1 else 1], k, at(sx, 0)))
    for copy, ok in zip(faces, (down, up)):
        @pl.when(ok)
        def _(copy=copy):
            copy.start()
    loads[0].wait()
    loads[1].wait()
    own = jnp.concatenate([raw(x) for x in range(8)], axis=0)
    hb[...] = dot(select[...], own).astype(BF16)
    first = []
    for k, (sx, sy) in enumerate(DIRS):
        a, b = (0 if sx == 1 else 1), (0 if sy == 1 else 1)
        if sx == 0:
            src, dst = hb.at[pl.ds(b * 32, 32)], hlr.at[pl.ds(b * 32, 32)]
        elif sy == 0:
            first.append(faces[a])
            continue
        else:
            src, dst = hb.at[pl.ds(b * 32 + 16 - a * 16, 16)], hc.at[a, b]
        first.append(remote(src, dst, k, at(sx, sy)))
    start(first, (0,))
    for sx, ok in ((1, down), (-1, up)):
        @pl.when(ok)
        def _(sx=sx):
            for copy, d in zip(first, DIRS):
                if d[0] == sx and d[1]:
                    copy.start()

    for load in loads[2:9]:
        load.wait()
    w1f[...] = jnp.zeros_like(w1f)
    for tap in range(27):
        w1f[tap * 4:tap * 4 + 4] = w1t[tap].astype(F32)
    small = dot_nt(eye[:32, :32], w1f[...].astype(BF16)).astype(BF16)
    base = dot(small, toeplitz[...])
    for r in range(16):
        y = 2 * (r % 8) + r // 8
        block = base[:, :768] if y == 0 else pltpu.roll(base[:, :768], y, 1)
        block = jnp.where(jnp.abs(place[...] - float(y)) < 1.5, block, 0.0)
        if y == 0:
            block = block + base[:, 768:1536]
        if y == 15:
            block = block + base[:, 1536:]
        w1[r * 32:r * 32 + 32, :] = block[:, :720].astype(BF16)
    bias1[...] = jnp.zeros_like(bias1)
    bias1[:, 0:32] = jnp.broadcast_to(b1r[...], (128, 32))
    b1 = jnp.transpose(bias1[...])[:32]
    b1 = jnp.concatenate([b1, b1], axis=1)
    spread = dot(own, depth_map[...]).astype(BF16)
    for x in range(8):
        for t in range(3):
            xs[x + 1, t * 80:t * 80 + 64] = spread[x * 64:x * 64 + 64, t * 256:t * 256 + 256]
    finish_all(first)
    sides = [jnp.where(left, hlr[0:32].astype(F32), 0.0), jnp.where(right, hlr[32:64].astype(F32), 0.0)]
    for a, ok in ((0, up), (1, down)):
        for b, ok2 in ((0, left), (1, right)):
            sides.append(jnp.where(jnp.logical_and(ok, ok2), hc[a, b].astype(F32), 0.0))
    rims = dot(expand[...], jnp.concatenate(sides, axis=0).astype(BF16))
    blocks = [rims[:128]]
    for a, ok in ((0, up), (1, down)):
        rows = [hx[a, n].reshape(64, 128) for n in range(2)]
        blocks.append(jnp.where(ok, jnp.concatenate(rows, axis=1).astype(F32), 0.0))
        blocks.append(rims[128 + a * 16:144 + a * 16])
    spread = dot(jnp.concatenate(blocks, axis=0).astype(BF16), depth_map[...]).astype(BF16)
    pieces = [(x + 1, 64, x * 16, 16) for x in range(8)]
    pieces += [(0, 0, 128, 64), (0, 64, 192, 16), (9, 0, 208, 64), (9, 64, 272, 16)]
    for index, row, at_row, size in pieces:
        for t in range(3):
            xs[index, t * 80 + row:t * 80 + row + size] = spread[at_row:at_row + size, t * 256:t * 256 + 256]

    b1all = jnp.concatenate([b1] * 16, axis=0)

    def layer1(j):
        total = None
        for px in range(2):
            x = 2 * j + px
            pre = dot(w1[...], xs[x:x + 3].reshape(720, 256)) + b1all
            t = jnp.tanh(0.5 * pre)
            value = pre * (0.65 + 0.35 * t)
            sl[x] = 0.65 + 0.35 * t + 0.175 * pre * (1.0 - t * t)
            value = value[:256] + value[256:]
            value = value[:, :128] + value[:, 128:]
            total = value if total is None else total + value
        pool[j + 1, 1, 32:288] = (total * 0.125).astype(BF16)

    second = []
    for k, (sx, sy) in enumerate(DIRS):
        src_x, dst_x = {0: (pl.ds(1, 4),) * 2, 1: (4, 0), -1: (1, 5)}[sx]
        src_y, dst_y = {0: (pl.ds(32, 256),) * 2, 1: (pl.ds(256, 32), pl.ds(0, 32)), -1: (pl.ds(32, 32), pl.ds(288, 32))}[sy]
        second.append(remote(pool.at[src_x, 1, src_y], pool.at[dst_x, 1, dst_y], 8 + k, at(sx, sy)))
    layer1(0)
    layer1(3)
    start(second, (1, -1))
    layer1(1)
    layer1(2)
    start(second, (0,))

    for load in loads[9:]:
        load.wait()
    w2[...] = dot_nt(eye[:64, :64], w2t[...]).astype(BF16)
    for dx in range(3):
        for dy in range(3):
            at_lane = ((2 - dx) * 3 + 2 - dy) * 64
            row = (dx * 3 + dy) * 96
            w2b[:, at_lane:at_lane + 64] = w2t[row:row + 96, :]
    bias2[...] = jnp.zeros_like(bias2)
    bias2[:, 0:64] = jnp.broadcast_to(b2r[...], (128, 64))
    b2 = jnp.transpose(bias2[...])[:64]
    b2 = jnp.concatenate([b2, b2], axis=1)
    for i in range(1, 5):
        spread = dot(pool[i, 1, 32:288], pool_map[...]).astype(BF16)
        pool[i, 0, 32:288] = spread[:, :128]
        pool[i, 2, 32:288] = spread[:, 128:]
    none = jnp.zeros((32, 128), BF16)

    def piece(i, dz, r):
        return none if i in (0, 5) or r in (0, 9) else pool[i, dz, r * 32:r * 32 + 32]

    def pair(i, dz, r):
        return jnp.concatenate([piece(i, dz, r), piece(i + 2, dz, r)], axis=1)

    for j in range(2):
        for y in range(8):
            patch = jnp.concatenate(
                [pair(j + dx, dz, y + dy) for dx in range(3) for dy in range(3) for dz in range(3)], axis=0)
            pre2[j, y] = dot(w2[...], patch) + b2

    for q in range(4):
        part = jnp.concatenate(
            [cot[(n * 8 + h * 4 + q) * 32:(n * 8 + h * 4 + q) * 32 + 32, :] for n in range(2) for h in range(2)], axis=0
        )
        turned = dot_nt(eye[:64, :64], part).astype(BF16)
        cots[q * 64:q * 64 + 64] = dot(turned, cot_map[...]) * 0.125

    acc2[...] = jnp.zeros_like(acc2)
    for i in (0, 5):
        gs[i] = jnp.zeros((768, 128), BF16)
    for i in range(1, 5):
        gs[i, 0:128] = jnp.zeros((128, 128), BF16)
        gs[i, 640:768] = jnp.zeros((128, 128), BF16)
    for i, picked in enumerate((
        [(0, dy) for dy in range(3)], [(2, dy) for dy in range(3)], [(dx, 0) for dx in range(3)], [(dx, 2) for dx in range(3)]
    )):
        rows = [w2t[(dx * 3 + dy) * 96:(dx * 3 + dy) * 96 + 96, :] for dx, dy in picked]
        w2e[i] = dot_nt(eye[:64, :64], jnp.concatenate(rows, axis=0)).astype(BF16)
    finish_all(second)
    for ok, index in ((up, 0), (down, 5)):
        @pl.when(jnp.logical_not(ok))
        def _(index=index):
            pool[index, 1] = jnp.zeros((320, 128), BF16)
    for ok, index in ((left, 0), (right, 288)):
        @pl.when(jnp.logical_not(ok))
        def _(index=index):
            pool[:, 1, index:index + 32] = jnp.zeros((6, 32, 128), BF16)

    for i in (0, 5):
        spread = dot(pool[i, 1], pool_map[...]).astype(BF16)
        pool[i, 0] = spread[:, :128]
        pool[i, 2] = spread[:, 128:]
    rims = [(i, r) for i in range(1, 5) for r in (0, 288)]
    spread = dot(jnp.concatenate([pool[i, 1, r:r + 32] for i, r in rims], axis=0), pool_map[...]).astype(BF16)
    for q, (i, r) in enumerate(rims):
        pool[i, 0, r:r + 32] = spread[q * 32:q * 32 + 32, :128]
        pool[i, 2, r:r + 32] = spread[q * 32:q * 32 + 32, 128:]
    for side, i in ((0, 0), (1, 5)):
        for y in range(4):
            patch = jnp.concatenate(
                [jnp.concatenate([pool[i, dz, (q + dy) * 32:(q + dy) * 32 + 32] for q in (y, y + 4)], axis=1)
                 for dy in range(3) for dz in range(3)], axis=0)
            term = dot(w2e[side], patch)
            lanes = slice(side * 128, side * 128 + 128)
            pre2[side, y, :, lanes] += term[:, :128]
            pre2[side, y + 4, :, lanes] += term[:, 128:]
    for side, y, r in ((2, 0, 0), (3, 7, 288)):
        for j in range(2):
            patch = jnp.concatenate(
                [jnp.concatenate([none if i in (0, 5) else pool[i, dz, r:r + 32] for i in (j + dx, j + dx + 2)], axis=1)
                 for dx in range(3) for dz in range(3)], axis=0)
            pre2[j, y] += dot(w2e[side], patch)
    for j in range(2):
        for y in range(8):
            pre = pre2[j, y]
            t = jnp.tanh(0.5 * pre)
            slope = 0.65 + 0.35 * t + 0.175 * pre * (1.0 - t * t)
            grad = (slope * cots[(y // 2) * 64:(y // 2) * 64 + 64, :]).astype(BF16)
            gs[j + 1, (y + 2) * 64:(y + 3) * 64] = grad[:, :128]
            gs[j + 3, (y + 2) * 64:(y + 3) * 64] = grad[:, 128:]

    def depth_terms(part):
        return part[32:64] + before2(part[64:96]) + after2(part[0:32])

    for side, i, u in ((0, 1, 2), (1, 4, 0)):
        for y in range(5):
            patch = jnp.concatenate([gs[i, q * 64:q * 64 + 192] for q in (y, y + 5)], axis=1)
            terms = dot(w2b[:, u * 192:u * 192 + 192], patch) * 0.125
            xe[side, y * 32:y * 32 + 32] = depth_terms(terms[:, :128]).astype(BF16)
            xe[side, (y + 5) * 32:(y + 6) * 32] = depth_terms(terms[:, 128:]).astype(BF16)

    def back2(j, y):
        patch = jnp.concatenate(
            [jnp.concatenate([gs[i, (y + 1) * 64:(y + 4) * 64] for i in (j + u, j + u + 2)], axis=1) for u in range(3)],
            axis=0)
        terms = dot(w2b[...], patch) * 0.125
        return depth_terms(terms[:, :128]), depth_terms(terms[:, 128:])

    for side, y in ((0, -1), (1, 8)):
        for j in range(2):
            one, two = back2(j, y)
            ye[side, j] = one.astype(BF16)
            ye[side, j + 2] = two.astype(BF16)
    third = []
    for k, (sx, sy) in enumerate(DIRS):
        a, b = (0 if sx == 1 else 1), (0 if sy == 1 else 1)
        if sx == 0:
            src, dst = ye.at[1 - b], rye.at[b]
        elif sy == 0:
            src, dst = xe.at[1 - a, pl.ds(32, 256)], rxe.at[a]
        else:
            src, dst = xe.at[1 - a, pl.ds(288 if sy == 1 else 0, 32)], rce.at[a, b]
        third.append(remote(src, dst, 16 + k, at(sx, sy)))
    start(third, (1, -1, 0))

    def cell(ref, i, where, start, size):
        rows = slice(start, start + size)
        return jnp.concatenate([ref[(i,) + where + (rows,)], ref[(i + 2,) + where + (rows,)]], axis=1)

    for j in range(2):
        for y in range(8):
            grad = cell(gs, j + 1, (), (y + 2) * 64, 64)
            for half in range(2):
                patch = jnp.concatenate(
                    [cell(pool, j + dx, (dz,), (y + dy) * 32 + half * 16, 16)
                     for dx in range(3) for dy in range(3) for dz in range(3)], axis=0)
                acc2[half, :, 0:432] += dot_nt(grad, patch)
    pair2 = remote(acc2.at[1 - dp], r2dp, 24, (gx, gy, 1 - dp))
    pair2.start()
    for j in range(2):
        for y in range(8):
            one, two = back2(j, y)
            gp[j, y * 32:y * 32 + 32] = one
            gp[j + 2, y * 32:y * 32 + 32] = two
    for b in range(6):
        width = min(128, 720 - b * 128)
        w1tr[b * 128:b * 128 + width] = dot_nt(eye[:width, :width], w1[:, b * 128:b * 128 + width]).astype(BF16)
    finish_all(third)

    for a, ok, i in ((0, up, 0), (1, down, 3)):
        gp[i] += jnp.where(ok, rxe[a].astype(F32), 0.0)
        for b, ok2, r in ((0, left, 0), (1, right, 224)):
            gp[i, r:r + 32] += jnp.where(jnp.logical_and(ok, ok2), rce[a, b].astype(F32), 0.0)
    for b, ok, r in ((0, left, 0), (1, right, 224)):
        for i in range(4):
            gp[i, r:r + 32] += jnp.where(ok, rye[b, i].astype(F32), 0.0)

    pair2.wait()
    s2a[...] = (acc2[dp] + r2dp[...]).reshape(gxn, 8, 512)
    along2 = []
    for d in range(1, gxn):
        along2.append(remote(s2a.at[lax.rem(gx + d, gxn)], r2gx.at[d - 1], 24 + d, at(d, 0)))
        along2[-1].start()

    for x in range(8):
        spread = gp[x // 2]
        spread = jnp.concatenate([spread, spread], axis=1)
        spread = jnp.concatenate([spread, spread], axis=0)
        gf[x] = (sl[x] * spread).astype(BF16)

    for x in range(8):
        term = dot_nt(gf[x], xs[x:x + 3].reshape(720, 256))
        acc1[...] = term if x == 0 else acc1[...] + term

    taps = None
    for dy in range(3):
        kept = None
        for r in range(16):
            y = 2 * (r % 8) + r // 8
            term = jnp.where(place[:, :720] == float(y + dy - 1), acc1[r * 32:r * 32 + 32], 0.0)
            kept = term if kept is None else kept + term
        parts = split_dot(kept, gather[...])
        if dy:
            parts = pltpu.roll(parts, 3 * dy, 1)
        taps = parts if taps is None else taps + parts
    for g in range(8):
        s1[g] = taps[4 * g:4 * g + 4]
    along1 = []
    for d in range(gxn):
        for e in range(2):
            if d + e:
                peer = (lax.rem(gx + d, gxn), gy, lax.rem(dp + e, 2))
                along1.append(remote(s1.at[peer[0]], r1gx.at[2 * d + e - 1], 47 + 2 * d + e, peer))
                along1[-1].start()

    rows = [w1tr[g * 80 + 64:g * 80 + 80, :] for g in range(9)]
    rows = jnp.concatenate(rows, axis=0)
    rows = jnp.concatenate([rows[:, 0:32], rows[:, 480:512]], axis=1)
    ends_of = [dot(rows, jnp.concatenate([gf[x, 0:32], gf[x, 480:512]], axis=0)) for x in range(8)]
    depth = []
    for dz in range(3):
        sums = []
        for i in range(10):
            parts = [ends_of[i - dx][(dx * 3 + dz) * 16:(dx * 3 + dz) * 16 + 8] for dx in range(3) if 0 <= i - dx < 8]
            sums.append(functools.reduce(lambda p, q: p + q, parts))
        depth.append(jnp.concatenate(sums, axis=0))
    outer = depth[1] + before(depth[2]) + after(depth[0])
    sby[...] = dot(regroup[...], outer[8:72].astype(BF16)).astype(BF16)
    for i, x, dx in ((0, 0, 0), (1, 7, 2)):
        face = dot(w1tr[dx * 240:dx * 240 + 240], gf[x])
        sx_[i] = (face[80:144] + before(face[160:224]) + after(face[0:64])).astype(BF16)
        corner = outer[i * 72:i * 72 + 8]
        sc[i] = jnp.concatenate([corner, corner], axis=0).astype(BF16)
    fourth = []
    for k, (sx, sy) in enumerate(DIRS):
        a, b = (0 if sx == 1 else 1), (0 if sy == 1 else 1)
        if sx == 0:
            src, dst = sby.at[pl.ds(32 - b * 32, 32)], ry.at[pl.ds(32 - b * 32, 32)]
        elif sy == 0:
            src, dst = sx_.at[1 if sx == 1 else 0], rx.at[a]
        else:
            src, dst = sc.at[1 if sx == 1 else 0], rc.at[a, b]
        fourth.append(remote(src, dst, 40 + k, at(sx, sy)))
    start(fourth, (1, -1, 0))

    for x in range(8):
        term = dot(w1tr[...], gf[x]).reshape(3, 240, 256)
        if x == 0:
            gi[0:3] = term
        else:
            gi[x:x + 2] += term[:2]
            gi[x + 2] = term[2]

    for x in range(8):
        gi[x + 1, 80:144] += before(gi[x + 1, 160:224]) + after(gi[x + 1, 0:64])
    for copy in along1:
        copy.wait()
    total1 = s1[gx]
    for i in range(2 * gxn - 1):
        total1 = total1 + r1gx[i]
    s1b[...] = total1
    across1 = []
    for d in range(1, gyn):
        across1.append(remote(s1b, r1gy.at[d - 1], 62 + d, at(0, d)))
        across1[-1].start()
    for copy in along2:
        copy.wait()
    total2 = s2a[gx]
    for d in range(1, gxn):
        total2 = total2 + r2gx[d - 1]
    for g in range(8):
        s2b[g] = total2[g:g + 1]
    across2 = []
    for d in range(1, gyn):
        across2.append(remote(s2b.at[lax.rem(gy + d, gyn)], r2gy.at[d - 1], 31 + d, at(0, d)))
        across2[-1].start()
    finish_all(fourth)
    y16 = lax.broadcasted_iota(jnp.int32, (4, 16, 256), 1)

    def ends(low_rows, high_rows):
        low_part = jnp.where(jnp.logical_and(y16 == 0, left), low_rows[4:8][:, None, :], 0.0)
        high_part = jnp.where(jnp.logical_and(y16 == 15, right), high_rows[0:4][:, None, :], 0.0)
        return (low_part + high_part).reshape(64, 256)

    for a, ok, x in ((0, up, 1), (1, down, 8)):
        term = rx[a].astype(F32) + ends(rc[a, 0].astype(F32), rc[a, 1].astype(F32))
        gi[x, 80:144] += jnp.where(ok, term, 0.0)
    sides = [jnp.where(right, ry[0:32].astype(F32), 0.0), jnp.where(left, ry[32:64].astype(F32), 0.0)]
    extra = dot(scatter[...], jnp.concatenate(sides, axis=0).astype(BF16))
    for x in range(8):
        out[x] = (gi[x + 1, 80:144] + extra[x * 64:x * 64 + 64]).astype(BF16)

    for copy in across2:
        copy.wait()
    total2 = s2b[gy]
    for d in range(1, gyn):
        total2 = total2 + r2gy[d - 1]
    total2 = jnp.concatenate([total2 * (1.0 / (CELLS / 8) ** 0.5)] * 8, axis=0)[:, :432]
    gw2[...] = split_dot(total2, reorder[...])[0:1]
    for copy in across1:
        copy.wait()
    total1 = s1b[...]
    for d in range(1, gyn):
        total1 = total1 + r1gy[d - 1]
    mine = None
    for q in range(4):
        for c in range(4):
            ok = jnp.logical_and(gy // 2 == q, (gy % 2) * 2 + dp == c)
            term = jnp.where(ok, total1[q:q + 1, c * 32:c * 32 + 32], 0.0)
            mine = term if mine is None else mine + term
    gw1[...] = mine[:, 0:27] * (1.0 / CELLS ** 0.5)


def write_back(total, restore, part1, part2, out, gw1, gw2):
    natural = dot(total[...].reshape(512, 256), restore[...]).astype(BF16)
    for x in range(8):
        for n in range(2):
            out[n, :, x] = natural[x * 64:x * 64 + 64, n * 128:n * 128 + 128].reshape(4, 16, 128)
    gw1[...] = part1[...]
    gw2[...] = part2[...]


def on_device(gxn, gyn, consts, inputs, cotangent, w_first, w_second, b_first, b_second):
    cot = jnp.transpose(cotangent, (0, 2, 3, 4, 1)).reshape(512, 64)
    w1t = jnp.transpose(w_first, (2, 3, 4, 1, 0)).reshape(27, 4, 32)
    w2t = jnp.transpose(w_second, (2, 3, 4, 1, 0)).reshape(864, 64)
    vmem = pl.BlockSpec(memory_space=pltpu.VMEM)
    b1, b2 = b_first.reshape(1, 32), b_second.reshape(1, 64)
    c = {name: jnp.asarray(value) for name, value in consts.items()}
    operands = (
        inputs, c["select"], w1t, c["eye"], c["toeplitz"], c["place"], c["depth_map"], b1, c["expand"], w2t, cot, b2,
        c["pool_map"], c["cot_map"], c["gather"], c["reorder"], c["regroup"], c["scatter"],
    )
    scratch = [
        ((10, 240, 256), BF16), ((64, 256), BF16), ((64, 256), BF16), ((2, 2, 4, 16, 128), BF16),
        ((2, 2, 16, 256), BF16), ((512, 720), BF16), ((720, 512), BF16), ((64, 864), BF16), ((96, 576), BF16),
        ((128, 128), F32), ((128, 128), F32), ((8, 512, 256), F32), ((8, 512, 256), BF16), ((6, 3, 320, 128), BF16),
        ((256, 256), F32), ((6, 768, 128), BF16), ((4, 256, 128), F32),
        ((2, 64, 512), F32), ((64, 512), F32), ((gxn, 8, 512), F32), ((gxn - 1, 8, 512), F32), ((gyn, 1, 512), F32),
        ((gyn - 1, 1, 512), F32), ((10, 240, 256), F32), ((64, 256), BF16), ((64, 256), BF16),
        ((2, 64, 256), BF16), ((2, 64, 256), BF16), ((2, 16, 256), BF16), ((2, 2, 16, 256), BF16), ((512, 720), F32),
        ((gxn, 4, 128), F32), ((2 * gxn - 1, 4, 128), F32), ((4, 128), F32),
        ((gyn - 1, 4, 128), F32), ((128, 32), F32), ((4, 64, 288), BF16), ((2, 8, 64, 256), F32),
        ((2, 320, 128), BF16), ((2, 4, 32, 128), BF16), ((2, 256, 128), BF16), ((2, 4, 32, 128), BF16),
        ((2, 2, 32, 128), BF16),
    ]
    total, part1, part2 = pl.pallas_call(
        functools.partial(kernel, gxn, gyn),
        out_shape=(
            jax.ShapeDtypeStruct((8, 64, 256), BF16),
            jax.ShapeDtypeStruct((1, 27), F32),
            jax.ShapeDtypeStruct((1, 432), F32),
        ),
        in_specs=[pl.BlockSpec(memory_space=pl.ANY)] * NLOAD,
        out_specs=(vmem, vmem, vmem),
        scratch_shapes=[pltpu.VMEM(v.shape, v.dtype) for v in operands]
        + [pltpu.VMEM(s, d) for s, d in scratch]
        + [pltpu.SemaphoreType.DMA((70,)), pltpu.SemaphoreType.DMA((70,)), pltpu.SemaphoreType.DMA((NLOAD,))],
        compiler_params=pltpu.CompilerParams(
            collective_id=0, has_side_effects=True, vmem_limit_bytes=60 * 1024 * 1024
        ),
    )(*operands)
    result, part1, part2 = pl.pallas_call(
        write_back,
        out_shape=(
            jax.ShapeDtypeStruct(inputs.shape, BF16),
            jax.ShapeDtypeStruct((1, 27), F32),
            jax.ShapeDtypeStruct((1, 432), F32),
        ),
        in_specs=[vmem] * 4,
        out_specs=(vmem, vmem, vmem),
    )(total, c["restore"], part1, part2)
    return result, part1.reshape(27), part2.reshape(432)


def solution(mesh):
    consts = constants()
    return jax.shard_map(
        functools.partial(on_device, mesh.shape["gx"], mesh.shape["gy"], consts),
        mesh=mesh,
        in_specs=(P("dp", None, "gx", "gy", None), P("dp", None, "gx", "gy", None), P(), P(), P(), P()),
        out_specs=(P("dp", None, "gx", "gy", None), P(("gx", "gy", "dp")), P(("gx", "gy", "dp"))),
        check_vma=False,
    )
```
